32 devices in a mesh: grp: 4 (over z), bis: 8 (over y, x, core).
Axes of the slice: x: 2, y: 2, z: 4, core: 2. Of those that a mesh axis runs over, the one named last changes fastest.
Arguments:
- state: float32 [5, 1024, 512], P(None, ('grp', 'bis')), may hold values from -0.75 to 2, as said below
- order: int32 [32, 8], P(('grp', 'bis')), may hold values from 0 to 7, each once within a row
- sweep: float32 [1024, 512], P(('grp', 'bis')), may hold values from 0.1 to 0.45
- owner: int32 [256, 1], P(('grp', 'bis')), may hold values from 0 to 7; in each aligned block of 8 rows (0 to 7, 8 to 15, ...) at most 2 rows name the same one
- slot_target: int32 [256], P(('grp', 'bis')), may hold values from 0 to 7
Outputs:
- mass_out: float32 [1024, 512], P(('grp', 'bis'))
- energy_out: float32 [1024, 512], P(('grp', 'bis'))
- velocity: float32 [2, 1024, 512], P(None, ('grp', 'bis'))
The draws below stay inside these ranges and needn't reach their ends.
Inputs may be any that keep to these rules, and one draw needn't show every extreme that they name: `state`: velocities up to 0.75 in size, densities and energies from 1 to 2, adiabatic indices from 1.3 to 1.7. `order`: each row of a device is a permutation. Among the row blocks of one device no owner is named more than 2 times, a bound that some block reaches.
All inputs are finite; a program needn't handle non-finite values.
Results may differ from the reference program's by a relative error of at most 0.00016.
Values sent between devices are 32-bit elements; how exact they have to be, the bound alone decides.
No kernel may reach another device: no remote copies, remote signals or barrier semaphores. Data moves between devices by JAX's collectives and lax.ppermute only.
A program may use at most 64 MiB of HBM per device.

```python
import math
import jax
import jax.numpy as jnp
import numpy as np

W = 512
BR = 4
STEPS = 2
CAP = 2
NBLK = 8
ROWS = 1024
BLOCKS = 256
N_GRP = 4
N_BIS = 8


def draw_state(key, part):
    keys = jax.random.split(key, 5)
    shape = (ROWS, W)
    rho = jax.random.uniform(keys[0], shape, jnp.float32, 1.0, 2.0)
    ene = 1.0 + jax.random.uniform(keys[1], shape, jnp.float32, 0.0, 1.0)
    velu = 0.3 * jnp.clip(jax.random.normal(keys[2], shape, jnp.float32), -2.5, 2.5)
    velv = 0.3 * jnp.clip(jax.random.normal(keys[3], shape, jnp.float32), -2.5, 2.5)
    gam = jax.random.uniform(keys[4], shape, jnp.float32, 1.3, 1.7)
    return jnp.stack([rho, ene, velu, velv, gam]).astype(jnp.float32)


def touch_ends(values, own_key, smallest, top_value):
    longest = values.shape.index(max(values.shape))
    spots = []
    for shift in (0, 1):
        where = [jax.random.randint(jax.random.fold_in(own_key, axis), (), 0, length) for axis, length in enumerate(values.shape)]
        where[longest] = (where[longest] + shift) % values.shape[longest]
        spots.append(tuple(where))
    return values.at[spots[0]].set(smallest).at[spots[1]].set(top_value)


def block_levels(rng, extent, cuts, least, largest):
    level, own = 1.0, jax.random.fold_in(rng, 6)
    for axis_at, blocks in cuts:
        draws = jnp.exp(jax.random.uniform(jax.random.fold_in(own, axis_at), (blocks,), jnp.float32, least / len(cuts), largest / len(cuts)))
        level = level * jnp.repeat(draws, extent[axis_at] // blocks).reshape([-1 if axis == axis_at else 1 for axis in range(len(extent))])
    return level


def assign_block(key, own, number, rows, number_of, top, most, slope):
    sequence = jax.random.permutation(key, number_of)
    packed, usual = portions_of(number_of, rows * top, most, slope, True), portions_of(number_of, rows * top, most, slope, False)
    places = jnp.arange(number_of)

    def named(tallies, turn):
        used = int((tallies > 0).sum())
        fixed = max(1, used // 4)
        moved = fixed + (places - fixed + turn * (used - fixed)) % max(1, number_of - fixed)
        return jnp.zeros((number_of,), jnp.int32).at[sequence[jnp.where(places < fixed, places, moved)]].set(jnp.asarray(tallies, jnp.int32))

    tallies = jnp.where(number % 4 == 0, named(packed, number // 4), named(usual, number - number // 4 - 1))
    mixed = jax.random.permutation(jax.random.fold_in(own, 3), number_of)
    donor, sink = mixed[0:number_of // 2 * 2:2], mixed[1:number_of // 2 * 2:2]
    slack = jnp.minimum(tallies[donor] - 1, most - tallies[sink]) // 2
    slack = jnp.where((donor == sequence[0]) | (sink == sequence[0]) | (tallies[sink] == 0), 0, jnp.maximum(slack, 0))
    moved = jax.random.randint(jax.random.fold_in(own, 4), (number_of // 2,), 0, 1 << 20) % (slack + 1)
    tallies = tallies.at[donor].add(-moved).at[sink].add(moved)
    members = jnp.searchsorted(jnp.cumsum(tallies), jnp.arange(rows * top), side="right").astype(jnp.int32)
    listing = members.reshape(top, rows).T
    listing = listing[jax.random.permutation(jax.random.fold_in(own, 1), rows)]
    turn = jax.random.randint(jax.random.fold_in(own, 2), (rows, 1), 0, top)
    return jnp.take_along_axis(listing, (jnp.arange(top)[None, :] + turn) % top, axis=1)


def portions_of(number_of, total, limit, slope, full):
    loads = [(1 << 20) // math.isqrt(standing ** slope) + 1 for standing in range(1, number_of + 1)]
    largest = limit if full else min(limit, max(-(-total // number_of), total * loads[0] // sum(loads)))
    least = 1 if total - largest >= number_of - 1 else 0
    given, surplus = [largest] + [least] * (number_of - 1), total - largest - least * (number_of - 1)
    while surplus > 0:
        movable = [i for i in range(1, number_of) if given[i] < largest] or [i for i in range(1, number_of) if given[i] < limit]
        whole, budget = sum([loads[i] for i in movable]), surplus
        for i in movable:
            more = min(limit - given[i], max(1, budget * loads[i] // whole), surplus)
            given[i] = given[i] + more
            surplus = surplus - more
    return np.array(given)


def setup_inputs(seed: int = 0) -> dict:
    arg_keys = jax.random.split(jax.random.key(seed), 6)
    state = draw_state(jax.random.fold_in(arg_keys[5], 71), 0)
    order = jax.vmap(lambda own: jax.random.permutation(own, N_BIS))(jax.random.split(arg_keys[1], (N_GRP * N_BIS))).reshape((N_GRP * N_BIS, N_BIS)).astype(jnp.int32)
    sweep = jnp.clip(0.1 + 0.35 * jax.random.uniform(arg_keys[2], (ROWS, W), jnp.float32) ** block_levels(arg_keys[2], (ROWS, W), ((0, 32),), -0.2, 0.2), 0.1, 0.45)
    owner_keys = jax.random.split(jax.random.fold_in(arg_keys[3], 1), BLOCKS // NBLK)
    owner_turns = jax.random.permutation(jax.random.fold_in(arg_keys[3], 3), BLOCKS // NBLK)
    owner = jax.vmap(lambda own, number: assign_block(jax.random.fold_in(arg_keys[3], 2), own, number, NBLK, N_BIS, 1, CAP, 2))(owner_keys, owner_turns).reshape((BLOCKS, 1))
    slot_target = touch_ends(jax.random.randint(arg_keys[4], (BLOCKS,), 0, NBLK), jax.random.fold_in(arg_keys[4], 1), 0, NBLK - 1).astype(jnp.int32)
    return {"state": state, "order": order, "sweep": sweep, "owner": owner, "slot_target": slot_target}


STEP_DT = 0.15


def advance(fields, volume, valid):
    rho = fields[0]
    ene = fields[1]
    velu = fields[2]
    velv = fields[3]
    gam = fields[4]
    press = (gam - 1.0) * rho * ene
    wide_p = jnp.pad(press[1:-1], ((0, 0), (1, 1)))
    wide_v = jnp.pad(velv[1:-1], ((0, 0), (1, 1)))
    grad_x = 0.5 * (press[2:] - press[:-2])
    grad_y = 0.5 * (wide_p[:, 2:] - wide_p[:, :-2])
    spread = 0.5 * (velu[2:] - velu[:-2] + wide_v[:, 2:] - wide_v[:, :-2])
    dens = jnp.where(valid, rho[1:-1], 1.0)
    growth = 1.0 + STEP_DT * spread
    center_g = gam[1:-1]
    updated = jnp.stack([
        dens / growth,
        ene[1:-1] * (1.0 - STEP_DT * (center_g - 1.0) * spread),
        velu[1:-1] - STEP_DT * grad_x / dens,
        velv[1:-1] - STEP_DT * grad_y / dens,
        center_g,
    ])
    updated = jnp.where(valid[None], updated, 0.0)
    return updated, volume * growth


def reference(state, order, sweep, owner, slot_target):
    blocks = state.reshape(5, N_GRP, N_BIS, NBLK, BR, W)
    order_g = order.reshape(N_GRP, N_BIS, N_BIS)
    picked = jnp.take_along_axis(blocks, order_g[None, :, :, :, None, None], axis=3)
    fields = jnp.transpose(picked, (0, 1, 3, 2, 4, 5)).reshape(5, ROWS, W)
    volume = jnp.ones((ROWS, W), jnp.float32)
    valid = jnp.ones((ROWS, 1), bool)
    for step in range(STEPS):
        padded = jnp.pad(fields, ((0, 0), (1, 1), (0, 0)))
        fields, volume = advance(padded, volume, valid)
    mass = fields[0] * volume
    heat = mass * fields[1]
    frac = sweep * volume / (1.0 + volume)
    amounts = jnp.stack([mass, heat])
    stay = ((1.0 - frac) * amounts).reshape(2, ROWS // BR, BR, W)
    leave = jnp.roll((frac * amounts).reshape(2, ROWS // BR, BR, W), 1, axis=2)
    partial_value = (stay + leave).reshape(2, N_GRP, N_BIS * NBLK, BR * W)
    partial_value = jnp.transpose(partial_value, (1, 2, 0, 3))
    labels = (owner[:, 0].reshape(N_GRP, N_BIS * NBLK) * NBLK + slot_target.reshape(N_GRP, N_BIS * NBLK)).astype(jnp.int32)

    def one_group(data, seg):
        return jax.ops.segment_sum(data, seg, num_segments=N_BIS * NBLK)

    summed = jax.vmap(one_group)(partial_value, labels)
    summed = jnp.transpose(summed, (2, 0, 1, 3)).reshape(2, ROWS, W)
    return summed[0], summed[1], fields[2:4]
```

```python
import functools

import jax
import jax.numpy as jnp
from jax import lax
from jax.experimental import pallas as pl
from jax.experimental.pallas import tpu as pltpu
from jax.sharding import PartitionSpec as P

BR = 4
CAP = 2
HALF_DT = 0.075
NF = 5
RHO, ENE, VELU, VELV, GAM = range(NF)
FAR_P, FAR_U = 5, 6
SMEM = pl.BlockSpec(memory_space=pltpu.SMEM)
VMEM = pl.BlockSpec(memory_space=pltpu.VMEM)


def sublane(width):
    return lax.broadcasted_iota(jnp.int32, (8, width), 0)


def turn(tile, shift):
    return pltpu.roll(tile, shift, 0)


def where_am_i():
    return lax.axis_index("grp"), lax.axis_index("bis")


def pack_kernel(n, order, state, *outs):
    chips = n // 2
    width = state.shape[2]
    _, me = where_am_i()
    chip = me // 2
    sub = sublane(width)
    first = me == 0
    chip_bufs, across = outs[:chips], outs[chips]

    def tile_of(field, block):
        return state[field, pl.ds(pl.multiple_of(block // 2 * 8, 8), 8), :]

    def halo(index):
        block = order[0, index]
        odd = block % 2 * 4
        near = odd + jnp.where(first, 0, BR - 1)
        far = odd + jnp.where(first, 1, BR - 2)
        tiles = [tile_of(field, block) for field in range(NF)]
        press = (tiles[GAM] - 1.0) * tiles[RHO] * tiles[ENE]
        out = turn(tiles[0], (8 - near) % 8)
        for field in range(1, NF):
            out = jnp.where(sub == field, turn(tiles[field], (field + 8 - near) % 8), out)
        out = jnp.where(sub == FAR_P, turn(press, (FAR_P + 8 - far) % 8), out)
        return jnp.where(sub == FAR_U, turn(tiles[VELU], (FAR_U + 8 - far) % 8), out)

    for mask in range(chips):
        goal = chip ^ mask
        low = order[0, 2 * goal]
        high = order[0, 2 * goal + 1]
        for field in range(NF):
            even = turn(tile_of(field, low), low % 2 * 4)
            odd = turn(tile_of(field, high), 4 - high % 2 * 4)
            chip_bufs[mask][8 * field : 8 * field + 8, :] = jnp.where(sub < 4, even, odd)
        beyond = jnp.where(first, jnp.minimum(2 * goal + 2, n - 1), jnp.maximum(2 * goal - 1, 0))
        chip_bufs[mask][8 * NF :, :] = halo(beyond)
    across[...] = halo(jnp.where(first, 0, n - 1))


def step_kernel(n, *refs):
    chips = n // 2
    refs = list(refs)
    take = lambda count: [refs.pop(0) for _ in range(count)]
    owner, slot, owner_sib, slot_sib = take(4)
    mine, theirs = take(chips), take(chips)
    across, across_sib, sweep, sweep_sib = take(4)
    (vel,) = take(1)
    sends = take(chips)
    fld, prs, vols, coef, halo, bins, tags, count = take(8)
    grp, me = where_am_i()
    chip, core = me // 2, me % 2
    width = sweep.shape[1]
    rows = sweep.shape[0]
    tiles = 2 * chips
    sub = sublane(width)
    lane = lax.broadcasted_iota(jnp.int32, (8, width), 1)
    is_low = core == 0

    def pair(own, sib):
        return jnp.where(is_low, own, sib), jnp.where(is_low, sib, own)

    def at(tile):
        return pl.ds(pl.multiple_of(tile * 8, 8), 8)

    for mask in range(chips):
        source = chip ^ mask
        for field in range(NF):
            span = pl.ds(8 * field, 8)
            even, odd = pair(mine[mask][span, :], theirs[mask][span, :])
            fld[field, at(1 + source), :] = jnp.where(sub < 4, even, turn(odd, 4))
            fld[field, at(1 + chips + source), :] = jnp.where(sub < 4, turn(even, 4), odd)
        even, odd = pair(mine[mask][8 * NF :, :], theirs[mask][8 * NF :, :])
        halo[0, source] = even
        halo[1, source] = odd
    even, odd = pair(across[...], across_sib[...])
    top = jnp.where(chip == 0, even, halo[1, chips - 1])
    bottom = jnp.where(chip == chips - 1, odd, halo[0, 0])

    def line(tile, index):
        return jnp.broadcast_to(tile[index : index + 1, :], (8, width))

    for tile, place, near in ((top, 0, 7), (bottom, tiles + 1, 0)):
        span = at(place)
        for field in (RHO, ENE, VELV, GAM):
            fld[field, span, :] = line(tile, field)
        fld[VELU, span, :] = jnp.where(sub == near, line(tile, VELU), line(tile, FAR_U))
        press = (line(tile, GAM) - 1.0) * line(tile, RHO) * line(tile, ENE)
        prs[0, span, :] = jnp.where(sub == near, press, line(tile, FAR_P))

    def left_right(x):
        left = jnp.where(lane == 0, 0.0, pltpu.roll(x, 1, 1))
        right = jnp.where(lane == width - 1, 0.0, pltpu.roll(x, width - 1, 1))
        return right - left

    def down_up(ref, index, tile, x, clip=False):
        before = ref[index, at(jnp.maximum(tile - 1, 0) if clip else tile - 1), :]
        after = ref[index, at(jnp.minimum(tile + 1, tiles + 1) if clip else tile + 1), :]
        return turn(jnp.where(sub == 0, after, x), 7) - turn(jnp.where(sub == 7, before, x), 1)

    def pressure(tile, _):
        span = at(tile)
        prs[0, span, :] = (fld[GAM, span, :] - 1.0) * fld[RHO, span, :] * fld[ENE, span, :]
        return 0

    lax.fori_loop(1, tiles + 1, pressure, 0, unroll=n <= 8)

    def first(tile, _):
        span = at(tile)
        velu, velv, press = fld[VELU, span, :], fld[VELV, span, :], prs[0, span, :]
        push = HALF_DT * (down_up(fld, VELU, tile, velu, True) + left_right(velv))
        grow = 1.0 + push
        scale = HALF_DT / fld[RHO, span, :]
        keep = 1.0 - (fld[GAM, span, :] - 1.0) * push
        nxt_p = press * keep / grow
        nxt_u = velu - down_up(prs, 0, tile, press, True) * scale
        nxt_v = velv - left_right(press) * scale
        prs[1, span, :] = nxt_p
        vols[0, span, :] = nxt_u
        vols[1, span, :] = nxt_v
        vols[2, span, :] = grow
        vols[3, span, :] = fld[ENE, span, :] * keep
        coef[span, :] = scale * grow
        return 0

    lax.fori_loop(0, tiles + 2, first, 0, unroll=n <= 8)
    inside_top = jnp.logical_or(grp > 0, chip > 0)
    inside_bottom = jnp.logical_or(grp < lax.axis_size("grp") - 1, chip < chips - 1)
    for place, inside in ((0, inside_top), (tiles + 1, inside_bottom)):
        span = at(place)
        prs[1, span, :] = jnp.where(inside, prs[1, span, :], 0.0)
        vols[0, span, :] = jnp.where(inside, vols[0, span, :], 0.0)

    def velocity(index, _):
        tile = 1 + core * chips + index
        span, dest = at(tile), at(index)
        press, scale = prs[1, span, :], coef[span, :]
        vel[0, dest, :] = vols[0, span, :] - down_up(prs, 1, tile, press) * scale
        vel[1, dest, :] = vols[1, span, :] - left_right(press) * scale
        return 0

    lax.fori_loop(0, chips, velocity, 0, unroll=n <= 8)

    for mask in range(chips + 1):
        count[mask] = 0
        tags[mask] = jnp.full((8, 128), -1.0, jnp.float32)
    sub128 = sublane(128)

    def cyclic(x):
        return jnp.where(sub % BR == 0, turn(x, 8 - (BR - 1)), turn(x, 1))

    def place(tile_out, who, where_to):
        fits = who % 2 == core
        mask = jnp.where(fits, (who // 2) ^ chip, chips)
        rank = count[mask]
        count[mask] = jnp.where(fits, rank + 1, 0)
        bins[mask, rank] = tile_out
        tags[mask] = jnp.where(sub128 == rank, where_to.astype(jnp.float32), tags[mask])

    def second(device, index):
        tile = 1 + device * chips + index
        span = at(tile)
        push = HALF_DT * (down_up(vols, 0, tile, vols[0, span, :]) + left_right(vols[1, span, :]))
        volume = vols[2, span, :] * (1.0 + push)
        heat_e = vols[3, span, :] * (1.0 - (fld[GAM, span, :] - 1.0) * push)
        mass = fld[RHO, span, :]
        heat = mass * heat_e
        from_own = (core == 0) if device == 0 else (core == 1)
        swept = jnp.where(from_own, sweep[at(index), :], sweep_sib[at(index), :])
        frac = swept * volume / (1.0 + volume)
        mass_go, heat_go = frac * mass, frac * heat
        mass_part = mass - mass_go + cyclic(mass_go)
        heat_part = heat - heat_go + cyclic(heat_go)
        for bit, tile_out in (
            (0, jnp.where(sub < 4, mass_part, turn(heat_part, 4))),
            (1, jnp.where(sub < 4, turn(mass_part, 4), heat_part)),
        ):
            block = 2 * index + bit
            who = jnp.where(from_own, owner[block, 0], owner_sib[block, 0])
            where_to = jnp.where(from_own, slot[block], slot_sib[block])
            place(tile_out, who, where_to)

    for device in range(2):
        lax.fori_loop(0, chips, lambda index, _, device=device: (second(device, index), 0)[1], 0, unroll=n <= 8)

    for mask in range(chips):
        for rank in range(2 * CAP):
            for part in range(width // 128):
                sends[mask][rank * (width // 128) + part] = bins[mask, rank, :, part * 128 : part * 128 + 128]
        sends[mask][2 * CAP * (width // 128)] = tags[mask]


def land_kernel(n, *refs):
    chips = n // 2
    arrived = refs[:chips]
    mass, energy = refs[chips:]
    parts = mass.shape[1] // 128
    sub = sublane(128)

    def tile_pair(index, _):
        span = pl.ds(pl.multiple_of(index * 8, 8), 8)
        sums = [[jnp.zeros((8, 128), jnp.float32) for _ in range(parts)] for _ in range(2)]
        for buf in arrived:
            tag_tile = buf[2 * CAP * parts]
            for rank in range(2 * CAP):
                tag = jnp.broadcast_to(tag_tile[rank : rank + 1, :], (8, 128))
                for bit in range(2):
                    hit = tag == (2 * index + bit) * 1.0
                    for part in range(parts):
                        sums[bit][part] += jnp.where(hit, buf[rank * parts + part], 0.0)
        for part in range(parts):
            cols = slice(part * 128, part * 128 + 128)
            even, odd = sums[0][part], sums[1][part]
            mass[span, cols] = jnp.where(sub < 4, even, turn(odd, 4))
            energy[span, cols] = jnp.where(sub < 4, turn(even, 4), odd)
        return 0

    lax.fori_loop(0, chips, tile_pair, 0, unroll=n <= 8)


def shards(state, order, sweep, owner, slot_target):
    n = lax.axis_size("bis")
    groups = lax.axis_size("grp")
    chips = n // 2
    rows, width = sweep.shape
    parts = width // 128
    f32 = jnp.float32
    params = pltpu.CompilerParams(vmem_limit_bytes=48 * 1024 * 1024)

    def to_sibling(x):
        return lax.ppermute(x, "bis", [(i, i ^ 1) for i in range(n)])

    def to_chip(x, mask):
        return lax.ppermute(x, "bis", [(i, i ^ 2 * mask) for i in range(n)]) if mask else x

    sweep_sib, owner_sib, slot_sib = to_sibling(sweep), to_sibling(owner), to_sibling(slot_target)

    packed = pl.pallas_call(
        functools.partial(pack_kernel, n),
        out_shape=[jax.ShapeDtypeStruct((8 * (NF + 1), width), f32)] * chips
        + [jax.ShapeDtypeStruct((8, width), f32)],
        in_specs=[SMEM, VMEM],
        out_specs=[VMEM] * (chips + 1),
        compiler_params=params,
        name="pack",
    )(order, state)
    links = []
    for grp in range(groups - 1):
        low, high = grp * n + n - 1, (grp + 1) * n
        links += [(low, high), (high, low)]
    across = lax.ppermute(packed[chips], ("grp", "bis"), links)
    mine = [to_chip(packed[mask], mask) for mask in range(chips)]
    theirs = [to_sibling(x) for x in mine]
    across_sib = to_sibling(across)

    stack = (2 * chips + 2) * 8
    send_shape = (2 * CAP * parts + 1, 8, 128)
    out = pl.pallas_call(
        functools.partial(step_kernel, n),
        out_shape=[jax.ShapeDtypeStruct((2, rows, width), f32)]
        + [jax.ShapeDtypeStruct(send_shape, f32)] * chips,
        in_specs=[SMEM] * 4 + [VMEM] * (2 * chips + 4),
        out_specs=[VMEM] * (chips + 1),
        scratch_shapes=[
            pltpu.VMEM((NF, stack, width), f32),
            pltpu.VMEM((2, stack, width), f32),
            pltpu.VMEM((4, stack, width), f32),
            pltpu.VMEM((stack, width), f32),
            pltpu.VMEM((2, chips, 8, width), f32),
            pltpu.VMEM((chips + 1, 2 * CAP, 8, width), f32),
            pltpu.VMEM((chips + 1, 8, 128), f32),
            pltpu.SMEM((chips + 1,), jnp.int32),
        ],
        compiler_params=params,
        name="substeps",
    )(owner, slot_target, owner_sib, slot_sib, *mine, *theirs, across, across_sib, sweep, sweep_sib)
    vel = out[0]
    arrived = [to_chip(out[1 + mask], mask) for mask in range(chips)]
    mass, energy = pl.pallas_call(
        functools.partial(land_kernel, n),
        out_shape=[jax.ShapeDtypeStruct((rows, width), f32)] * 2,
        in_specs=[VMEM] * chips,
        out_specs=[VMEM] * 2,
        compiler_params=params,
        name="land",
    )(*arrived)
    return mass, energy, vel


def solution(mesh):
    placed = (
        P(None, ("grp", "bis"), None),
        P(("grp", "bis"), None),
        P(("grp", "bis"), None),
        P(("grp", "bis"), None),
        P(("grp", "bis")),
    )
    return jax.shard_map(
        shards,
        mesh=mesh,
        in_specs=placed,
        out_specs=(P(("grp", "bis"), None), P(("grp", "bis"), None), P(None, ("grp", "bis"), None)),
        check_vma=False,
    )
```

```python
import functools

import jax
import jax.numpy as jnp
from jax import lax
from jax.experimental import pallas as pl
from jax.experimental.pallas import tpu as pltpu
from jax.sharding import PartitionSpec as P

BR = 4
CAP = 2
HALF_DT = 0.075
NF = 5
RHO, ENE, VELU, VELV, GAM = range(NF)
FAR_P, FAR_U = 5, 6
SMEM = pl.BlockSpec(memory_space=pltpu.SMEM)
VMEM = pl.BlockSpec(memory_space=pltpu.VMEM)


def sublane(width):
    return lax.broadcasted_iota(jnp.int32, (8, width), 0)


def turn(tile, shift):
    return pltpu.roll(tile, shift, 0)


def where_am_i():
    return lax.axis_index("grp"), lax.axis_index("bis")


def pack_kernel(n, *refs):
    chips = n // 2
    order_in, owner_in, slot_in, sweep_in, state_in = refs[:5]
    chip_bufs, across = refs[5 : 5 + chips], refs[5 + chips]
    order, owner, slot, state, sems = refs[6 + chips :]
    width = state.shape[2]
    rows = state.shape[1]
    home = 8 * (NF + 1)
    copies = [pltpu.make_async_copy(order_in, order, sems.at[0])]
    copies += [pltpu.make_async_copy(state_in.at[field], state.at[field], sems.at[1 + field]) for field in range(NF)]
    copies += [
        pltpu.make_async_copy(owner_in, owner, sems.at[1 + NF]),
        pltpu.make_async_copy(slot_in, slot, sems.at[2 + NF]),
        pltpu.make_async_copy(sweep_in, chip_bufs[0].at[home : home + rows, :], sems.at[3 + NF]),
    ]
    for copy in copies:
        copy.start()
    _, me = where_am_i()
    chip = me // 2
    sub = sublane(width)
    first = me == 0
    copies[0].wait()

    def tile_of(field, block):
        return state[field, pl.ds(pl.multiple_of(block // 2 * 8, 8), 8), :]

    def halo(index):
        block = order[index]
        odd = block % 2 * 4
        near = odd + jnp.where(first, 0, BR - 1)
        far = odd + jnp.where(first, 1, BR - 2)
        tiles = [tile_of(field, block) for field in range(NF)]
        press = (tiles[GAM] - 1.0) * tiles[RHO] * tiles[ENE]
        out = turn(tiles[0], (8 - near) % 8)
        for field in range(1, NF):
            out = jnp.where(sub == field, turn(tiles[field], (field + 8 - near) % 8), out)
        out = jnp.where(sub == FAR_P, turn(press, (FAR_P + 8 - far) % 8), out)
        return jnp.where(sub == FAR_U, turn(tiles[VELU], (FAR_U + 8 - far) % 8), out)

    for field in range(NF):
        copies[1 + field].wait()
        for mask in range(chips):
            goal = chip ^ mask
            low = order[2 * goal]
            high = order[2 * goal + 1]
            even = turn(tile_of(field, low), low % 2 * 4)
            odd = turn(tile_of(field, high), 4 - high % 2 * 4)
            chip_bufs[mask][8 * field : 8 * field + 8, :] = jnp.where(sub < 4, even, odd)
    for mask in range(chips):
        goal = chip ^ mask
        beyond = jnp.where(first, jnp.minimum(2 * goal + 2, n - 1), jnp.maximum(2 * goal - 1, 0))
        chip_bufs[mask][8 * NF : home, :] = halo(beyond)
    across[...] = halo(jnp.where(first, 0, n - 1))
    for copy in copies[1 + NF :]:
        copy.wait()
    lane = lax.broadcasted_iota(jnp.int32, (1, width), 1)
    for block in range(n):
        line = jnp.where(lane == 0, owner[block], slot[block])
        chip_bufs[0][home + rows + block : home + rows + block + 1, :] = line.astype(jnp.float32)


def step_kernel(n, *refs):
    chips = n // 2
    refs = list(refs)
    take = lambda count: [refs.pop(0) for _ in range(count)]
    owner, slot = take(2)
    mine, theirs = take(chips), take(chips)
    across, across_sib, sweep = take(3)
    (vel,) = take(1)
    sends = take(chips)
    fld, prs, vols, coef, halo, bins, tags, count, named, sem = take(10)
    grp, me = where_am_i()
    chip, core = me // 2, me % 2
    width = sweep.shape[1]
    rows = sweep.shape[0]
    home = 8 * (NF + 1)
    sweep_sib = theirs[0].at[home : home + rows, :]
    tiles = 2 * chips
    sub = sublane(width)
    lane = lax.broadcasted_iota(jnp.int32, (8, width), 1)
    is_low = core == 0

    def pair(own, sib):
        return jnp.where(is_low, own, sib), jnp.where(is_low, sib, own)

    def at(tile):
        return pl.ds(pl.multiple_of(tile * 8, 8), 8)

    naming = pltpu.make_async_copy(theirs[0].at[home + rows : home + rows + n, 0:128], named, sem)
    naming.start()

    for mask in range(chips):
        source = chip ^ mask
        for field in range(NF):
            span = pl.ds(8 * field, 8)
            even, odd = pair(mine[mask][span, :], theirs[mask][span, :])
            fld[field, at(1 + source), :] = jnp.where(sub < 4, even, turn(odd, 4))
            fld[field, at(1 + chips + source), :] = jnp.where(sub < 4, turn(even, 4), odd)
        even, odd = pair(mine[mask][8 * NF : home, :], theirs[mask][8 * NF : home, :])
        halo[0, source] = even
        halo[1, source] = odd
    even, odd = pair(across[...], across_sib[...])
    inside_top = jnp.logical_or(grp > 0, chip > 0)
    inside_bottom = jnp.logical_or(grp < lax.axis_size("grp") - 1, chip < chips - 1)
    top = jnp.where(inside_top, jnp.where(chip == 0, even, halo[1, chips - 1]), 0.0)
    bottom = jnp.where(inside_bottom, jnp.where(chip == chips - 1, odd, halo[0, 0]), 0.0)

    def line(tile, index):
        return jnp.broadcast_to(tile[index : index + 1, :], (8, width))

    for tile, place, near in ((top, 0, 7), (bottom, tiles + 1, 0)):
        span = at(place)
        for field in (RHO, ENE, VELV, GAM):
            fld[field, span, :] = line(tile, field)
        fld[VELU, span, :] = jnp.where(sub == near, line(tile, VELU), line(tile, FAR_U))
        press = (line(tile, GAM) - 1.0) * line(tile, RHO) * line(tile, ENE)
        prs[0, span, :] = jnp.where(sub == near, press, line(tile, FAR_P))

    def left_right(x):
        left = jnp.where(lane == 0, 0.0, pltpu.roll(x, 1, 1))
        right = jnp.where(lane == width - 1, 0.0, pltpu.roll(x, width - 1, 1))
        return right - left

    def down_up(ref, index, tile, x, clip=False):
        before = ref[index, at(jnp.maximum(tile - 1, 0) if clip else tile - 1), :]
        after = ref[index, at(jnp.minimum(tile + 1, tiles + 1) if clip else tile + 1), :]
        return turn(jnp.where(sub == 0, after, x), 7) - turn(jnp.where(sub == 7, before, x), 1)

    def pressure(tile, _):
        span = at(tile)
        prs[0, span, :] = (fld[GAM, span, :] - 1.0) * fld[RHO, span, :] * fld[ENE, span, :]
        return 0

    lax.fori_loop(1, tiles + 1, pressure, 0, unroll=n <= 8)

    def first(tile, _):
        span = at(tile)
        velu, velv, press = fld[VELU, span, :], fld[VELV, span, :], prs[0, span, :]
        push = HALF_DT * (down_up(fld, VELU, tile, velu, True) + left_right(velv))
        grow = 1.0 + push
        scale = HALF_DT / fld[RHO, span, :]
        keep = 1.0 - (fld[GAM, span, :] - 1.0) * push
        nxt_p = press * keep / grow
        nxt_u = velu - down_up(prs, 0, tile, press, True) * scale
        nxt_v = velv - left_right(press) * scale
        prs[1, span, :] = nxt_p
        vols[0, span, :] = nxt_u
        vols[1, span, :] = nxt_v
        vols[2, span, :] = grow
        vols[3, span, :] = fld[ENE, span, :] * keep
        coef[span, :] = scale * grow
        return 0

    lax.fori_loop(0, tiles + 2, first, 0, unroll=n <= 8)
    for place, inside in ((0, inside_top), (tiles + 1, inside_bottom)):
        span = at(place)
        prs[1, span, :] = jnp.where(inside, prs[1, span, :], 0.0)
        vols[0, span, :] = jnp.where(inside, vols[0, span, :], 0.0)

    def velocity(index, _):
        tile = 1 + core * chips + index
        span, dest = at(tile), at(index)
        press, scale = prs[1, span, :], coef[span, :]
        vel[0, dest, :] = vols[0, span, :] - down_up(prs, 1, tile, press) * scale
        vel[1, dest, :] = vols[1, span, :] - left_right(press) * scale
        return 0

    lax.fori_loop(0, chips, velocity, 0, unroll=n <= 8)

    naming.wait()
    for mask in range(chips + 1):
        count[mask] = 0
        tags[mask] = jnp.full((8, 128), -1.0, jnp.float32)
    sub128 = sublane(128)

    def cyclic(x):
        return jnp.where(sub % BR == 0, turn(x, 8 - (BR - 1)), turn(x, 1))

    def place(tile_out, who, where_to):
        fits = who % 2 == core
        mask = jnp.where(fits, (who // 2) ^ chip, chips)
        rank = count[mask]
        count[mask] = jnp.where(fits, rank + 1, 0)
        bins[mask, rank] = tile_out
        tags[mask] = jnp.where(sub128 == rank, where_to, tags[mask])

    def second(device, index):
        tile = 1 + device * chips + index
        span = at(tile)
        push = HALF_DT * (down_up(vols, 0, tile, vols[0, span, :]) + left_right(vols[1, span, :]))
        volume = vols[2, span, :] * (1.0 + push)
        heat_e = vols[3, span, :] * (1.0 - (fld[GAM, span, :] - 1.0) * push)
        mass = fld[RHO, span, :]
        heat = mass * heat_e
        from_own = (core == 0) if device == 0 else (core == 1)
        swept = jnp.where(from_own, sweep[at(index), :], sweep_sib[at(index), :])
        frac = swept * volume / (1.0 + volume)
        mass_go, heat_go = frac * mass, frac * heat
        mass_part = mass - mass_go + cyclic(mass_go)
        heat_part = heat - heat_go + cyclic(heat_go)
        for bit, tile_out in (
            (0, jnp.where(sub < 4, mass_part, turn(heat_part, 4))),
            (1, jnp.where(sub < 4, turn(mass_part, 4), heat_part)),
        ):
            block = 2 * index + bit
            who = jnp.where(from_own, owner[block], named[block, 0].astype(jnp.int32))
            where_to = jnp.where(from_own, slot[block].astype(jnp.float32), named[block, 1])
            place(tile_out, who, where_to)

    for device in range(2):
        lax.fori_loop(0, chips, lambda index, _, device=device: (second(device, index), 0)[1], 0, unroll=n <= 8)

    for mask in range(chips):
        for rank in range(2 * CAP):
            for part in range(width // 128):
                sends[mask][rank * (width // 128) + part] = bins[mask, rank, :, part * 128 : part * 128 + 128]
        sends[mask][2 * CAP * (width // 128)] = tags[mask]


def land_kernel(n, *refs):
    chips = n // 2
    arrived = refs[:chips]
    mass, energy = refs[chips:]
    parts = mass.shape[1] // 128
    sub = sublane(128)

    def tile_pair(index, _):
        span = pl.ds(pl.multiple_of(index * 8, 8), 8)
        sums = [[jnp.zeros((8, 128), jnp.float32) for _ in range(parts)] for _ in range(2)]
        for buf in arrived:
            tag_tile = buf[2 * CAP * parts]
            for rank in range(2 * CAP):
                tag = jnp.broadcast_to(tag_tile[rank : rank + 1, :], (8, 128))
                for bit in range(2):
                    hit = tag == (2 * index + bit) * 1.0
                    for part in range(parts):
                        sums[bit][part] += jnp.where(hit, buf[rank * parts + part], 0.0)
        for part in range(parts):
            cols = slice(part * 128, part * 128 + 128)
            even, odd = sums[0][part], sums[1][part]
            mass[span, cols] = jnp.where(sub < 4, even, turn(odd, 4))
            energy[span, cols] = jnp.where(sub < 4, turn(even, 4), odd)
        return 0

    lax.fori_loop(0, chips, tile_pair, 0, unroll=n <= 8)


def across_links(groups, n):
    pairs = []
    for grp in range(groups):
        base = grp * n
        pairs += [(base + i, base + i + 1) for i in range(2, n - 2, 2)]
        if grp + 1 < groups:
            turn_at = n - 2 if grp % 2 == 0 else 1
            pairs += [(base + n - 1, base + n), (base + turn_at, base + n + turn_at)]
    used = {i for pair in pairs for i in pair}
    left = [i for i in range(groups * n) if i not in used]
    pairs += [(left[i], left[i + 1]) for i in range(0, len(left), 2)]
    return [link for low, high in pairs for link in ((low, high), (high, low))]


def shards(state, order, sweep, owner, slot_target):
    n = lax.axis_size("bis")
    groups = lax.axis_size("grp")
    chips = n // 2
    rows, width = sweep.shape
    parts = width // 128
    f32 = jnp.float32
    params = pltpu.CompilerParams(vmem_limit_bytes=48 * 1024 * 1024)

    def to_sibling(x):
        return lax.ppermute(x, "bis", [(i, i ^ 1) for i in range(n)])

    def to_chip(x, mask):
        return lax.ppermute(x, "bis", [(i, i ^ 2 * mask) for i in range(n)]) if mask else x

    owner = owner.reshape(n)
    extra = -(-(rows + n) // 8) * 8
    packed = pl.pallas_call(
        functools.partial(pack_kernel, n),
        out_shape=[
            jax.ShapeDtypeStruct((8 * (NF + 1) + (0 if mask else extra), width), f32) for mask in range(chips)
        ]
        + [jax.ShapeDtypeStruct((8, width), f32)],
        in_specs=[pl.BlockSpec(memory_space=pl.ANY)] * 5,
        out_specs=[VMEM] * (chips + 1),
        scratch_shapes=[
            pltpu.SMEM((n,), jnp.int32),
            pltpu.SMEM((n,), jnp.int32),
            pltpu.SMEM((n,), jnp.int32),
            pltpu.VMEM((NF, rows, width), f32),
            pltpu.SemaphoreType.DMA((NF + 4,)),
        ],
        compiler_params=params,
        name="pack",
    )(order.reshape(n), owner, slot_target, sweep, state)
    across = lax.ppermute(packed[chips], ("grp", "bis"), across_links(groups, n))
    mine = [to_chip(packed[mask], mask) for mask in range(chips)]
    theirs = [to_sibling(x) for x in mine]
    across_sib = to_sibling(across)

    stack = (2 * chips + 2) * 8
    send_shape = (2 * CAP * parts + 1, 8, 128)
    out = pl.pallas_call(
        functools.partial(step_kernel, n),
        out_shape=[jax.ShapeDtypeStruct((2, rows, width), f32)]
        + [jax.ShapeDtypeStruct(send_shape, f32)] * chips,
        in_specs=[SMEM] * 2 + [VMEM] * (2 * chips + 3),
        out_specs=[VMEM] * (chips + 1),
        scratch_shapes=[
            pltpu.VMEM((NF, stack, width), f32),
            pltpu.VMEM((2, stack, width), f32),
            pltpu.VMEM((4, stack, width), f32),
            pltpu.VMEM((stack, width), f32),
            pltpu.VMEM((2, chips, 8, width), f32),
            pltpu.VMEM((chips + 1, 2 * CAP, 8, width), f32),
            pltpu.VMEM((chips + 1, 8, 128), f32),
            pltpu.SMEM((chips + 1,), jnp.int32),
            pltpu.SMEM((n, 128), f32),
            pltpu.SemaphoreType.DMA,
        ],
        compiler_params=params,
        name="substeps",
    )(owner, slot_target, *mine, *theirs, across, across_sib, sweep)
    vel = out[0]
    arrived = [to_chip(out[1 + mask], mask) for mask in range(chips)]
    mass, energy = pl.pallas_call(
        functools.partial(land_kernel, n),
        out_shape=[jax.ShapeDtypeStruct((rows, width), f32)] * 2,
        in_specs=[VMEM] * chips,
        out_specs=[VMEM] * 2,
        compiler_params=params,
        name="land",
    )(*arrived)
    return mass, energy, vel


def solution(mesh):
    placed = (
        P(None, ("grp", "bis"), None),
        P(("grp", "bis"), None),
        P(("grp", "bis"), None),
        P(("grp", "bis"), None),
        P(("grp", "bis")),
    )
    return jax.shard_map(
        shards,
        mesh=mesh,
        in_specs=placed,
        out_specs=(P(("grp", "bis"), None), P(("grp", "bis"), None), P(None, ("grp", "bis"), None)),
        check_vma=False,
    )
```

```python
import functools

import jax
import jax.numpy as jnp
from jax import lax
from jax.experimental import pallas as pl
from jax.experimental.pallas import tpu as pltpu
from jax.sharding import PartitionSpec as P

BR = 4
CAP = 2
ZR = 48
HALF_DT = 0.075
NF = 5
RHO, ENE, VELU, VELV, GAM = range(NF)
FAR_P, FAR_U = 5, 6
SMEM = pl.BlockSpec(memory_space=pltpu.SMEM)
VMEM = pl.BlockSpec(memory_space=pltpu.VMEM)


def sublane(width):
    return lax.broadcasted_iota(jnp.int32, (8, width), 0)


def turn(tile, shift):
    return pltpu.roll(tile, shift, 0)


def where_am_i():
    return lax.axis_index("grp"), lax.axis_index("bis")


def pack_kernel(n, *refs):
    chips = n // 2
    order_in, owner_in, slot_in, sweep_in, state_in = refs[:5]
    chip_bufs, across = refs[5 : 5 + chips], refs[5 + chips]
    order, owner, slot, state, sems = refs[6 + chips :]
    width = state.shape[2]
    rows = state.shape[1]
    home = 8 * (NF + 1)
    copies = [pltpu.make_async_copy(order_in, order, sems.at[0])]
    copies += [pltpu.make_async_copy(state_in.at[field], state.at[field], sems.at[1 + field]) for field in range(NF)]
    copies += [
        pltpu.make_async_copy(owner_in, owner, sems.at[1 + NF]),
        pltpu.make_async_copy(slot_in, slot, sems.at[2 + NF]),
        pltpu.make_async_copy(sweep_in, chip_bufs[0].at[home : home + rows, :], sems.at[3 + NF]),
    ]
    for copy in copies:
        copy.start()
    _, me = where_am_i()
    chip = me // 2
    sub = sublane(width)
    first = me == 0
    copies[0].wait()

    def tile_of(field, block):
        return state[field, pl.ds(pl.multiple_of(block // 2 * 8, 8), 8), :]

    def halo(index):
        block = order[index]
        odd = block % 2 * 4
        near = odd + jnp.where(first, 0, BR - 1)
        far = odd + jnp.where(first, 1, BR - 2)
        tiles = [tile_of(field, block) for field in range(NF)]
        press = (tiles[GAM] - 1.0) * tiles[RHO] * tiles[ENE]
        out = turn(tiles[0], (8 - near) % 8)
        for field in range(1, NF):
            out = jnp.where(sub == field, turn(tiles[field], (field + 8 - near) % 8), out)
        out = jnp.where(sub == FAR_P, turn(press, (FAR_P + 8 - far) % 8), out)
        return jnp.where(sub == FAR_U, turn(tiles[VELU], (FAR_U + 8 - far) % 8), out)

    for field in range(NF):
        copies[1 + field].wait()
        for mask in range(chips):
            goal = chip ^ mask
            low = order[2 * goal]
            high = order[2 * goal + 1]
            even = turn(tile_of(field, low), low % 2 * 4)
            odd = turn(tile_of(field, high), 4 - high % 2 * 4)
            chip_bufs[mask][8 * field : 8 * field + 8, :] = jnp.where(sub < 4, even, odd)
    for mask in range(chips):
        goal = chip ^ mask
        beyond = jnp.where(first, jnp.minimum(2 * goal + 2, n - 1), jnp.maximum(2 * goal - 1, 0))
        chip_bufs[mask][8 * NF : home, :] = halo(beyond)
    across[0:8, :] = halo(jnp.where(first, 0, n - 1))
    for copy in copies[1 + NF :]:
        copy.wait()
    lane = lax.broadcasted_iota(jnp.int32, (1, width), 1)
    for block in range(n):
        line = jnp.where(lane == 0, owner[block], slot[block])
        chip_bufs[0][home + rows + block : home + rows + block + 1, :] = line.astype(jnp.float32)


def step_kernel(n, *refs):
    chips = n // 2
    refs = list(refs)
    take = lambda count: [refs.pop(0) for _ in range(count)]
    owner, slot = take(2)
    mine, theirs = take(chips), take(chips)
    across, across_sib, sweep = take(3)
    (vel,) = take(1)
    sends = take(chips)
    fld, prs, vols, coef, halo, bins, tags, count, staged, named, sem = take(11)
    grp, me = where_am_i()
    chip, core = me // 2, me % 2
    width = sweep.shape[1]
    rows = sweep.shape[0]
    home = 8 * (NF + 1)
    sweep_sib = theirs[0].at[home : home + rows, :]
    tiles = 2 * chips
    sub = sublane(width)
    lane = lax.broadcasted_iota(jnp.int32, (8, width), 1)
    is_low = core == 0

    def pair(own, sib):
        return jnp.where(is_low, own, sib), jnp.where(is_low, sib, own)

    def at(tile):
        return pl.ds(pl.multiple_of(tile * 8, 8), 8)

    staged[...] = theirs[0][home + rows : home + rows + n, 0:128].astype(jnp.int32)
    naming = pltpu.make_async_copy(staged, named, sem)
    naming.start()

    for mask in range(chips):
        source = chip ^ mask
        for field in range(NF):
            span = pl.ds(8 * field, 8)
            even, odd = pair(mine[mask][span, :], theirs[mask][span, :])
            fld[field, at(1 + source), :] = jnp.where(sub < 4, even, turn(odd, 4))
            fld[field, at(1 + chips + source), :] = jnp.where(sub < 4, turn(even, 4), odd)
        even, odd = pair(mine[mask][8 * NF : home, :], theirs[mask][8 * NF : home, :])
        halo[0, source] = even
        halo[1, source] = odd
    even, odd = pair(across[0:8, :], across_sib[0:8, :])
    inside_top = jnp.logical_or(grp > 0, chip > 0)
    inside_bottom = jnp.logical_or(grp < lax.axis_size("grp") - 1, chip < chips - 1)
    top = jnp.where(inside_top, jnp.where(chip == 0, even, halo[1, chips - 1]), 0.0)
    bottom = jnp.where(inside_bottom, jnp.where(chip == chips - 1, odd, halo[0, 0]), 0.0)

    def line(tile, index):
        return jnp.broadcast_to(tile[index : index + 1, :], (8, width))

    for tile, place, near in ((top, 0, 7), (bottom, tiles + 1, 0)):
        span = at(place)
        for field in (RHO, ENE, VELV, GAM):
            fld[field, span, :] = line(tile, field)
        fld[VELU, span, :] = jnp.where(sub == near, line(tile, VELU), line(tile, FAR_U))
        press = (line(tile, GAM) - 1.0) * line(tile, RHO) * line(tile, ENE)
        prs[0, span, :] = jnp.where(sub == near, press, line(tile, FAR_P))

    def left_right(x):
        left = jnp.where(lane == 0, 0.0, pltpu.roll(x, 1, 1))
        right = jnp.where(lane == width - 1, 0.0, pltpu.roll(x, width - 1, 1))
        return right - left

    def down_up(ref, index, tile, x, clip=False):
        before = ref[index, at(jnp.maximum(tile - 1, 0) if clip else tile - 1), :]
        after = ref[index, at(jnp.minimum(tile + 1, tiles + 1) if clip else tile + 1), :]
        return turn(jnp.where(sub == 0, after, x), 7) - turn(jnp.where(sub == 7, before, x), 1)

    def pressure(tile, _):
        span = at(tile)
        prs[0, span, :] = (fld[GAM, span, :] - 1.0) * fld[RHO, span, :] * fld[ENE, span, :]
        return 0

    lax.fori_loop(1, tiles + 1, pressure, 0, unroll=n <= 8)

    def first(tile, _):
        span = at(tile)
        velu, velv, press = fld[VELU, span, :], fld[VELV, span, :], prs[0, span, :]
        push = HALF_DT * (down_up(fld, VELU, tile, velu, True) + left_right(velv))
        grow = 1.0 + push
        scale = HALF_DT / fld[RHO, span, :]
        keep = 1.0 - (fld[GAM, span, :] - 1.0) * push
        nxt_p = press * keep / grow
        nxt_u = velu - down_up(prs, 0, tile, press, True) * scale
        nxt_v = velv - left_right(press) * scale
        prs[1, span, :] = nxt_p
        vols[0, span, :] = nxt_u
        vols[1, span, :] = nxt_v
        vols[2, span, :] = grow
        vols[3, span, :] = fld[ENE, span, :] * keep
        coef[span, :] = scale * grow
        return 0

    lax.fori_loop(0, tiles + 2, first, 0, unroll=n <= 8)
    for place, inside in ((0, inside_top), (tiles + 1, inside_bottom)):
        span = at(place)
        prs[1, span, :] = jnp.where(inside, prs[1, span, :], 0.0)
        vols[0, span, :] = jnp.where(inside, vols[0, span, :], 0.0)

    def velocity(index, _):
        tile = 1 + core * chips + index
        span, dest = at(tile), at(index)
        press, scale = prs[1, span, :], coef[span, :]
        vel[0, dest, :] = vols[0, span, :] - down_up(prs, 1, tile, press) * scale
        vel[1, dest, :] = vols[1, span, :] - left_right(press) * scale
        return 0

    lax.fori_loop(0, chips, velocity, 0, unroll=n <= 8)

    naming.wait()
    for mask in range(chips + 1):
        count[mask] = 0
        tags[mask] = jnp.full((8, 128), -1.0, jnp.float32)
    sub128 = sublane(128)

    def cyclic(x):
        return jnp.where(sub % BR == 0, turn(x, 8 - (BR - 1)), turn(x, 1))

    def place(tile_out, who, where_to):
        fits = who % 2 == core
        mask = jnp.where(fits, (who // 2) ^ chip, chips)
        rank = count[mask]
        count[mask] = jnp.where(fits, rank + 1, 0)
        bins[mask, rank] = tile_out
        tags[mask] = jnp.where(sub128 == rank, jnp.full((8, 128), where_to).astype(jnp.float32), tags[mask])

    def second(device, index):
        tile = 1 + device * chips + index
        span = at(tile)
        push = HALF_DT * (down_up(vols, 0, tile, vols[0, span, :]) + left_right(vols[1, span, :]))
        volume = vols[2, span, :] * (1.0 + push)
        heat_e = vols[3, span, :] * (1.0 - (fld[GAM, span, :] - 1.0) * push)
        mass = fld[RHO, span, :]
        heat = mass * heat_e
        from_own = (core == 0) if device == 0 else (core == 1)
        swept = jnp.where(from_own, sweep[at(index), :], sweep_sib[at(index), :])
        frac = swept * volume / (1.0 + volume)
        mass_go, heat_go = frac * mass, frac * heat
        mass_part = mass - mass_go + cyclic(mass_go)
        heat_part = heat - heat_go + cyclic(heat_go)
        for bit, tile_out in (
            (0, jnp.where(sub < 4, mass_part, turn(heat_part, 4))),
            (1, jnp.where(sub < 4, turn(mass_part, 4), heat_part)),
        ):
            block = 2 * index + bit
            who = jnp.where(from_own, owner[block], named[block, 0])
            where_to = jnp.where(from_own, slot[block], named[block, 1])
            place(tile_out, who, where_to)

    for device in range(2):
        lax.fori_loop(0, chips, lambda index, _, device=device: (second(device, index), 0)[1], 0, unroll=n <= 8)

    for mask in range(chips):
        for rank in range(2 * CAP):
            for part in range(width // 128):
                sends[mask][rank * (width // 128) + part] = bins[mask, rank, :, part * 128 : part * 128 + 128]
        sends[mask][2 * CAP * (width // 128)] = tags[mask]


def land_kernel(n, *refs):
    chips = n // 2
    arrived = refs[:chips]
    mass, energy = refs[chips:]
    parts = mass.shape[1] // 128
    sub = sublane(128)

    def tile_pair(index, _):
        span = pl.ds(pl.multiple_of(index * 8, 8), 8)
        sums = [[jnp.zeros((8, 128), jnp.float32) for _ in range(parts)] for _ in range(2)]
        for buf in arrived:
            tag_tile = buf[2 * CAP * parts]
            for rank in range(2 * CAP):
                tag = jnp.broadcast_to(tag_tile[rank : rank + 1, :], (8, 128))
                for bit in range(2):
                    hit = tag == (2 * index + bit) * 1.0
                    for part in range(parts):
                        sums[bit][part] += jnp.where(hit, buf[rank * parts + part], 0.0)
        for part in range(parts):
            cols = slice(part * 128, part * 128 + 128)
            even, odd = sums[0][part], sums[1][part]
            mass[span, cols] = jnp.where(sub < 4, even, turn(odd, 4))
            energy[span, cols] = jnp.where(sub < 4, turn(even, 4), odd)
        return 0

    lax.fori_loop(0, chips, tile_pair, 0, unroll=n <= 8)


def across_links(groups, n):
    pairs = []
    for grp in range(groups):
        base = grp * n
        pairs += [(base + i, base + i + 1) for i in range(2, n - 2, 2)]
        if grp + 1 < groups:
            turn_at = n - 2 if grp % 2 == 0 else 1
            pairs += [(base + n - 1, base + n), (base + turn_at, base + n + turn_at)]
    used = {i for pair in pairs for i in pair}
    left = [i for i in range(groups * n) if i not in used]
    pairs += [(left[i], left[i + 1]) for i in range(0, len(left), 2)]
    return [link for low, high in pairs for link in ((low, high), (high, low))]


def shards(state, order, sweep, owner, slot_target):
    n = lax.axis_size("bis")
    groups = lax.axis_size("grp")
    chips = n // 2
    rows, width = sweep.shape
    parts = width // 128
    f32 = jnp.float32
    params = pltpu.CompilerParams(vmem_limit_bytes=48 * 1024 * 1024)

    def to_sibling(x):
        return lax.ppermute(x, "bis", [(i, i ^ 1) for i in range(n)])

    def to_chip(x, mask):
        return lax.ppermute(x, "bis", [(i, i ^ 2 * mask) for i in range(n)]) if mask else x

    owner = owner.reshape(n)
    extra = -(-(rows + n) // 8) * 8
    packed = pl.pallas_call(
        functools.partial(pack_kernel, n),
        out_shape=[
            jax.ShapeDtypeStruct((8 * (NF + 1) + (0 if mask else extra), width), f32) for mask in range(chips)
        ]
        + [jax.ShapeDtypeStruct((ZR, width), f32)],
        in_specs=[pl.BlockSpec(memory_space=pl.ANY)] * 5,
        out_specs=[VMEM] * (chips + 1),
        scratch_shapes=[
            pltpu.SMEM((n,), jnp.int32),
            pltpu.SMEM((n,), jnp.int32),
            pltpu.SMEM((n,), jnp.int32),
            pltpu.VMEM((NF, rows, width), f32),
            pltpu.SemaphoreType.DMA((NF + 4,)),
        ],
        compiler_params=params,
        name="pack",
    )(*[pltpu.with_memory_space_constraint(x, pltpu.HBM) for x in (order.reshape(n), owner, slot_target, sweep, state)])
    across = lax.ppermute(packed[chips], ("grp", "bis"), across_links(groups, n))
    mine = [to_chip(packed[mask], mask) for mask in range(chips)]
    theirs = [to_sibling(x) for x in mine]
    across_sib = to_sibling(across)

    stack = (2 * chips + 2) * 8
    send_shape = (2 * CAP * parts + 1, 8, 128)
    out = pl.pallas_call(
        functools.partial(step_kernel, n),
        out_shape=[jax.ShapeDtypeStruct((2, rows, width), f32)]
        + [jax.ShapeDtypeStruct(send_shape, f32)] * chips,
        in_specs=[SMEM] * 2 + [VMEM] * (2 * chips + 3),
        out_specs=[VMEM] * (chips + 1),
        scratch_shapes=[
            pltpu.VMEM((NF, stack, width), f32),
            pltpu.VMEM((2, stack, width), f32),
            pltpu.VMEM((4, stack, width), f32),
            pltpu.VMEM((stack, width), f32),
            pltpu.VMEM((2, chips, 8, width), f32),
            pltpu.VMEM((chips + 1, 2 * CAP, 8, width), f32),
            pltpu.VMEM((chips + 1, 8, 128), f32),
            pltpu.SMEM((chips + 1,), jnp.int32),
            pltpu.VMEM((n, 128), jnp.int32),
            pltpu.SMEM((n, 128), jnp.int32),
            pltpu.SemaphoreType.DMA,
        ],
        compiler_params=params,
        name="substeps",
    )(owner, slot_target, *mine, *theirs, across, across_sib, sweep)
    vel = out[0]
    arrived = [to_chip(out[1 + mask], mask) for mask in range(chips)]
    mass, energy = pl.pallas_call(
        functools.partial(land_kernel, n),
        out_shape=[jax.ShapeDtypeStruct((rows, width), f32)] * 2,
        in_specs=[VMEM] * chips,
        out_specs=[VMEM] * 2,
        compiler_params=params,
        name="land",
    )(*arrived)
    return mass, energy, vel


def solution(mesh):
    placed = (
        P(None, ("grp", "bis"), None),
        P(("grp", "bis"), None),
        P(("grp", "bis"), None),
        P(("grp", "bis"), None),
        P(("grp", "bis")),
    )
    return jax.shard_map(
        shards,
        mesh=mesh,
        in_specs=placed,
        out_specs=(P(("grp", "bis"), None), P(("grp", "bis"), None), P(None, ("grp", "bis"), None)),
        check_vma=False,
    )
```

```python
import functools

import jax
import jax.numpy as jnp
from jax import lax
from jax.experimental import pallas as pl
from jax.experimental.pallas import tpu as pltpu
from jax.sharding import PartitionSpec as P

BR = 4
CAP = 2
ZR = 48
HALF_DT = 0.075
NF = 5
RHO, ENE, VELU, VELV, GAM = range(NF)
FAR_P, FAR_U = 5, 6
SMEM = pl.BlockSpec(memory_space=pltpu.SMEM)
VMEM = pl.BlockSpec(memory_space=pltpu.VMEM)


def sublane(width):
    return lax.broadcasted_iota(jnp.int32, (8, width), 0)


def turn(tile, shift):
    return pltpu.roll(tile, shift, 0)


def where_am_i():
    return lax.axis_index("grp"), lax.axis_index("bis")


def routes(chips):
    bits = chips.bit_length() - 1
    half = bits // 2 if bits % 2 == 0 else 0
    swap = lambda mask: (mask << half | mask >> bits - half) & chips - 1
    masks = sorted(range(1, chips), key=lambda mask: (-mask.bit_count(), mask))
    return [(0, 0)] + [(mask, swap(mask)) for mask in masks]


def reached(route, core):
    return route[0] if route[0] == route[1] else jnp.where(core == 0, route[0], route[1])


def pack_kernel(n, *refs):
    chips = n // 2
    order_in, owner_in, slot_in, sweep_in, state_in = refs[:5]
    chip_bufs, across = refs[5 : 5 + chips], refs[5 + chips]
    order, owner, slot, state, sems = refs[6 + chips :]
    width = state.shape[2]
    rows = state.shape[1]
    home = 8 * (NF + 1)
    copies = [pltpu.make_async_copy(order_in, order, sems.at[0])]
    copies += [pltpu.make_async_copy(state_in.at[field], state.at[field], sems.at[1 + field]) for field in range(NF)]
    copies += [
        pltpu.make_async_copy(owner_in, owner, sems.at[1 + NF]),
        pltpu.make_async_copy(slot_in, slot, sems.at[2 + NF]),
        pltpu.make_async_copy(sweep_in, chip_bufs[0].at[home : home + rows, :], sems.at[3 + NF]),
    ]
    for copy in copies:
        copy.start()
    _, me = where_am_i()
    chip, core = me // 2, me % 2
    sub = sublane(width)
    first = me == 0
    goals = [chip ^ reached(route, core) for route in routes(chips)]
    copies[0].wait()

    def tile_of(field, block):
        return state[field, pl.ds(pl.multiple_of(block // 2 * 8, 8), 8), :]

    def halo(index):
        block = order[index]
        odd = block % 2 * 4
        near = odd + jnp.where(first, 0, BR - 1)
        far = odd + jnp.where(first, 1, BR - 2)
        tiles = [tile_of(field, block) for field in range(NF)]
        press = (tiles[GAM] - 1.0) * tiles[RHO] * tiles[ENE]
        out = turn(tiles[0], (8 - near) % 8)
        for field in range(1, NF):
            out = jnp.where(sub == field, turn(tiles[field], (field + 8 - near) % 8), out)
        out = jnp.where(sub == FAR_P, turn(press, (FAR_P + 8 - far) % 8), out)
        return jnp.where(sub == FAR_U, turn(tiles[VELU], (FAR_U + 8 - far) % 8), out)

    for field in range(NF):
        copies[1 + field].wait()
        for buf, goal in zip(chip_bufs, goals):
            low = order[2 * goal]
            high = order[2 * goal + 1]
            even = turn(tile_of(field, low), low % 2 * 4)
            odd = turn(tile_of(field, high), 4 - high % 2 * 4)
            buf[8 * field : 8 * field + 8, :] = jnp.where(sub < 4, even, odd)
    for buf, goal in zip(chip_bufs, goals):
        beyond = jnp.where(first, jnp.minimum(2 * goal + 2, n - 1), jnp.maximum(2 * goal - 1, 0))
        buf[8 * NF : home, :] = halo(beyond)
    across[0:8, :] = halo(jnp.where(first, 0, n - 1))
    for copy in copies[1 + NF :]:
        copy.wait()
    lane = lax.broadcasted_iota(jnp.int32, (1, width), 1)
    for block in range(n):
        line = jnp.where(lane == 0, owner[block], slot[block])
        chip_bufs[0][home + rows + block : home + rows + block + 1, :] = line.astype(jnp.float32)


def step_kernel(n, *refs):
    chips = n // 2
    refs = list(refs)
    take = lambda count: [refs.pop(0) for _ in range(count)]
    owner, slot = take(2)
    mine, theirs = take(chips), take(chips)
    across, across_sib, sweep = take(3)
    (vel,) = take(1)
    sends = take(chips)
    fld, prs, vols, coef, halo, bins, tags, count, staged, named, sem = take(11)
    grp, me = where_am_i()
    chip, core = me // 2, me % 2
    width = sweep.shape[1]
    rows = sweep.shape[0]
    home = 8 * (NF + 1)
    sweep_sib = theirs[0].at[home : home + rows, :]
    tiles = 2 * chips
    sub = sublane(width)
    lane = lax.broadcasted_iota(jnp.int32, (8, width), 1)
    is_low = core == 0

    def pair(own, sib):
        return jnp.where(is_low, own, sib), jnp.where(is_low, sib, own)

    def at(tile):
        return pl.ds(pl.multiple_of(tile * 8, 8), 8)

    staged[...] = theirs[0][home + rows : home + rows + n, 0:128].astype(jnp.int32)
    naming = pltpu.make_async_copy(staged, named, sem)
    naming.start()

    paths = routes(chips)
    for index, path in enumerate(paths):
        source = chip ^ reached(path, core)
        own, sib = mine[index], theirs[paths.index((path[1], path[0]))]
        for field in range(NF):
            span = pl.ds(8 * field, 8)
            even, odd = pair(own[span, :], sib[span, :])
            fld[field, at(1 + source), :] = jnp.where(sub < 4, even, turn(odd, 4))
            fld[field, at(1 + chips + source), :] = jnp.where(sub < 4, turn(even, 4), odd)
        even, odd = pair(own[8 * NF : home, :], sib[8 * NF : home, :])
        halo[0, source] = even
        halo[1, source] = odd
    even, odd = pair(across[0:8, :], across_sib[0:8, :])
    inside_top = jnp.logical_or(grp > 0, chip > 0)
    inside_bottom = jnp.logical_or(grp < lax.axis_size("grp") - 1, chip < chips - 1)
    top = jnp.where(inside_top, jnp.where(chip == 0, even, halo[1, chips - 1]), 0.0)
    bottom = jnp.where(inside_bottom, jnp.where(chip == chips - 1, odd, halo[0, 0]), 0.0)

    def line(tile, index):
        return jnp.broadcast_to(tile[index : index + 1, :], (8, width))

    for tile, place, near in ((top, 0, 7), (bottom, tiles + 1, 0)):
        span = at(place)
        for field in (RHO, ENE, VELV, GAM):
            fld[field, span, :] = line(tile, field)
        fld[VELU, span, :] = jnp.where(sub == near, line(tile, VELU), line(tile, FAR_U))
        press = (line(tile, GAM) - 1.0) * line(tile, RHO) * line(tile, ENE)
        prs[0, span, :] = jnp.where(sub == near, press, line(tile, FAR_P))

    def left_right(x):
        left = jnp.where(lane == 0, 0.0, pltpu.roll(x, 1, 1))
        right = jnp.where(lane == width - 1, 0.0, pltpu.roll(x, width - 1, 1))
        return right - left

    def down_up(ref, index, tile, x, clip=False):
        before = ref[index, at(jnp.maximum(tile - 1, 0) if clip else tile - 1), :]
        after = ref[index, at(jnp.minimum(tile + 1, tiles + 1) if clip else tile + 1), :]
        return turn(jnp.where(sub == 0, after, x), 7) - turn(jnp.where(sub == 7, before, x), 1)

    def pressure(tile, _):
        span = at(tile)
        prs[0, span, :] = (fld[GAM, span, :] - 1.0) * fld[RHO, span, :] * fld[ENE, span, :]
        return 0

    lax.fori_loop(1, tiles + 1, pressure, 0, unroll=n <= 8)

    def first(tile, _):
        span = at(tile)
        velu, velv, press = fld[VELU, span, :], fld[VELV, span, :], prs[0, span, :]
        push = HALF_DT * (down_up(fld, VELU, tile, velu, True) + left_right(velv))
        grow = 1.0 + push
        scale = HALF_DT / fld[RHO, span, :]
        keep = 1.0 - (fld[GAM, span, :] - 1.0) * push
        nxt_p = press * keep / grow
        nxt_u = velu - down_up(prs, 0, tile, press, True) * scale
        nxt_v = velv - left_right(press) * scale
        prs[1, span, :] = nxt_p
        vols[0, span, :] = nxt_u
        vols[1, span, :] = nxt_v
        vols[2, span, :] = grow
        vols[3, span, :] = fld[ENE, span, :] * keep
        coef[span, :] = scale * grow
        return 0

    lax.fori_loop(0, tiles + 2, first, 0, unroll=n <= 8)
    for place, inside in ((0, inside_top), (tiles + 1, inside_bottom)):
        span = at(place)
        prs[1, span, :] = jnp.where(inside, prs[1, span, :], 0.0)
        vols[0, span, :] = jnp.where(inside, vols[0, span, :], 0.0)

    def velocity(index, _):
        tile = 1 + core * chips + index
        span, dest = at(tile), at(index)
        press, scale = prs[1, span, :], coef[span, :]
        vel[0, dest, :] = vols[0, span, :] - down_up(prs, 1, tile, press) * scale
        vel[1, dest, :] = vols[1, span, :] - left_right(press) * scale
        return 0

    lax.fori_loop(0, chips, velocity, 0, unroll=n <= 8)

    naming.wait()
    for mask in range(chips + 1):
        count[mask] = 0
        tags[mask] = jnp.full((8, 128), -1.0, jnp.float32)
    sub128 = sublane(128)

    def cyclic(x):
        return jnp.where(sub % BR == 0, turn(x, 8 - (BR - 1)), turn(x, 1))

    def place(tile_out, who, where_to):
        fits = who % 2 == core
        mask = jnp.where(fits, (who // 2) ^ chip, chips)
        rank = count[mask]
        count[mask] = jnp.where(fits, rank + 1, 0)
        bins[mask, rank] = tile_out
        tags[mask] = jnp.where(sub128 == rank, jnp.full((8, 128), where_to).astype(jnp.float32), tags[mask])

    def second(device, index):
        tile = 1 + device * chips + index
        span = at(tile)
        push = HALF_DT * (down_up(vols, 0, tile, vols[0, span, :]) + left_right(vols[1, span, :]))
        volume = vols[2, span, :] * (1.0 + push)
        heat_e = vols[3, span, :] * (1.0 - (fld[GAM, span, :] - 1.0) * push)
        mass = fld[RHO, span, :]
        heat = mass * heat_e
        from_own = (core == 0) if device == 0 else (core == 1)
        swept = jnp.where(from_own, sweep[at(index), :], sweep_sib[at(index), :])
        frac = swept * volume / (1.0 + volume)
        mass_go, heat_go = frac * mass, frac * heat
        mass_part = mass - mass_go + cyclic(mass_go)
        heat_part = heat - heat_go + cyclic(heat_go)
        for bit, tile_out in (
            (0, jnp.where(sub < 4, mass_part, turn(heat_part, 4))),
            (1, jnp.where(sub < 4, turn(mass_part, 4), heat_part)),
        ):
            block = 2 * index + bit
            who = jnp.where(from_own, owner[block], named[block, 0])
            where_to = jnp.where(from_own, slot[block], named[block, 1])
            place(tile_out, who, where_to)

    for device in range(2):
        lax.fori_loop(0, chips, lambda index, _, device=device: (second(device, index), 0)[1], 0, unroll=n <= 8)

    for send, path in zip(sends, paths):
        mask = reached(path, core)
        for rank in range(2 * CAP):
            for part in range(width // 128):
                send[rank * (width // 128) + part] = bins[mask, rank, :, part * 128 : part * 128 + 128]
        send[2 * CAP * (width // 128)] = tags[mask]


def land_kernel(n, *refs):
    chips = n // 2
    arrived = refs[:chips]
    mass, energy = refs[chips:]
    parts = mass.shape[1] // 128
    sub = sublane(128)

    def tile_pair(index, _):
        span = pl.ds(pl.multiple_of(index * 8, 8), 8)
        sums = [[jnp.zeros((8, 128), jnp.float32) for _ in range(parts)] for _ in range(2)]
        for buf in arrived:
            tag_tile = buf[2 * CAP * parts]
            for rank in range(2 * CAP):
                tag = jnp.broadcast_to(tag_tile[rank : rank + 1, :], (8, 128))
                for bit in range(2):
                    hit = tag == (2 * index + bit) * 1.0
                    for part in range(parts):
                        sums[bit][part] += jnp.where(hit, buf[rank * parts + part], 0.0)
        for part in range(parts):
            cols = slice(part * 128, part * 128 + 128)
            even, odd = sums[0][part], sums[1][part]
            mass[span, cols] = jnp.where(sub < 4, even, turn(odd, 4))
            energy[span, cols] = jnp.where(sub < 4, turn(even, 4), odd)
        return 0

    lax.fori_loop(0, chips, tile_pair, 0, unroll=n <= 8)


def across_links(groups, n):
    pairs = []
    for grp in range(groups):
        base = grp * n
        pairs += [(base + i, base + i + 1) for i in range(2, n - 2, 2)]
        if grp + 1 < groups:
            turn_at = n - 2 if grp % 2 == 0 else 1
            pairs += [(base + n - 1, base + n), (base + turn_at, base + n + turn_at)]
    used = {i for pair in pairs for i in pair}
    left = [i for i in range(groups * n) if i not in used]
    pairs += [(left[i], left[i + 1]) for i in range(0, len(left), 2)]
    return [link for low, high in pairs for link in ((low, high), (high, low))]


def shards(state, order, sweep, owner, slot_target):
    n = lax.axis_size("bis")
    groups = lax.axis_size("grp")
    chips = n // 2
    rows, width = sweep.shape
    parts = width // 128
    f32 = jnp.float32
    params = pltpu.CompilerParams(vmem_limit_bytes=48 * 1024 * 1024)

    def to_sibling(x):
        return lax.ppermute(x, "bis", [(i, i ^ 1) for i in range(n)])

    def to_chip(x, path):
        return lax.ppermute(x, "bis", [(i, i ^ 2 * path[i % 2]) for i in range(n)]) if path[0] else x

    paths = routes(chips)

    owner = owner.reshape(n)
    extra = -(-(rows + n) // 8) * 8
    packed = pl.pallas_call(
        functools.partial(pack_kernel, n),
        out_shape=[
            jax.ShapeDtypeStruct((8 * (NF + 1) + (0 if mask else extra), width), f32) for mask in range(chips)
        ]
        + [jax.ShapeDtypeStruct((ZR, width), f32)],
        in_specs=[pl.BlockSpec(memory_space=pl.ANY)] * 5,
        out_specs=[VMEM] * (chips + 1),
        scratch_shapes=[
            pltpu.SMEM((n,), jnp.int32),
            pltpu.SMEM((n,), jnp.int32),
            pltpu.SMEM((n,), jnp.int32),
            pltpu.VMEM((NF, rows, width), f32),
            pltpu.SemaphoreType.DMA((NF + 4,)),
        ],
        compiler_params=params,
        name="pack",
    )(*[pltpu.with_memory_space_constraint(x, pltpu.HBM) for x in (order.reshape(n), owner, slot_target, sweep, state)])
    across = lax.ppermute(packed[chips], ("grp", "bis"), across_links(groups, n))
    mine = [to_chip(x, path) for x, path in zip(packed, paths)]
    theirs = [to_sibling(x) for x in mine]
    across_sib = to_sibling(across)

    stack = (2 * chips + 2) * 8
    send_shape = (2 * CAP * parts + 1, 8, 128)
    out = pl.pallas_call(
        functools.partial(step_kernel, n),
        out_shape=[jax.ShapeDtypeStruct((2, rows, width), f32)]
        + [jax.ShapeDtypeStruct(send_shape, f32)] * chips,
        in_specs=[SMEM] * 2 + [VMEM] * (2 * chips + 3),
        out_specs=[VMEM] * (chips + 1),
        scratch_shapes=[
            pltpu.VMEM((NF, stack, width), f32),
            pltpu.VMEM((2, stack, width), f32),
            pltpu.VMEM((4, stack, width), f32),
            pltpu.VMEM((stack, width), f32),
            pltpu.VMEM((2, chips, 8, width), f32),
            pltpu.VMEM((chips + 1, 2 * CAP, 8, width), f32),
            pltpu.VMEM((chips + 1, 8, 128), f32),
            pltpu.SMEM((chips + 1,), jnp.int32),
            pltpu.VMEM((n, 128), jnp.int32),
            pltpu.SMEM((n, 128), jnp.int32),
            pltpu.SemaphoreType.DMA,
        ],
        compiler_params=params,
        name="substeps",
    )(owner, slot_target, *mine, *theirs, across, across_sib, sweep)
    vel = out[0]
    arrived = [to_chip(x, path) for x, path in zip(out[1:], paths)]
    mass, energy = pl.pallas_call(
        functools.partial(land_kernel, n),
        out_shape=[jax.ShapeDtypeStruct((rows, width), f32)] * 2,
        in_specs=[VMEM] * chips,
        out_specs=[VMEM] * 2,
        compiler_params=params,
        name="land",
    )(*arrived)
    return mass, energy, vel


def solution(mesh):
    placed = (
        P(None, ("grp", "bis"), None),
        P(("grp", "bis"), None),
        P(("grp", "bis"), None),
        P(("grp", "bis"), None),
        P(("grp", "bis")),
    )
    return jax.shard_map(
        shards,
        mesh=mesh,
        in_specs=placed,
        out_specs=(P(("grp", "bis"), None), P(("grp", "bis"), None), P(None, ("grp", "bis"), None)),
        check_vma=False,
    )
```

```python
import functools

import jax
import jax.numpy as jnp
from jax import lax
from jax.experimental import pallas as pl
from jax.experimental.pallas import tpu as pltpu
from jax.sharding import PartitionSpec as P

BR = 4
CAP = 2
ZR = 48
HALF_DT = 0.075
NF = 5
RHO, ENE, VELU, VELV, GAM = range(NF)
FAR_P, FAR_U = 5, 6
SMEM = pl.BlockSpec(memory_space=pltpu.SMEM)
VMEM = pl.BlockSpec(memory_space=pltpu.VMEM)


def sublane(width):
    return lax.broadcasted_iota(jnp.int32, (8, width), 0)


def turn(tile, shift):
    return pltpu.roll(tile, shift, 0)


def left_right(x):
    width = x.shape[1]
    lane = lax.broadcasted_iota(jnp.int32, x.shape, 1)
    left = jnp.where(lane == 0, 0.0, pltpu.roll(x, 1, 1))
    right = jnp.where(lane == width - 1, 0.0, pltpu.roll(x, width - 1, 1))
    return right - left


def at(tile):
    return pl.ds(pl.multiple_of(tile * 8, 8), 8)


def down_up(ref, tile, x, clip=None):
    sub = sublane(x.shape[1])
    before = ref[at(tile - 1 if clip is None else jnp.maximum(tile - 1, 0)), :]
    after = ref[at(tile + 1 if clip is None else jnp.minimum(tile + 1, clip)), :]
    return turn(jnp.where(sub == 0, after, x), 7) - turn(jnp.where(sub == 7, before, x), 1)


def where_am_i():
    return lax.axis_index("grp"), lax.axis_index("bis")


def routes(chips):
    bits = chips.bit_length() - 1
    half = bits // 2 if bits % 2 == 0 else 0
    swap = lambda mask: (mask << half | mask >> bits - half) & chips - 1
    masks = sorted(range(1, chips), key=lambda mask: (-mask.bit_count(), mask))
    return [(0, 0)] + [(mask, swap(mask)) for mask in masks]


def reached(route, core):
    return route[0] if route[0] == route[1] else jnp.where(core == 0, route[0], route[1])


def pack_kernel(n, *refs):
    chips = n // 2
    order_in, owner_in, slot_in, sweep_in, state_in = refs[:5]
    chip_bufs, across = refs[5 : 5 + chips], refs[5 + chips]
    order, owner, slot, state, sems = refs[6 + chips :]
    width = state.shape[2]
    rows = state.shape[1]
    home = 8 * (NF + 1)
    copies = [pltpu.make_async_copy(order_in, order, sems.at[0])]
    copies += [pltpu.make_async_copy(state_in.at[field], state.at[field], sems.at[1 + field]) for field in range(NF)]
    copies += [
        pltpu.make_async_copy(owner_in, owner, sems.at[1 + NF]),
        pltpu.make_async_copy(slot_in, slot, sems.at[2 + NF]),
        pltpu.make_async_copy(sweep_in, chip_bufs[0].at[home : home + rows, :], sems.at[3 + NF]),
    ]
    for copy in copies:
        copy.start()
    _, me = where_am_i()
    chip, core = me // 2, me % 2
    sub = sublane(width)
    first = me == 0
    goals = [chip ^ reached(route, core) for route in routes(chips)]
    copies[0].wait()

    def tile_of(field, block):
        return state[field, pl.ds(pl.multiple_of(block // 2 * 8, 8), 8), :]

    def halo(index):
        block = order[index]
        odd = block % 2 * 4
        near = odd + jnp.where(first, 0, BR - 1)
        far = odd + jnp.where(first, 1, BR - 2)
        tiles = [tile_of(field, block) for field in range(NF)]
        press = (tiles[GAM] - 1.0) * tiles[RHO] * tiles[ENE]
        out = turn(tiles[0], (8 - near) % 8)
        for field in range(1, NF):
            out = jnp.where(sub == field, turn(tiles[field], (field + 8 - near) % 8), out)
        out = jnp.where(sub == FAR_P, turn(press, (FAR_P + 8 - far) % 8), out)
        return jnp.where(sub == FAR_U, turn(tiles[VELU], (FAR_U + 8 - far) % 8), out)

    for field in range(NF):
        copies[1 + field].wait()
        for buf, goal in zip(chip_bufs, goals):
            low = order[2 * goal]
            high = order[2 * goal + 1]
            even = turn(tile_of(field, low), low % 2 * 4)
            odd = turn(tile_of(field, high), 4 - high % 2 * 4)
            buf[8 * field : 8 * field + 8, :] = jnp.where(sub < 4, even, odd)
    for buf, goal in zip(chip_bufs, goals):
        beyond = jnp.where(first, jnp.minimum(2 * goal + 2, n - 1), jnp.maximum(2 * goal - 1, 0))
        buf[8 * NF : home, :] = halo(beyond)
    across[0:8, :] = halo(jnp.where(first, 0, n - 1))
    for copy in copies[1 + NF :]:
        copy.wait()
    lane = lax.broadcasted_iota(jnp.int32, (1, width), 1)
    for block in range(n):
        line = jnp.where(lane < width // 2, owner[block], slot[block])
        chip_bufs[0][home + rows + block : home + rows + block + 1, :] = line.astype(jnp.float32)


def tag_kernel(n, rows, own_home, sib_home, code, tags):
    chips = n // 2
    width = own_home.shape[1]
    _, me = where_am_i()
    chip, core = me // 2, me % 2
    span = pl.ds(8 * (NF + 1) + rows, n)
    own, sib = own_home[span, :].astype(jnp.int32), sib_home[span, :].astype(jnp.int32)
    both = (jnp.where(core == 0, own, sib), jnp.where(core == 0, sib, own))
    line_id = lax.broadcasted_iota(jnp.int32, (n, 128), 0)
    sub = sublane(128)
    slots = []
    for device, info in enumerate(both):
        owner = info[:, 0:128]
        rank = jnp.zeros((n, 128), jnp.int32)
        for block in range(n):
            same = jnp.logical_and(owner == owner[block : block + 1, :], line_id > block)
            rank = jnp.where(same, rank + 1, rank)
        mine = (owner & 1) == core
        place = ((owner >> 1) ^ chip) * (2 * CAP) + (device * CAP) + rank
        slots.append(jnp.where(mine, place, -1))
        code[device] = slots[device]
    for index, path in enumerate(routes(chips)):
        want = sub + reached(path, core) * (2 * CAP)
        tile = jnp.full((8, 128), -1, jnp.int32)
        for device, info in enumerate(both):
            for block in range(n):
                hit = jnp.logical_and(want == slots[device][block : block + 1, :], sub < 2 * CAP)
                tile = jnp.where(hit, info[block : block + 1, width - 128 :], tile)
        tags[index] = tile.astype(jnp.float32)


def step_kernel(n, *refs):
    chips = n // 2
    refs = list(refs)
    take = lambda count: [refs.pop(0) for _ in range(count)]
    code, tags = take(2)
    mine, theirs = take(chips), take(chips)
    across, across_sib, sweep = take(3)
    nxt_prs, nxt_u, nxt_v, coef = take(4)
    sends = take(chips)
    fld, prs, vols, halo, parts = take(5)
    grp, me = where_am_i()
    chip, core = me // 2, me % 2
    width = sweep.shape[1]
    rows = sweep.shape[0]
    home = 8 * (NF + 1)
    sweep_sib = theirs[0].at[home : home + rows, :]
    tiles = 2 * chips
    sub = sublane(width)
    is_low = core == 0

    def pair(own, sib):
        return jnp.where(is_low, own, sib), jnp.where(is_low, sib, own)

    paths = routes(chips)
    for index, path in enumerate(paths):
        source = chip ^ reached(path, core)
        own, sib = mine[index], theirs[paths.index((path[1], path[0]))]
        for field in range(NF):
            span = pl.ds(8 * field, 8)
            even, odd = pair(own[span, :], sib[span, :])
            fld[field, at(1 + source), :] = jnp.where(sub < 4, even, turn(odd, 4))
            fld[field, at(1 + chips + source), :] = jnp.where(sub < 4, turn(even, 4), odd)
        even, odd = pair(own[8 * NF : home, :], sib[8 * NF : home, :])
        halo[0, source] = even
        halo[1, source] = odd
    even, odd = pair(across[0:8, :], across_sib[0:8, :])
    inside_top = jnp.logical_or(grp > 0, chip > 0)
    inside_bottom = jnp.logical_or(grp < lax.axis_size("grp") - 1, chip < chips - 1)
    top = jnp.where(inside_top, jnp.where(chip == 0, even, halo[1, chips - 1]), 0.0)
    bottom = jnp.where(inside_bottom, jnp.where(chip == chips - 1, odd, halo[0, 0]), 0.0)

    def line(tile, index):
        return jnp.broadcast_to(tile[index : index + 1, :], (8, width))

    for tile, place, near in ((top, 0, 7), (bottom, tiles + 1, 0)):
        span = at(place)
        for field in (RHO, ENE, VELV, GAM):
            fld[field, span, :] = line(tile, field)
        fld[VELU, span, :] = jnp.where(sub == near, line(tile, VELU), line(tile, FAR_U))
        press = (line(tile, GAM) - 1.0) * line(tile, RHO) * line(tile, ENE)
        prs[span, :] = jnp.where(sub == near, press, line(tile, FAR_P))

    def pressure(tile, _):
        span = at(tile)
        prs[span, :] = (fld[GAM, span, :] - 1.0) * fld[RHO, span, :] * fld[ENE, span, :]
        return 0

    lax.fori_loop(1, tiles + 1, pressure, 0, unroll=n <= 8)

    def first(tile, _):
        span = at(tile)
        velu, velv, press = fld[VELU, span, :], fld[VELV, span, :], prs[span, :]
        push = HALF_DT * (down_up(fld.at[VELU], tile, velu, tiles + 1) + left_right(velv))
        grow = 1.0 + push
        scale = HALF_DT / fld[RHO, span, :]
        keep = 1.0 - (fld[GAM, span, :] - 1.0) * push
        nxt_prs[span, :] = press * keep / grow
        nxt_u[span, :] = velu - down_up(prs, tile, press, tiles + 1) * scale
        nxt_v[span, :] = velv - left_right(press) * scale
        coef[span, :] = scale * grow
        vols[0, span, :] = grow
        vols[1, span, :] = fld[ENE, span, :] * keep
        return 0

    lax.fori_loop(0, tiles + 2, first, 0, unroll=n <= 8)
    for place, inside in ((0, inside_top), (tiles + 1, inside_bottom)):
        span = at(place)
        nxt_prs[span, :] = jnp.where(inside, nxt_prs[span, :], 0.0)
        nxt_u[span, :] = jnp.where(inside, nxt_u[span, :], 0.0)

    def cyclic(x):
        return jnp.where(sub % BR == 0, turn(x, 8 - (BR - 1)), turn(x, 1))

    def second(device, index):
        tile = 1 + device * chips + index
        span = at(tile)
        push = HALF_DT * (down_up(nxt_u, tile, nxt_u[span, :]) + left_right(nxt_v[span, :]))
        volume = vols[0, span, :] * (1.0 + push)
        heat_e = vols[1, span, :] * (1.0 - (fld[GAM, span, :] - 1.0) * push)
        mass = fld[RHO, span, :]
        heat = mass * heat_e
        from_own = (core == 0) if device == 0 else (core == 1)
        swept = jnp.where(from_own, sweep[at(index), :], sweep_sib[at(index), :])
        frac = swept * volume / (1.0 + volume)
        mass_go, heat_go = frac * mass, frac * heat
        mass_part = mass - mass_go + cyclic(mass_go)
        heat_part = heat - heat_go + cyclic(heat_go)
        parts[device, 2 * index] = jnp.where(sub < 4, mass_part, turn(heat_part, 4))
        parts[device, 2 * index + 1] = jnp.where(sub < 4, turn(mass_part, 4), heat_part)

    for device in range(2):
        lax.fori_loop(0, chips, lambda index, _, device=device: (second(device, index), 0)[1], 0, unroll=n <= 8)

    pieces = width // 128
    for index, (send, path) in enumerate(zip(sends, paths)):
        base = reached(path, core) * (2 * CAP)
        for device in range(2):
            for turn_of in range(CAP):
                rank = device * CAP + turn_of
                found = [jnp.zeros((8, 128), jnp.float32)] * pieces
                for block in range(n):
                    hit = jnp.broadcast_to(code[device, block : block + 1, :], (8, 128)) == base + rank
                    found = [
                        jnp.where(hit, parts[device, block, :, piece * 128 : piece * 128 + 128], found[piece])
                        for piece in range(pieces)
                    ]
                for piece in range(pieces):
                    send[rank * pieces + piece] = found[piece]
        send[2 * CAP * pieces] = tags[index]


def velocity_kernel(n, prs, velu, velv, coef, vel):
    chips = n // 2
    _, me = where_am_i()

    def one(index, _):
        tile = 1 + me % 2 * chips + index
        span, dest = at(tile), at(index)
        press, scale = prs[span, :], coef[span, :]
        vel[0, dest, :] = velu[span, :] - down_up(prs, tile, press) * scale
        vel[1, dest, :] = velv[span, :] - left_right(press) * scale
        return 0

    lax.fori_loop(0, chips, one, 0, unroll=n <= 8)


def land_kernel(n, *refs):
    chips = n // 2
    arrived = refs[:chips]
    mass_out, energy_out, mass, energy, sems = refs[chips:]
    parts = mass.shape[1] // 128
    sub = sublane(128)

    def send(source, target, which, index):
        span = pl.ds(pl.multiple_of(index * 8, 8), 8)
        return pltpu.make_async_copy(source.at[span, :], target.at[span, :], sems.at[which, index])

    def tile_pair(index, _):
        span = pl.ds(pl.multiple_of(index * 8, 8), 8)
        sums = [[jnp.zeros((8, 128), jnp.float32) for _ in range(parts)] for _ in range(2)]
        for buf in arrived:
            tag_tile = buf[2 * CAP * parts]
            for rank in range(2 * CAP):
                tag = jnp.broadcast_to(tag_tile[rank : rank + 1, :], (8, 128))
                for bit in range(2):
                    hit = tag == (2 * index + bit) * 1.0
                    for part in range(parts):
                        sums[bit][part] += jnp.where(hit, buf[rank * parts + part], 0.0)
        for part in range(parts):
            cols = slice(part * 128, part * 128 + 128)
            even, odd = sums[0][part], sums[1][part]
            mass[span, cols] = jnp.where(sub < 4, even, turn(odd, 4))
            energy[span, cols] = jnp.where(sub < 4, turn(even, 4), odd)
        send(mass, mass_out, 0, index).start()
        send(energy, energy_out, 1, index).start()
        return 0

    lax.fori_loop(0, chips, tile_pair, 0, unroll=n <= 8)
    for index in range(chips):
        send(mass, mass_out, 0, index).wait()
        send(energy, energy_out, 1, index).wait()


def across_links(groups, n):
    pairs = []
    for grp in range(groups):
        base = grp * n
        pairs += [(base + i, base + i + 1) for i in range(2, n - 2, 2)]
        if grp + 1 < groups:
            turn_at = n - 2 if grp % 2 == 0 else 1
            pairs += [(base + n - 1, base + n), (base + turn_at, base + n + turn_at)]
    used = {i for pair in pairs for i in pair}
    left = [i for i in range(groups * n) if i not in used]
    pairs += [(left[i], left[i + 1]) for i in range(0, len(left), 2)]
    return [link for low, high in pairs for link in ((low, high), (high, low))]


def shards(state, order, sweep, owner, slot_target):
    n = lax.axis_size("bis")
    groups = lax.axis_size("grp")
    chips = n // 2
    rows, width = sweep.shape
    parts = width // 128
    f32 = jnp.float32
    params = pltpu.CompilerParams(vmem_limit_bytes=48 * 1024 * 1024)

    def to_sibling(x):
        return lax.ppermute(x, "bis", [(i, i ^ 1) for i in range(n)])

    def to_chip(x, path):
        return lax.ppermute(x, "bis", [(i, i ^ 2 * path[i % 2]) for i in range(n)]) if path[0] else x

    paths = routes(chips)

    owner = owner.reshape(n)
    extra = -(-(rows + n) // 8) * 8
    packed = pl.pallas_call(
        functools.partial(pack_kernel, n),
        out_shape=[
            jax.ShapeDtypeStruct((8 * (NF + 1) + (0 if mask else extra), width), f32) for mask in range(chips)
        ]
        + [jax.ShapeDtypeStruct((ZR, width), f32)],
        in_specs=[pl.BlockSpec(memory_space=pl.ANY)] * 5,
        out_specs=[VMEM] * (chips + 1),
        scratch_shapes=[
            pltpu.SMEM((n,), jnp.int32),
            pltpu.SMEM((n,), jnp.int32),
            pltpu.SMEM((n,), jnp.int32),
            pltpu.VMEM((NF, rows, width), f32),
            pltpu.SemaphoreType.DMA((NF + 4,)),
        ],
        compiler_params=params,
        name="pack",
    )(*[pltpu.with_memory_space_constraint(x, pltpu.HBM) for x in (order.reshape(n), owner, slot_target, sweep, state)])
    across = lax.ppermute(packed[chips], ("grp", "bis"), across_links(groups, n))
    mine = [to_chip(x, path) for x, path in zip(packed, paths)]
    theirs = [to_sibling(x) for x in mine]
    across_sib = to_sibling(across)

    code, tags = pl.pallas_call(
        functools.partial(tag_kernel, n, rows),
        out_shape=[
            jax.ShapeDtypeStruct((2, n, 128), jnp.int32),
            jax.ShapeDtypeStruct((chips, 8, 128), f32),
        ],
        in_specs=[VMEM] * 2,
        out_specs=[VMEM] * 2,
        compiler_params=params,
        name="tags",
    )(mine[0], theirs[0])

    stack = (2 * chips + 2) * 8
    send_shape = (2 * CAP * parts + 1, 8, 128)
    out = pl.pallas_call(
        functools.partial(step_kernel, n),
        out_shape=[jax.ShapeDtypeStruct((stack, width), f32)] * 4
        + [jax.ShapeDtypeStruct(send_shape, f32)] * chips,
        in_specs=[VMEM] * (2 * chips + 5),
        out_specs=[VMEM] * (chips + 4),
        scratch_shapes=[
            pltpu.VMEM((NF, stack, width), f32),
            pltpu.VMEM((stack, width), f32),
            pltpu.VMEM((2, stack, width), f32),
            pltpu.VMEM((2, chips, 8, width), f32),
            pltpu.VMEM((2, n, 8, width), f32),
        ],
        compiler_params=params,
        name="substeps",
    )(code, tags, *mine, *theirs, across, across_sib, sweep)
    arrived = [to_chip(x, path) for x, path in zip(out[4:], paths)]
    vel = pl.pallas_call(
        functools.partial(velocity_kernel, n),
        out_shape=jax.ShapeDtypeStruct((2, rows, width), f32),
        in_specs=[VMEM] * 4,
        out_specs=VMEM,
        compiler_params=params,
        name="velocities",
    )(*out[:4])
    mass, energy = pl.pallas_call(
        functools.partial(land_kernel, n),
        out_shape=[jax.ShapeDtypeStruct((rows, width), f32)] * 2,
        in_specs=[VMEM] * chips,
        out_specs=[pl.BlockSpec(memory_space=pl.ANY)] * 2,
        scratch_shapes=[
            pltpu.VMEM((rows, width), f32),
            pltpu.VMEM((rows, width), f32),
            pltpu.SemaphoreType.DMA((2, chips)),
        ],
        compiler_params=params,
        name="land",
    )(*arrived)
    return mass, energy, vel


def solution(mesh):
    placed = (
        P(None, ("grp", "bis"), None),
        P(("grp", "bis"), None),
        P(("grp", "bis"), None),
        P(("grp", "bis"), None),
        P(("grp", "bis")),
    )
    return jax.shard_map(
        shards,
        mesh=mesh,
        in_specs=placed,
        out_specs=(P(("grp", "bis"), None), P(("grp", "bis"), None), P(None, ("grp", "bis"), None)),
        check_vma=False,
    )
```

```python
import functools

import jax
import jax.numpy as jnp
from jax import lax
from jax.experimental import pallas as pl
from jax.experimental.pallas import tpu as pltpu
from jax.sharding import PartitionSpec as P

BR = 4
CAP = 2
ZR = 8
HALF_DT = 0.075
NF = 5
RHO, ENE, VELU, VELV, GAM = range(NF)
FAR_P, FAR_U = 5, 6
SMEM = pl.BlockSpec(memory_space=pltpu.SMEM)
VMEM = pl.BlockSpec(memory_space=pltpu.VMEM)


def sublane(width):
    return lax.broadcasted_iota(jnp.int32, (8, width), 0)


def turn(tile, shift):
    return pltpu.roll(tile, shift, 0)


def left_right(x):
    width = x.shape[1]
    lane = lax.broadcasted_iota(jnp.int32, x.shape, 1)
    left = jnp.where(lane == 0, 0.0, pltpu.roll(x, 1, 1))
    right = jnp.where(lane == width - 1, 0.0, pltpu.roll(x, width - 1, 1))
    return right - left


def at(tile):
    return pl.ds(pl.multiple_of(tile * 8, 8), 8)


def down_up(ref, tile, x, clip=None):
    sub = sublane(x.shape[1])
    before = ref[at(tile - 1 if clip is None else jnp.maximum(tile - 1, 0)), :]
    after = ref[at(tile + 1 if clip is None else jnp.minimum(tile + 1, clip)), :]
    return turn(jnp.where(sub == 0, after, x), 7) - turn(jnp.where(sub == 7, before, x), 1)


def where_am_i():
    return lax.axis_index("grp"), lax.axis_index("bis")


def routes(chips):
    bits = chips.bit_length() - 1
    half = bits // 2 if bits % 2 == 0 else 0
    swap = lambda mask: (mask << half | mask >> bits - half) & chips - 1
    masks = sorted(range(1, chips), key=lambda mask: (-mask.bit_count(), mask))
    return [(0, 0)] + [(mask, swap(mask)) for mask in masks]


def reached(route, core):
    return route[0] if route[0] == route[1] else jnp.where(core == 0, route[0], route[1])


def pack_kernel(n, *refs):
    chips = n // 2
    order_in, owner_in, slot_in, sweep_in, state_in = refs[:5]
    chip_bufs, across = refs[5 : 5 + chips], refs[5 + chips]
    order, owner, slot, state, sems = refs[6 + chips :]
    width = state.shape[2]
    rows = state.shape[1]
    home = 8 * (NF + 1)
    copies = [pltpu.make_async_copy(order_in, order, sems.at[0])]
    copies += [pltpu.make_async_copy(state_in.at[field], state.at[field], sems.at[1 + field]) for field in range(NF)]
    copies += [
        pltpu.make_async_copy(owner_in, owner, sems.at[1 + NF]),
        pltpu.make_async_copy(slot_in, slot, sems.at[2 + NF]),
        pltpu.make_async_copy(sweep_in, chip_bufs[0].at[home : home + rows, :], sems.at[3 + NF]),
    ]
    for copy in copies:
        copy.start()
    _, me = where_am_i()
    chip, core = me // 2, me % 2
    sub = sublane(width)
    first = me == 0
    goals = [chip ^ reached(route, core) for route in routes(chips)]
    copies[0].wait()

    def tile_of(field, block):
        return state[field, pl.ds(pl.multiple_of(block // 2 * 8, 8), 8), :]

    def halo(buf, base, index):
        block = order[index]
        near = block * 4 + jnp.where(first, 0, BR - 1)
        far = block * 4 + jnp.where(first, 1, BR - 2)
        for field in range(NF):
            buf[base + field : base + field + 1, :] = state[field, pl.ds(near, 1), :]
        line = lambda field: state[field, pl.ds(far, 1), :]
        buf[base + FAR_P : base + FAR_P + 1, :] = (line(GAM) - 1.0) * line(RHO) * line(ENE)
        buf[base + FAR_U : base + FAR_U + 1, :] = line(VELU)

    for field in range(NF):
        copies[1 + field].wait()
        for buf, goal in zip(chip_bufs, goals):
            low = order[2 * goal]
            high = order[2 * goal + 1]
            for line in range(BR):
                buf[8 * field + line : 8 * field + line + 1, :] = state[field, pl.ds(low * BR + line, 1), :]
                buf[8 * field + BR + line : 8 * field + BR + line + 1, :] = state[field, pl.ds(high * BR + line, 1), :]
    for buf, goal in zip(chip_bufs, goals):
        beyond = jnp.where(first, jnp.minimum(2 * goal + 2, n - 1), jnp.maximum(2 * goal - 1, 0))
        halo(buf, 8 * NF, beyond)
    halo(across, 0, jnp.where(first, 0, n - 1))
    for copy in copies[1 + NF :]:
        copy.wait()
    lane = lax.broadcasted_iota(jnp.int32, (1, width), 1)
    for block in range(n):
        line = jnp.where(lane < width // 2, owner[block], slot[block])
        chip_bufs[0][home + rows + block : home + rows + block + 1, :] = line.astype(jnp.float32)


def tag_kernel(n, rows, own_home, sib_home, code, tags):
    chips = n // 2
    width = own_home.shape[1]
    _, me = where_am_i()
    chip, core = me // 2, me % 2
    span = pl.ds(8 * (NF + 1) + rows, n)
    own, sib = own_home[span, :].astype(jnp.int32), sib_home[span, :].astype(jnp.int32)
    both = (jnp.where(core == 0, own, sib), jnp.where(core == 0, sib, own))
    line_id = lax.broadcasted_iota(jnp.int32, (n, 128), 0)
    sub = sublane(128)
    slots = []
    for device, info in enumerate(both):
        owner = info[:, 0:128]
        rank = jnp.zeros((n, 128), jnp.int32)
        for block in range(n):
            same = jnp.logical_and(owner == owner[block : block + 1, :], line_id > block)
            rank = jnp.where(same, rank + 1, rank)
        mine = (owner & 1) == core
        place = ((owner >> 1) ^ chip) * (2 * CAP) + (device * CAP) + rank
        slots.append(jnp.where(mine, place, -1))
        code[device] = slots[device]
    for index, path in enumerate(routes(chips)):
        want = sub + reached(path, core) * (2 * CAP)
        tile = jnp.full((8, 128), -1, jnp.int32)
        for device, info in enumerate(both):
            for block in range(n):
                hit = jnp.logical_and(want == slots[device][block : block + 1, :], sub < 2 * CAP)
                tile = jnp.where(hit, info[block : block + 1, width - 128 :], tile)
        tags[index] = tile.astype(jnp.float32)


def step_kernel(n, *refs):
    chips = n // 2
    refs = list(refs)
    take = lambda count: [refs.pop(0) for _ in range(count)]
    code, tags = take(2)
    mine, theirs = take(chips), take(chips)
    across, across_sib, sweep = take(3)
    nxt_prs, nxt_u, nxt_v, coef = take(4)
    sends = take(chips)
    fld, prs, vols, halo, parts = take(5)
    grp, me = where_am_i()
    chip, core = me // 2, me % 2
    width = sweep.shape[1]
    rows = sweep.shape[0]
    home = 8 * (NF + 1)
    sweep_sib = theirs[0].at[home : home + rows, :]
    tiles = 2 * chips
    sub = sublane(width)
    is_low = core == 0

    def pair(own, sib):
        return jnp.where(is_low, own, sib), jnp.where(is_low, sib, own)

    paths = routes(chips)
    for index, path in enumerate(paths):
        source = chip ^ reached(path, core)
        own, sib = mine[index], theirs[paths.index((path[1], path[0]))]
        for field in range(NF):
            span = pl.ds(8 * field, 8)
            even, odd = pair(own[span, :], sib[span, :])
            fld[field, at(1 + source), :] = jnp.where(sub < 4, even, turn(odd, 4))
            fld[field, at(1 + chips + source), :] = jnp.where(sub < 4, turn(even, 4), odd)
        even, odd = pair(own[8 * NF : home, :], sib[8 * NF : home, :])
        halo[0, source] = even
        halo[1, source] = odd
    even, odd = pair(across[0:8, :], across_sib[0:8, :])
    inside_top = jnp.logical_or(grp > 0, chip > 0)
    inside_bottom = jnp.logical_or(grp < lax.axis_size("grp") - 1, chip < chips - 1)
    top = jnp.where(inside_top, jnp.where(chip == 0, even, halo[1, chips - 1]), 0.0)
    bottom = jnp.where(inside_bottom, jnp.where(chip == chips - 1, odd, halo[0, 0]), 0.0)

    def line(tile, index):
        return jnp.broadcast_to(tile[index : index + 1, :], (8, width))

    for tile, place, near in ((top, 0, 7), (bottom, tiles + 1, 0)):
        span = at(place)
        for field in (RHO, ENE, VELV, GAM):
            fld[field, span, :] = line(tile, field)
        fld[VELU, span, :] = jnp.where(sub == near, line(tile, VELU), line(tile, FAR_U))
        press = (line(tile, GAM) - 1.0) * line(tile, RHO) * line(tile, ENE)
        prs[span, :] = jnp.where(sub == near, press, line(tile, FAR_P))

    def pressure(tile, _):
        span = at(tile)
        prs[span, :] = (fld[GAM, span, :] - 1.0) * fld[RHO, span, :] * fld[ENE, span, :]
        return 0

    lax.fori_loop(1, tiles + 1, pressure, 0, unroll=n <= 8)

    def first(tile, _):
        span = at(tile)
        velu, velv, press = fld[VELU, span, :], fld[VELV, span, :], prs[span, :]
        push = HALF_DT * (down_up(fld.at[VELU], tile, velu, tiles + 1) + left_right(velv))
        grow = 1.0 + push
        scale = HALF_DT / fld[RHO, span, :]
        keep = 1.0 - (fld[GAM, span, :] - 1.0) * push
        nxt_prs[span, :] = press * keep / grow
        nxt_u[span, :] = velu - down_up(prs, tile, press, tiles + 1) * scale
        nxt_v[span, :] = velv - left_right(press) * scale
        coef[span, :] = scale * grow
        vols[0, span, :] = grow
        vols[1, span, :] = fld[ENE, span, :] * keep
        return 0

    lax.fori_loop(0, tiles + 2, first, 0, unroll=n <= 8)
    for place, inside in ((0, inside_top), (tiles + 1, inside_bottom)):
        span = at(place)
        nxt_prs[span, :] = jnp.where(inside, nxt_prs[span, :], 0.0)
        nxt_u[span, :] = jnp.where(inside, nxt_u[span, :], 0.0)

    def cyclic(x):
        return jnp.where(sub % BR == 0, turn(x, 8 - (BR - 1)), turn(x, 1))

    def second(device, index):
        tile = 1 + device * chips + index
        span = at(tile)
        push = HALF_DT * (down_up(nxt_u, tile, nxt_u[span, :]) + left_right(nxt_v[span, :]))
        volume = vols[0, span, :] * (1.0 + push)
        heat_e = vols[1, span, :] * (1.0 - (fld[GAM, span, :] - 1.0) * push)
        mass = fld[RHO, span, :]
        heat = mass * heat_e
        from_own = (core == 0) if device == 0 else (core == 1)
        swept = jnp.where(from_own, sweep[at(index), :], sweep_sib[at(index), :])
        frac = swept * volume / (1.0 + volume)
        mass_go, heat_go = frac * mass, frac * heat
        mass_part = mass - mass_go + cyclic(mass_go)
        heat_part = heat - heat_go + cyclic(heat_go)
        parts[device, 2 * index] = jnp.where(sub < 4, mass_part, turn(heat_part, 4))
        parts[device, 2 * index + 1] = jnp.where(sub < 4, turn(mass_part, 4), heat_part)

    for device in range(2):
        lax.fori_loop(0, chips, lambda index, _, device=device: (second(device, index), 0)[1], 0, unroll=n <= 8)

    pieces = width // 128
    for index, (send, path) in enumerate(zip(sends, paths)):
        base = reached(path, core) * (2 * CAP)
        for device in range(2):
            for turn_of in range(CAP):
                rank = device * CAP + turn_of
                found = [jnp.zeros((8, 128), jnp.float32)] * pieces
                for block in range(n):
                    hit = jnp.broadcast_to(code[device, block : block + 1, :], (8, 128)) == base + rank
                    found = [
                        jnp.where(hit, parts[device, block, :, piece * 128 : piece * 128 + 128], found[piece])
                        for piece in range(pieces)
                    ]
                for piece in range(pieces):
                    send[rank * pieces + piece] = found[piece]
        send[2 * CAP * pieces] = tags[index]


def velocity_kernel(n, prs, velu, velv, coef, vel):
    chips = n // 2
    _, me = where_am_i()

    def one(index, _):
        tile = 1 + me % 2 * chips + index
        span, dest = at(tile), at(index)
        press, scale = prs[span, :], coef[span, :]
        vel[0, dest, :] = velu[span, :] - down_up(prs, tile, press) * scale
        vel[1, dest, :] = velv[span, :] - left_right(press) * scale
        return 0

    lax.fori_loop(0, chips, one, 0, unroll=n <= 8)


def land_kernel(n, *refs):
    chips = n // 2
    arrived = refs[:chips]
    mass_out, energy_out, mass, energy, sems = refs[chips:]
    parts = mass.shape[1] // 128
    sub = sublane(128)

    def send(source, target, which, index):
        span = pl.ds(pl.multiple_of(index * 8, 8), 8)
        return pltpu.make_async_copy(source.at[span, :], target.at[span, :], sems.at[which, index])

    def tile_pair(index, _):
        span = pl.ds(pl.multiple_of(index * 8, 8), 8)
        sums = [[jnp.zeros((8, 128), jnp.float32) for _ in range(parts)] for _ in range(2)]
        for buf in arrived:
            tag_tile = buf[2 * CAP * parts]
            for rank in range(2 * CAP):
                tag = jnp.broadcast_to(tag_tile[rank : rank + 1, :], (8, 128))
                for bit in range(2):
                    hit = tag == (2 * index + bit) * 1.0
                    for part in range(parts):
                        sums[bit][part] += jnp.where(hit, buf[rank * parts + part], 0.0)
        for part in range(parts):
            cols = slice(part * 128, part * 128 + 128)
            even, odd = sums[0][part], sums[1][part]
            mass[span, cols] = jnp.where(sub < 4, even, turn(odd, 4))
            energy[span, cols] = jnp.where(sub < 4, turn(even, 4), odd)
        send(mass, mass_out, 0, index).start()
        send(energy, energy_out, 1, index).start()
        return 0

    lax.fori_loop(0, chips, tile_pair, 0, unroll=n <= 8)
    for index in range(chips):
        send(mass, mass_out, 0, index).wait()
        send(energy, energy_out, 1, index).wait()


def across_links(groups, n):
    pairs = []
    for grp in range(groups):
        base = grp * n
        pairs += [(base + i, base + i + 1) for i in range(2, n - 2, 2)]
        if grp + 1 < groups:
            turn_at = n - 2 if grp % 2 == 0 else 1
            pairs += [(base + n - 1, base + n), (base + turn_at, base + n + turn_at)]
    used = {i for pair in pairs for i in pair}
    left = [i for i in range(groups * n) if i not in used]
    pairs += [(left[i], left[i + 1]) for i in range(0, len(left), 2)]
    return [link for low, high in pairs for link in ((low, high), (high, low))]


def shards(state, order, sweep, owner, slot_target):
    n = lax.axis_size("bis")
    groups = lax.axis_size("grp")
    chips = n // 2
    rows, width = sweep.shape
    parts = width // 128
    f32 = jnp.float32
    params = pltpu.CompilerParams(vmem_limit_bytes=48 * 1024 * 1024)

    def to_sibling(x):
        return lax.ppermute(x, "bis", [(i, i ^ 1) for i in range(n)])

    def to_chip(x, path):
        return lax.ppermute(x, "bis", [(i, i ^ 2 * path[i % 2]) for i in range(n)]) if path[0] else x

    paths = routes(chips)

    owner = owner.reshape(n)
    extra = -(-(rows + n) // 8) * 8
    packed = pl.pallas_call(
        functools.partial(pack_kernel, n),
        out_shape=[
            jax.ShapeDtypeStruct((8 * (NF + 1) + (0 if mask else extra), width), f32) for mask in range(chips)
        ]
        + [jax.ShapeDtypeStruct((ZR, width), f32)],
        in_specs=[pl.BlockSpec(memory_space=pl.ANY)] * 5,
        out_specs=[VMEM] * (chips + 1),
        scratch_shapes=[
            pltpu.SMEM((n,), jnp.int32),
            pltpu.SMEM((n,), jnp.int32),
            pltpu.SMEM((n,), jnp.int32),
            pltpu.VMEM((NF, rows, width), f32),
            pltpu.SemaphoreType.DMA((NF + 4,)),
        ],
        compiler_params=params,
        name="pack",
    )(*[pltpu.with_memory_space_constraint(x, pltpu.HBM) for x in (order.reshape(n), owner, slot_target, sweep, state)])
    across = lax.ppermute(packed[chips], ("grp", "bis"), across_links(groups, n))
    mine = [to_chip(x, path) for x, path in zip(packed, paths)]
    theirs = [to_sibling(x) for x in mine]
    across_sib = to_sibling(jnp.concatenate([across] + [x[0:8] for x in mine[1:]]))

    code, tags = pl.pallas_call(
        functools.partial(tag_kernel, n, rows),
        out_shape=[
            jax.ShapeDtypeStruct((2, n, 128), jnp.int32),
            jax.ShapeDtypeStruct((chips, 8, 128), f32),
        ],
        in_specs=[VMEM] * 2,
        out_specs=[VMEM] * 2,
        compiler_params=params,
        name="tags",
    )(mine[0], theirs[0])

    stack = (2 * chips + 2) * 8
    send_shape = (2 * CAP * parts + 1, 8, 128)
    out = pl.pallas_call(
        functools.partial(step_kernel, n),
        out_shape=[jax.ShapeDtypeStruct((stack, width), f32)] * 4
        + [jax.ShapeDtypeStruct(send_shape, f32)] * chips,
        in_specs=[VMEM] * (2 * chips + 5),
        out_specs=[VMEM] * (chips + 4),
        scratch_shapes=[
            pltpu.VMEM((NF, stack, width), f32),
            pltpu.VMEM((stack, width), f32),
            pltpu.VMEM((2, stack, width), f32),
            pltpu.VMEM((2, chips, 8, width), f32),
            pltpu.VMEM((2, n, 8, width), f32),
        ],
        compiler_params=params,
        name="substeps",
    )(code, tags, *mine, *theirs, across, across_sib, sweep)
    arrived = [to_chip(x, path) for x, path in zip(out[4:], paths)]
    vel = pl.pallas_call(
        functools.partial(velocity_kernel, n),
        out_shape=jax.ShapeDtypeStruct((2, rows, width), f32),
        in_specs=[VMEM] * 4,
        out_specs=VMEM,
        compiler_params=params,
        name="velocities",
    )(*out[:4])
    mass, energy = pl.pallas_call(
        functools.partial(land_kernel, n),
        out_shape=[jax.ShapeDtypeStruct((rows, width), f32)] * 2,
        in_specs=[VMEM] * chips,
        out_specs=[pl.BlockSpec(memory_space=pl.ANY)] * 2,
        scratch_shapes=[
            pltpu.VMEM((rows, width), f32),
            pltpu.VMEM((rows, width), f32),
            pltpu.SemaphoreType.DMA((2, chips)),
        ],
        compiler_params=params,
        name="land",
    )(*arrived)
    return mass, energy, vel


def solution(mesh):
    placed = (
        P(None, ("grp", "bis"), None),
        P(("grp", "bis"), None),
        P(("grp", "bis"), None),
        P(("grp", "bis"), None),
        P(("grp", "bis")),
    )
    return jax.shard_map(
        shards,
        mesh=mesh,
        in_specs=placed,
        out_specs=(P(("grp", "bis"), None), P(("grp", "bis"), None), P(None, ("grp", "bis"), None)),
        check_vma=False,
    )
```

```python
import functools

import jax
import jax.numpy as jnp
from jax import lax
from jax.experimental import pallas as pl
from jax.experimental.pallas import tpu as pltpu
from jax.sharding import PartitionSpec as P

BR = 4
CAP = 2
SWAP1, CROSS1 = 1, 0
SWAP2, CROSS2 = 0, 1
ZR = 8
HALF_DT = 0.075
NF = 5
RHO, ENE, VELU, VELV, GAM = range(NF)
FAR_P, FAR_U = 5, 6
SMEM = pl.BlockSpec(memory_space=pltpu.SMEM)
VMEM = pl.BlockSpec(memory_space=pltpu.VMEM)


def sublane(width):
    return lax.broadcasted_iota(jnp.int32, (8, width), 0)


def turn(tile, shift):
    return pltpu.roll(tile, shift, 0)


def left_right(x):
    width = x.shape[1]
    lane = lax.broadcasted_iota(jnp.int32, x.shape, 1)
    left = jnp.where(lane == 0, 0.0, pltpu.roll(x, 1, 1))
    right = jnp.where(lane == width - 1, 0.0, pltpu.roll(x, width - 1, 1))
    return right - left


def at(tile):
    return pl.ds(pl.multiple_of(tile * 8, 8), 8)


def down_up(ref, tile, x, clip=None):
    sub = sublane(x.shape[1])
    before = ref[at(tile - 1 if clip is None else jnp.maximum(tile - 1, 0)), :]
    after = ref[at(tile + 1 if clip is None else jnp.minimum(tile + 1, clip)), :]
    return turn(jnp.where(sub == 0, after, x), 7) - turn(jnp.where(sub == 7, before, x), 1)


def target(path, core):
    return 2 * reached(path, core) + (1 if CROSS2 and path[0] else 0)


def where_am_i():
    return lax.axis_index("grp"), lax.axis_index("bis")


def routes(chips, swapped):
    bits = chips.bit_length() - 1
    half = bits // 2 if swapped and bits % 2 == 0 else 0
    swap = lambda mask: (mask << half | mask >> bits - half) & chips - 1
    masks = sorted(range(1, chips), key=lambda mask: (-mask.bit_count(), mask))
    return [(0, 0)] + [(mask, swap(mask)) for mask in masks]


def reached(route, core):
    return route[0] if route[0] == route[1] else jnp.where(core == 0, route[0], route[1])


def pack_kernel(n, *refs):
    chips = n // 2
    order_in, owner_in, slot_in, sweep_in, state_in = refs[:5]
    chip_bufs, across = refs[5 : 5 + chips], refs[5 + chips]
    order, owner, slot, state, sems = refs[6 + chips :]
    width = state.shape[2]
    rows = state.shape[1]
    home = 8 * (NF + 1)
    copies = [pltpu.make_async_copy(order_in, order, sems.at[0])]
    copies += [pltpu.make_async_copy(state_in.at[field], state.at[field], sems.at[1 + field]) for field in range(NF)]
    copies += [
        pltpu.make_async_copy(owner_in, owner, sems.at[1 + NF]),
        pltpu.make_async_copy(slot_in, slot, sems.at[2 + NF]),
        pltpu.make_async_copy(sweep_in, chip_bufs[0].at[home : home + rows, :], sems.at[3 + NF]),
    ]
    for copy in copies:
        copy.start()
    _, me = where_am_i()
    chip, core = me // 2, me % 2
    sub = sublane(width)
    first = me == 0
    goals = [chip ^ reached(route, core) for route in routes(chips, SWAP1)]
    copies[0].wait()

    def tile_of(field, block):
        return state[field, pl.ds(pl.multiple_of(block // 2 * 8, 8), 8), :]

    def halo(buf, base, index):
        block = order[index]
        near = block * 4 + jnp.where(first, 0, BR - 1)
        far = block * 4 + jnp.where(first, 1, BR - 2)
        for field in range(NF):
            buf[base + field : base + field + 1, :] = state[field, pl.ds(near, 1), :]
        line = lambda field: state[field, pl.ds(far, 1), :]
        buf[base + FAR_P : base + FAR_P + 1, :] = (line(GAM) - 1.0) * line(RHO) * line(ENE)
        buf[base + FAR_U : base + FAR_U + 1, :] = line(VELU)

    for field in range(NF):
        copies[1 + field].wait()
        for buf, goal in zip(chip_bufs, goals):
            low = order[2 * goal]
            high = order[2 * goal + 1]
            for line in range(BR):
                buf[8 * field + line : 8 * field + line + 1, :] = state[field, pl.ds(low * BR + line, 1), :]
                buf[8 * field + BR + line : 8 * field + BR + line + 1, :] = state[field, pl.ds(high * BR + line, 1), :]
    for buf, goal in zip(chip_bufs, goals):
        beyond = jnp.where(first, jnp.minimum(2 * goal + 2, n - 1), jnp.maximum(2 * goal - 1, 0))
        halo(buf, 8 * NF, beyond)
    halo(across, 0, jnp.where(first, 0, n - 1))
    for copy in copies[1 + NF :]:
        copy.wait()
    lane = lax.broadcasted_iota(jnp.int32, (1, width), 1)
    for block in range(n):
        line = jnp.where(lane < width // 2, owner[block], slot[block])
        chip_bufs[0][home + rows + block : home + rows + block + 1, :] = line.astype(jnp.float32)


def tag_kernel(n, rows, own_home, sib_home, code, tags):
    chips = n // 2
    width = own_home.shape[1]
    _, me = where_am_i()
    chip, core = me // 2, me % 2
    span = pl.ds(8 * (NF + 1) + rows, n)
    own, sib = own_home[span, :].astype(jnp.int32), sib_home[span, :].astype(jnp.int32)
    both = (jnp.where(core == 0, own, sib), jnp.where(core == 0, sib, own))
    line_id = lax.broadcasted_iota(jnp.int32, (n, 128), 0)
    sub = sublane(128)
    slots = []
    for device, info in enumerate(both):
        owner = info[:, 0:128]
        rank = jnp.zeros((n, 128), jnp.int32)
        for block in range(n):
            same = jnp.logical_and(owner == owner[block : block + 1, :], line_id > block)
            rank = jnp.where(same, rank + 1, rank)
        slots.append((owner ^ me) * (2 * CAP) + (device * CAP) + rank)
        code[device] = slots[device]
    for index, path in enumerate(routes(chips, SWAP2)):
        want = sub + target(path, core) * (2 * CAP)
        tile = jnp.full((8, 128), -1, jnp.int32)
        for device, info in enumerate(both):
            for block in range(n):
                hit = jnp.logical_and(want == slots[device][block : block + 1, :], sub < 2 * CAP)
                tile = jnp.where(hit, info[block : block + 1, width - 128 :], tile)
        tags[index] = tile.astype(jnp.float32)


def pack_partials(n, paths, core, code, tags, parts, sends):
    width = parts.shape[3]
    pieces = width // 128
    lanes = [slice(piece * 128, piece * 128 + 128) for piece in range(pieces)]
    for device in range(2):
        wants = [target(path, core) * (2 * CAP) + device * CAP + again for path in paths for again in range(CAP)]
        found = [[jnp.zeros((8, 128), jnp.float32)] * pieces for _ in wants]
        for block in range(n):
            taken = jnp.broadcast_to(code[device, block : block + 1, :], (8, 128))
            tile = [parts[device, block, :, lane] for lane in lanes]
            for index, want in enumerate(wants):
                hit = taken == want
                found[index] = [jnp.where(hit, new, old) for new, old in zip(tile, found[index])]
        for index in range(len(wants)):
            rank = device * CAP + index % CAP
            for piece in range(pieces):
                sends[index // CAP][rank * pieces + piece] = found[index][piece]
    for send, tag in zip(sends, tags):
        send[2 * CAP * pieces] = tag[...]


def step_kernel(n, *refs):
    chips = n // 2
    refs = list(refs)
    take = lambda count: [refs.pop(0) for _ in range(count)]
    code, tags = take(2)
    mine, theirs = take(chips), take(chips)
    across, across_sib, sweep = take(3)
    nxt_prs, nxt_u, nxt_v, coef = take(4)
    (parts,) = take(1)
    sends = take(chips - 1)
    fld, prs, vols, halo = take(4)
    grp, me = where_am_i()
    chip, core = me // 2, me % 2
    width = sweep.shape[1]
    rows = sweep.shape[0]
    home = 8 * (NF + 1)
    sweep_sib = theirs[0].at[home : home + rows, :]
    tiles = 2 * chips
    sub = sublane(width)
    is_low = core == 0

    def pair(own, sib):
        return jnp.where(is_low, own, sib), jnp.where(is_low, sib, own)

    for index, path in enumerate(routes(chips, SWAP1)):
        source = chip ^ reached(path, core)
        own, sib = mine[index], theirs[routes(chips, SWAP1).index((path[1], path[0]))]
        if CROSS1 and path[0]:
            own, sib = sib, own
        for field in range(NF):
            span = pl.ds(8 * field, 8)
            even, odd = pair(own[span, :], sib[span, :])
            fld[field, at(1 + source), :] = jnp.where(sub < 4, even, turn(odd, 4))
            fld[field, at(1 + chips + source), :] = jnp.where(sub < 4, turn(even, 4), odd)
        even, odd = pair(own[8 * NF : home, :], sib[8 * NF : home, :])
        halo[0, source] = even
        halo[1, source] = odd
    even, odd = pair(across[0:8, :], across_sib[0:8, :])
    inside_top = jnp.logical_or(grp > 0, chip > 0)
    inside_bottom = jnp.logical_or(grp < lax.axis_size("grp") - 1, chip < chips - 1)
    top = jnp.where(inside_top, jnp.where(chip == 0, even, halo[1, chips - 1]), 0.0)
    bottom = jnp.where(inside_bottom, jnp.where(chip == chips - 1, odd, halo[0, 0]), 0.0)

    def line(tile, index):
        return jnp.broadcast_to(tile[index : index + 1, :], (8, width))

    for tile, place, near in ((top, 0, 7), (bottom, tiles + 1, 0)):
        span = at(place)
        for field in (RHO, ENE, VELV, GAM):
            fld[field, span, :] = line(tile, field)
        fld[VELU, span, :] = jnp.where(sub == near, line(tile, VELU), line(tile, FAR_U))
        press = (line(tile, GAM) - 1.0) * line(tile, RHO) * line(tile, ENE)
        prs[span, :] = jnp.where(sub == near, press, line(tile, FAR_P))

    def pressure(tile, _):
        span = at(tile)
        prs[span, :] = (fld[GAM, span, :] - 1.0) * fld[RHO, span, :] * fld[ENE, span, :]
        return 0

    lax.fori_loop(1, tiles + 1, pressure, 0, unroll=n <= 8)

    def first(tile, _):
        span = at(tile)
        velu, velv, press = fld[VELU, span, :], fld[VELV, span, :], prs[span, :]
        push = HALF_DT * (down_up(fld.at[VELU], tile, velu, tiles + 1) + left_right(velv))
        grow = 1.0 + push
        scale = HALF_DT / fld[RHO, span, :]
        keep = 1.0 - (fld[GAM, span, :] - 1.0) * push
        nxt_prs[span, :] = press * keep / grow
        nxt_u[span, :] = velu - down_up(prs, tile, press, tiles + 1) * scale
        nxt_v[span, :] = velv - left_right(press) * scale
        coef[span, :] = scale * grow
        vols[0, span, :] = grow
        vols[1, span, :] = fld[ENE, span, :] * keep
        return 0

    lax.fori_loop(0, tiles + 2, first, 0, unroll=n <= 8)
    for place, inside in ((0, inside_top), (tiles + 1, inside_bottom)):
        span = at(place)
        nxt_prs[span, :] = jnp.where(inside, nxt_prs[span, :], 0.0)
        nxt_u[span, :] = jnp.where(inside, nxt_u[span, :], 0.0)

    def cyclic(x):
        return jnp.where(sub % BR == 0, turn(x, 8 - (BR - 1)), turn(x, 1))

    def second(device, index):
        tile = 1 + device * chips + index
        span = at(tile)
        push = HALF_DT * (down_up(nxt_u, tile, nxt_u[span, :]) + left_right(nxt_v[span, :]))
        volume = vols[0, span, :] * (1.0 + push)
        heat_e = vols[1, span, :] * (1.0 - (fld[GAM, span, :] - 1.0) * push)
        mass = fld[RHO, span, :]
        heat = mass * heat_e
        from_own = (core == 0) if device == 0 else (core == 1)
        swept = jnp.where(from_own, sweep[at(index), :], sweep_sib[at(index), :])
        frac = swept * volume / (1.0 + volume)
        mass_go, heat_go = frac * mass, frac * heat
        mass_part = mass - mass_go + cyclic(mass_go)
        heat_part = heat - heat_go + cyclic(heat_go)
        parts[device, 2 * index] = jnp.where(sub < 4, mass_part, turn(heat_part, 4))
        parts[device, 2 * index + 1] = jnp.where(sub < 4, turn(mass_part, 4), heat_part)

    for device in range(2):
        lax.fori_loop(0, chips, lambda index, _, device=device: (second(device, index), 0)[1], 0, unroll=n <= 8)

    pack_partials(n, routes(chips, SWAP2)[1:], core, code, [tags.at[1 + i] for i in range(chips - 1)], parts, sends)


def side_kernel(n, prs, velu, velv, coef, parts, code, tags, vel, home):
    chips = n // 2
    _, me = where_am_i()
    pack_partials(n, routes(chips, SWAP2)[:1], me % 2, code, [tags.at[0]], parts, [home])

    def one(index, _):
        tile = 1 + me % 2 * chips + index
        span, dest = at(tile), at(index)
        press, scale = prs[span, :], coef[span, :]
        vel[0, dest, :] = velu[span, :] - down_up(prs, tile, press) * scale
        vel[1, dest, :] = velv[span, :] - left_right(press) * scale
        return 0

    lax.fori_loop(0, chips, one, 0, unroll=n <= 8)


def land_kernel(n, final, *refs):
    chips = n // 2
    refs = list(refs)
    if final:
        mass_out, energy_out, sums_out, sems = refs[-4:]
        sums_in, arrived = refs[0], refs[1:-4]
    else:
        sums_in, arrived, sums_out = None, refs[:-1], refs[-1]
    parts = sums_out.shape[2] // 128
    sub = sublane(128)

    def send(which, index):
        span = pl.ds(pl.multiple_of(index * 8, 8), 8)
        target_ref = energy_out if which else mass_out
        return pltpu.make_async_copy(sums_out.at[which, span, :], target_ref.at[span, :], sems.at[which, index])

    def tile_pair(index, _):
        span = pl.ds(pl.multiple_of(index * 8, 8), 8)
        sums = [[jnp.zeros((8, 128), jnp.float32) for _ in range(parts)] for _ in range(2)]
        for buf in arrived:
            tag_tile = buf[2 * CAP * parts]
            for rank in range(2 * CAP):
                tag = jnp.broadcast_to(tag_tile[rank : rank + 1, :], (8, 128))
                for bit in range(2):
                    hit = tag == (2 * index + bit) * 1.0
                    for part in range(parts):
                        sums[bit][part] += jnp.where(hit, buf[rank * parts + part], 0.0)
        for part in range(parts):
            cols = slice(part * 128, part * 128 + 128)
            even, odd = sums[0][part], sums[1][part]
            mass, energy = jnp.where(sub < 4, even, turn(odd, 4)), jnp.where(sub < 4, turn(even, 4), odd)
            if final:
                mass, energy = mass + sums_in[0, span, cols], energy + sums_in[1, span, cols]
            sums_out[0, span, cols] = mass
            sums_out[1, span, cols] = energy
        if final:
            send(0, index).start()
            send(1, index).start()
        return 0

    lax.fori_loop(0, chips, tile_pair, 0, unroll=n <= 8)
    if final:
        for index in range(chips):
            send(0, index).wait()
            send(1, index).wait()


def across_links(groups, n):
    pairs = []
    for grp in range(groups):
        base = grp * n
        pairs += [(base + i, base + i + 1) for i in range(2, n - 2, 2)]
        if grp + 1 < groups:
            turn_at = n - 2 if grp % 2 == 0 else 1
            pairs += [(base + n - 1, base + n), (base + turn_at, base + n + turn_at)]
    used = {i for pair in pairs for i in pair}
    left = [i for i in range(groups * n) if i not in used]
    pairs += [(left[i], left[i + 1]) for i in range(0, len(left), 2)]
    return [link for low, high in pairs for link in ((low, high), (high, low))]


def shards(state, order, sweep, owner, slot_target):
    n = lax.axis_size("bis")
    groups = lax.axis_size("grp")
    chips = n // 2
    rows, width = sweep.shape
    parts = width // 128
    f32 = jnp.float32
    params = pltpu.CompilerParams(vmem_limit_bytes=48 * 1024 * 1024)

    def to_sibling(x):
        return lax.ppermute(x, "bis", [(i, i ^ 1) for i in range(n)])

    def to_chip(x, path, cross):
        links = [(i, i ^ 2 * path[i % 2] ^ cross) for i in range(n)]
        return lax.ppermute(x, "bis", links) if path[0] else x

    paths = routes(chips, SWAP1)

    owner = owner.reshape(n)
    extra = -(-(rows + n) // 8) * 8
    packed = pl.pallas_call(
        functools.partial(pack_kernel, n),
        out_shape=[
            jax.ShapeDtypeStruct((8 * (NF + 1) + (0 if mask else extra), width), f32) for mask in range(chips)
        ]
        + [jax.ShapeDtypeStruct((ZR, width), f32)],
        in_specs=[pl.BlockSpec(memory_space=pl.ANY)] * 5,
        out_specs=[VMEM] * (chips + 1),
        scratch_shapes=[
            pltpu.SMEM((n,), jnp.int32),
            pltpu.SMEM((n,), jnp.int32),
            pltpu.SMEM((n,), jnp.int32),
            pltpu.VMEM((NF, rows, width), f32),
            pltpu.SemaphoreType.DMA((NF + 4,)),
        ],
        compiler_params=params,
        name="pack",
    )(*[pltpu.with_memory_space_constraint(x, pltpu.HBM) for x in (order.reshape(n), owner, slot_target, sweep, state)])
    across = lax.ppermute(packed[chips], ("grp", "bis"), across_links(groups, n))
    mine = [to_chip(x, path, CROSS1) for x, path in zip(packed, paths)]
    theirs = [to_sibling(x) for x in mine]
    across_sib = to_sibling(jnp.concatenate([across] + [x[0:8] for x in mine[1:]]))

    code, tags = pl.pallas_call(
        functools.partial(tag_kernel, n, rows),
        out_shape=[
            jax.ShapeDtypeStruct((2, n, 128), jnp.int32),
            jax.ShapeDtypeStruct((chips, 8, 128), f32),
        ],
        in_specs=[VMEM] * 2,
        out_specs=[VMEM] * 2,
        compiler_params=params,
        name="tags",
    )(mine[0], theirs[0])

    stack = (2 * chips + 2) * 8
    send_shape = (2 * CAP * parts + 1, 8, 128)
    out = pl.pallas_call(
        functools.partial(step_kernel, n),
        out_shape=[jax.ShapeDtypeStruct((stack, width), f32)] * 4
        + [jax.ShapeDtypeStruct((2, n, 8, width), f32)]
        + [jax.ShapeDtypeStruct(send_shape, f32)] * (chips - 1),
        in_specs=[VMEM] * (2 * chips + 5),
        out_specs=[VMEM] * (chips + 4),
        scratch_shapes=[
            pltpu.VMEM((NF, stack, width), f32),
            pltpu.VMEM((stack, width), f32),
            pltpu.VMEM((2, stack, width), f32),
            pltpu.VMEM((2, chips, 8, width), f32),
        ],
        compiler_params=params,
        name="substeps",
    )(code, tags, *mine, *theirs, across, across_sib, sweep)
    arrived = [to_chip(x, path, CROSS2) for x, path in zip(out[5:], routes(chips, SWAP2)[1:])]
    vel, home = pl.pallas_call(
        functools.partial(side_kernel, n),
        out_shape=[jax.ShapeDtypeStruct((2, rows, width), f32), jax.ShapeDtypeStruct(send_shape, f32)],
        in_specs=[VMEM] * 7,
        out_specs=[VMEM] * 2,
        compiler_params=params,
        name="velocities",
    )(*out[:5], code, tags)
    arrived = [home] + arrived
    early = 2
    sums = pl.pallas_call(
        functools.partial(land_kernel, n, False),
        out_shape=jax.ShapeDtypeStruct((2, rows, width), f32),
        in_specs=[VMEM] * early,
        out_specs=VMEM,
        compiler_params=params,
        name="sums",
    )(*arrived[:early])
    mass, energy = pl.pallas_call(
        functools.partial(land_kernel, n, True),
        out_shape=[jax.ShapeDtypeStruct((rows, width), f32)] * 2,
        in_specs=[VMEM] * (1 + chips - early),
        out_specs=[pl.BlockSpec(memory_space=pl.ANY)] * 2,
        scratch_shapes=[pltpu.VMEM((2, rows, width), f32), pltpu.SemaphoreType.DMA((2, chips))],
        compiler_params=params,
        name="land",
    )(sums, *arrived[early:])
    return mass, energy, vel


def solution(mesh):
    placed = (
        P(None, ("grp", "bis"), None),
        P(("grp", "bis"), None),
        P(("grp", "bis"), None),
        P(("grp", "bis"), None),
        P(("grp", "bis")),
    )
    return jax.shard_map(
        shards,
        mesh=mesh,
        in_specs=placed,
        out_specs=(P(("grp", "bis"), None), P(("grp", "bis"), None), P(None, ("grp", "bis"), None)),
        check_vma=False,
    )
```

```python
import functools

import jax
import jax.numpy as jnp
from jax import lax
from jax.experimental import pallas as pl
from jax.experimental.pallas import tpu as pltpu
from jax.sharding import PartitionSpec as P

BR = 4
CAP = 2
ZR = 8
HALF_DT = 0.075
NF = 5
RHO, ENE, VELU, VELV, GAM = range(NF)
FAR_P, FAR_U, INFO = 5, 6, 7
SMEM = pl.BlockSpec(memory_space=pltpu.SMEM)
VMEM = pl.BlockSpec(memory_space=pltpu.VMEM)


def sublane(width):
    return lax.broadcasted_iota(jnp.int32, (8, width), 0)


def turn(tile, shift):
    return pltpu.roll(tile, shift, 0)


def left_right(x):
    width = x.shape[1]
    lane = lax.broadcasted_iota(jnp.int32, x.shape, 1)
    left = jnp.where(lane == 0, 0.0, pltpu.roll(x, 1, 1))
    right = jnp.where(lane == width - 1, 0.0, pltpu.roll(x, width - 1, 1))
    return right - left


def at(tile):
    return pl.ds(pl.multiple_of(tile * 8, 8), 8)


def down_up(ref, tile, x, clip=None):
    sub = sublane(x.shape[1])
    before = ref[at(tile - 1 if clip is None else jnp.maximum(tile - 1, 0)), :]
    after = ref[at(tile + 1 if clip is None else jnp.minimum(tile + 1, clip)), :]
    return turn(jnp.where(sub == 0, after, x), 7) - turn(jnp.where(sub == 7, before, x), 1)


def target(path, core):
    return 2 * reached(path, core) + (1 if path[0] else 0)


def where_am_i():
    return lax.axis_index("grp"), lax.axis_index("bis")


def routes(chips, swapped):
    bits = chips.bit_length() - 1
    half = bits // 2 if swapped and bits % 2 == 0 else 0
    swap = lambda mask: (mask << half | mask >> bits - half) & chips - 1
    masks = sorted(range(1, chips), key=lambda mask: (-mask.bit_count(), mask))
    return [(0, 0)] + [(mask, swap(mask)) for mask in masks]


def reached(route, core):
    return route[0] if route[0] == route[1] else jnp.where(core == 0, route[0], route[1])


def pack_kernel(n, *refs):
    chips = n // 2
    order_in, owner_in, slot_in, sweep_in, state_in = refs[:5]
    chip_bufs, across = refs[5 : 5 + chips], refs[5 + chips]
    order, owner, slot, state, sems = refs[6 + chips :]
    width = state.shape[2]
    rows = state.shape[1]
    home = 8 * (NF + 1)
    copies = [pltpu.make_async_copy(order_in, order, sems.at[0])]
    copies += [pltpu.make_async_copy(state_in.at[field], state.at[field], sems.at[1 + field]) for field in range(NF)]
    copies += [
        pltpu.make_async_copy(owner_in, owner, sems.at[1 + NF]),
        pltpu.make_async_copy(slot_in, slot, sems.at[2 + NF]),
        pltpu.make_async_copy(sweep_in, chip_bufs[0].at[home : home + rows, :], sems.at[3 + NF]),
    ]
    for copy in copies:
        copy.start()
    _, me = where_am_i()
    chip, core = me // 2, me % 2
    sub = sublane(width)
    first = me == 0
    goals = [chip ^ reached(route, core) for route in routes(chips, True)]
    copies[0].wait()

    def tile_of(field, block):
        return state[field, pl.ds(pl.multiple_of(block // 2 * 8, 8), 8), :]

    def halo(buf, base, index):
        block = order[index]
        near = block * 4 + jnp.where(first, 0, BR - 1)
        far = block * 4 + jnp.where(first, 1, BR - 2)
        for field in range(NF):
            buf[base + field : base + field + 1, :] = state[field, pl.ds(near, 1), :]
        line = lambda field: state[field, pl.ds(far, 1), :]
        buf[base + FAR_P : base + FAR_P + 1, :] = (line(GAM) - 1.0) * line(RHO) * line(ENE)
        buf[base + FAR_U : base + FAR_U + 1, :] = line(VELU)

    for field in range(NF):
        copies[1 + field].wait()
        for buf, goal in zip(chip_bufs, goals):
            low = order[2 * goal]
            high = order[2 * goal + 1]
            for line in range(BR):
                buf[8 * field + line : 8 * field + line + 1, :] = state[field, pl.ds(low * BR + line, 1), :]
                buf[8 * field + BR + line : 8 * field + BR + line + 1, :] = state[field, pl.ds(high * BR + line, 1), :]
    for buf, goal in zip(chip_bufs, goals):
        beyond = jnp.where(first, jnp.minimum(2 * goal + 2, n - 1), jnp.maximum(2 * goal - 1, 0))
        halo(buf, 8 * NF, beyond)
    halo(across, 0, jnp.where(first, 0, n - 1))
    for copy in copies[1 + NF :]:
        copy.wait()
    lane = lax.broadcasted_iota(jnp.int32, (1, width), 1)
    info = jnp.zeros((1, width), jnp.int32)
    for index in range(2 * n):
        value = owner[index] if index < n else slot[index - n]
        info = jnp.where(lane // (width // (2 * n)) == index, value, info)
    for buf in chip_bufs:
        buf[8 * NF + INFO : 8 * NF + INFO + 1, :] = info.astype(jnp.float32)
    for block in range(n):
        line = jnp.where(lane < width // 2, owner[block], slot[block])
        chip_bufs[0][home + rows + block : home + rows + block + 1, :] = line.astype(jnp.float32)


def code_kernel(n, rows, own_home, sib_home, code):
    _, me = where_am_i()
    span = pl.ds(8 * (NF + 1) + rows, n)
    own, sib = own_home[span, 0:128].astype(jnp.int32), sib_home[span, 0:128].astype(jnp.int32)
    line_id = lax.broadcasted_iota(jnp.int32, (n, 128), 0)
    for device in range(2):
        owner = jnp.where(me % 2 == device, own, sib)
        rank = jnp.zeros((n, 128), jnp.int32)
        for block in range(n):
            same = jnp.logical_and(owner == owner[block : block + 1, :], line_id > block)
            rank = jnp.where(same, rank + 1, rank)
        code[device] = (owner ^ me) * (2 * CAP) + (device * CAP) + rank


def labels_of(n, me, infos):
    step = infos[0].shape[1] // (2 * n)
    sub = sublane(128)
    tile = jnp.full((8, 128), -1.0, jnp.float32)
    for device, info in enumerate(infos):
        value = lambda index: jnp.broadcast_to(info[:, index * step : index * step + 1], (8, 128))
        place = jnp.full((8, 128), device * CAP, jnp.int32)
        for block in range(n):
            hit = value(block) == me.astype(jnp.float32)
            tile = jnp.where(jnp.logical_and(hit, sub == place), value(n + block), tile)
            place = jnp.where(hit, place + 1, place)
    return tile


def pack_partials(n, paths, core, code, parts, sends):
    width = parts.shape[3]
    pieces = width // 128
    lanes = [slice(piece * 128, piece * 128 + 128) for piece in range(pieces)]
    for device in range(2):
        wants = [target(path, core) * (2 * CAP) + device * CAP + again for path in paths for again in range(CAP)]
        found = [[jnp.zeros((8, 128), jnp.float32)] * pieces for _ in wants]
        for block in range(n):
            taken = jnp.broadcast_to(code[device, block : block + 1, :], (8, 128))
            tile = [parts[device, block, :, lane] for lane in lanes]
            for index, want in enumerate(wants):
                hit = taken == want
                found[index] = [jnp.where(hit, new, old) for new, old in zip(tile, found[index])]
        for index in range(len(wants)):
            rank = device * CAP + index % CAP
            for piece in range(pieces):
                sends[index // CAP][rank * pieces + piece] = found[index][piece]


def step_kernel(n, *refs):
    chips = n // 2
    refs = list(refs)
    take = lambda count: [refs.pop(0) for _ in range(count)]
    (code,) = take(1)
    mine, theirs = take(chips), take(chips)
    across, across_sib, sweep = take(3)
    nxt_prs, nxt_u, nxt_v, coef = take(4)
    (parts,) = take(1)
    sends = take(chips - 1)
    fld, prs, vols, halo = take(4)
    grp, me = where_am_i()
    chip, core = me // 2, me % 2
    width = sweep.shape[1]
    rows = sweep.shape[0]
    home = 8 * (NF + 1)
    sweep_sib = theirs[0].at[home : home + rows, :]
    tiles = 2 * chips
    sub = sublane(width)
    is_low = core == 0

    def pair(own, sib):
        return jnp.where(is_low, own, sib), jnp.where(is_low, sib, own)

    for index, path in enumerate(routes(chips, True)):
        source = chip ^ reached(path, core)
        own, sib = mine[index], theirs[routes(chips, True).index((path[1], path[0]))]
        for field in range(NF):
            span = pl.ds(8 * field, 8)
            even, odd = pair(own[span, :], sib[span, :])
            fld[field, at(1 + source), :] = jnp.where(sub < 4, even, turn(odd, 4))
            fld[field, at(1 + chips + source), :] = jnp.where(sub < 4, turn(even, 4), odd)
        even, odd = pair(own[8 * NF : home, :], sib[8 * NF : home, :])
        halo[0, source] = even
        halo[1, source] = odd
    even, odd = pair(across[0:8, :], across_sib[0:8, :])
    inside_top = jnp.logical_or(grp > 0, chip > 0)
    inside_bottom = jnp.logical_or(grp < lax.axis_size("grp") - 1, chip < chips - 1)
    top = jnp.where(inside_top, jnp.where(chip == 0, even, halo[1, chips - 1]), 0.0)
    bottom = jnp.where(inside_bottom, jnp.where(chip == chips - 1, odd, halo[0, 0]), 0.0)

    def line(tile, index):
        return jnp.broadcast_to(tile[index : index + 1, :], (8, width))

    for tile, place, near in ((top, 0, 7), (bottom, tiles + 1, 0)):
        span = at(place)
        for field in (RHO, ENE, VELV, GAM):
            fld[field, span, :] = line(tile, field)
        fld[VELU, span, :] = jnp.where(sub == near, line(tile, VELU), line(tile, FAR_U))
        press = (line(tile, GAM) - 1.0) * line(tile, RHO) * line(tile, ENE)
        prs[span, :] = jnp.where(sub == near, press, line(tile, FAR_P))

    def pressure(tile, _):
        span = at(tile)
        prs[span, :] = (fld[GAM, span, :] - 1.0) * fld[RHO, span, :] * fld[ENE, span, :]
        return 0

    lax.fori_loop(1, tiles + 1, pressure, 0, unroll=n <= 8)

    def first(tile, _):
        span = at(tile)
        velu, velv, press = fld[VELU, span, :], fld[VELV, span, :], prs[span, :]
        push = HALF_DT * (down_up(fld.at[VELU], tile, velu, tiles + 1) + left_right(velv))
        grow = 1.0 + push
        scale = HALF_DT / fld[RHO, span, :]
        keep = 1.0 - (fld[GAM, span, :] - 1.0) * push
        nxt_prs[span, :] = press * keep / grow
        nxt_u[span, :] = velu - down_up(prs, tile, press, tiles + 1) * scale
        nxt_v[span, :] = velv - left_right(press) * scale
        coef[span, :] = scale * grow
        vols[0, span, :] = grow
        vols[1, span, :] = fld[ENE, span, :] * keep
        return 0

    lax.fori_loop(0, tiles + 2, first, 0, unroll=n <= 8)
    for place, inside in ((0, inside_top), (tiles + 1, inside_bottom)):
        span = at(place)
        nxt_prs[span, :] = jnp.where(inside, nxt_prs[span, :], 0.0)
        nxt_u[span, :] = jnp.where(inside, nxt_u[span, :], 0.0)

    def cyclic(x):
        return jnp.where(sub % BR == 0, turn(x, 8 - (BR - 1)), turn(x, 1))

    def second(device, index):
        tile = 1 + device * chips + index
        span = at(tile)
        push = HALF_DT * (down_up(nxt_u, tile, nxt_u[span, :]) + left_right(nxt_v[span, :]))
        volume = vols[0, span, :] * (1.0 + push)
        heat_e = vols[1, span, :] * (1.0 - (fld[GAM, span, :] - 1.0) * push)
        mass = fld[RHO, span, :]
        heat = mass * heat_e
        from_own = (core == 0) if device == 0 else (core == 1)
        swept = jnp.where(from_own, sweep[at(index), :], sweep_sib[at(index), :])
        frac = swept * volume / (1.0 + volume)
        mass_go, heat_go = frac * mass, frac * heat
        mass_part = mass - mass_go + cyclic(mass_go)
        heat_part = heat - heat_go + cyclic(heat_go)
        parts[device, 2 * index] = jnp.where(sub < 4, mass_part, turn(heat_part, 4))
        parts[device, 2 * index + 1] = jnp.where(sub < 4, turn(mass_part, 4), heat_part)

    for device in range(2):
        lax.fori_loop(0, chips, lambda index, _, device=device: (second(device, index), 0)[1], 0, unroll=n <= 8)

    pack_partials(n, routes(chips, False)[1:], core, code, parts, sends)


def side_kernel(n, *refs):
    chips = n // 2
    prs, velu, velv, coef, parts, code = refs[:6]
    mine, theirs = refs[6 : 6 + chips], refs[6 + chips : 6 + 2 * chips]
    vel, home, labels = refs[6 + 2 * chips :]
    _, me = where_am_i()
    core = me % 2
    pack_partials(n, routes(chips, False)[:1], core, code, parts, [home])
    paths = routes(chips, True)
    line = slice(8 * NF + INFO, 8 * NF + INFO + 1)
    for index, (mask, _) in enumerate(routes(chips, False)):
        low, high = [path[0] for path in paths].index(mask), [path[1] for path in paths].index(mask)
        even = jnp.where(core == 0, mine[low][line, :], theirs[low][line, :])
        odd = jnp.where(core == 0, theirs[high][line, :], mine[high][line, :])
        labels[index] = labels_of(n, me, (even, odd))

    def one(index, _):
        tile = 1 + core * chips + index
        span, dest = at(tile), at(index)
        press, scale = prs[span, :], coef[span, :]
        vel[0, dest, :] = velu[span, :] - down_up(prs, tile, press) * scale
        vel[1, dest, :] = velv[span, :] - left_right(press) * scale
        return 0

    lax.fori_loop(0, chips, one, 0, unroll=n <= 8)


def land_kernel(n, final, *refs):
    chips = n // 2
    refs = list(refs)
    labels = refs.pop(0)
    if final:
        mass_out, energy_out, sums_out, sems = refs[-4:]
        sums_in, arrived = refs[0], refs[1:-4]
    else:
        sums_in, arrived, sums_out = None, refs[:-1], refs[-1]
    skipped = chips - len(arrived) if final else 0
    parts = sums_out.shape[2] // 128
    sub = sublane(128)

    def send(which, index):
        span = pl.ds(pl.multiple_of(index * 8, 8), 8)
        target_ref = energy_out if which else mass_out
        return pltpu.make_async_copy(sums_out.at[which, span, :], target_ref.at[span, :], sems.at[which, index])

    def tile_pair(index, _):
        span = pl.ds(pl.multiple_of(index * 8, 8), 8)
        sums = [[jnp.zeros((8, 128), jnp.float32) for _ in range(parts)] for _ in range(2)]
        for number, buf in enumerate(arrived):
            for rank in range(2 * CAP):
                tag = jnp.broadcast_to(labels[skipped + number, rank : rank + 1, :], (8, 128))
                for bit in range(2):
                    hit = tag == (2 * index + bit) * 1.0
                    for part in range(parts):
                        sums[bit][part] += jnp.where(hit, buf[rank * parts + part], 0.0)
        for part in range(parts):
            cols = slice(part * 128, part * 128 + 128)
            even, odd = sums[0][part], sums[1][part]
            mass, energy = jnp.where(sub < 4, even, turn(odd, 4)), jnp.where(sub < 4, turn(even, 4), odd)
            if final:
                mass, energy = mass + sums_in[0, span, cols], energy + sums_in[1, span, cols]
            sums_out[0, span, cols] = mass
            sums_out[1, span, cols] = energy
        if final:
            send(0, index).start()
            send(1, index).start()
        return 0

    lax.fori_loop(0, chips, tile_pair, 0, unroll=n <= 8)
    if final:
        for index in range(chips):
            send(0, index).wait()
            send(1, index).wait()


def across_links(groups, n):
    pairs = []
    for grp in range(groups):
        base = grp * n
        pairs += [(base + i, base + i + 1) for i in range(2, n - 2, 2)]
        if grp + 1 < groups:
            turn_at = n - 2 if grp % 2 == 0 else 1
            pairs += [(base + n - 1, base + n), (base + turn_at, base + n + turn_at)]
    used = {i for pair in pairs for i in pair}
    left = [i for i in range(groups * n) if i not in used]
    pairs += [(left[i], left[i + 1]) for i in range(0, len(left), 2)]
    return [link for low, high in pairs for link in ((low, high), (high, low))]


def shards(state, order, sweep, owner, slot_target):
    n = lax.axis_size("bis")
    groups = lax.axis_size("grp")
    chips = n // 2
    rows, width = sweep.shape
    parts = width // 128
    f32 = jnp.float32
    params = pltpu.CompilerParams(vmem_limit_bytes=48 * 1024 * 1024)

    def to_sibling(x):
        return lax.ppermute(x, "bis", [(i, i ^ 1) for i in range(n)])

    def to_chip(x, path, cross):
        links = [(i, i ^ 2 * path[i % 2] ^ cross) for i in range(n)]
        return lax.ppermute(x, "bis", links) if path[0] else x

    paths = routes(chips, True)

    owner = owner.reshape(n)
    extra = -(-(rows + n) // 8) * 8
    packed = pl.pallas_call(
        functools.partial(pack_kernel, n),
        out_shape=[
            jax.ShapeDtypeStruct((8 * (NF + 1) + (0 if mask else extra), width), f32) for mask in range(chips)
        ]
        + [jax.ShapeDtypeStruct((ZR, width), f32)],
        in_specs=[pl.BlockSpec(memory_space=pl.ANY)] * 5,
        out_specs=[VMEM] * (chips + 1),
        scratch_shapes=[
            pltpu.SMEM((n,), jnp.int32),
            pltpu.SMEM((n,), jnp.int32),
            pltpu.SMEM((n,), jnp.int32),
            pltpu.VMEM((NF, rows, width), f32),
            pltpu.SemaphoreType.DMA((NF + 4,)),
        ],
        compiler_params=params,
        name="pack",
    )(*[pltpu.with_memory_space_constraint(x, pltpu.HBM) for x in (order.reshape(n), owner, slot_target, sweep, state)])
    across = lax.ppermute(packed[chips], ("grp", "bis"), across_links(groups, n))
    mine = [to_chip(x, path, 0) for x, path in zip(packed, paths)]
    theirs = [to_sibling(x) for x in mine]
    across_sib = to_sibling(jnp.concatenate([across] + [x[0:8] for x in mine[1:]]))

    code = pl.pallas_call(
        functools.partial(code_kernel, n, rows),
        out_shape=jax.ShapeDtypeStruct((2, n, 128), jnp.int32),
        in_specs=[VMEM] * 2,
        out_specs=VMEM,
        compiler_params=params,
        name="code",
    )(mine[0], theirs[0])

    stack = (2 * chips + 2) * 8
    send_shape = (2 * CAP * parts, 8, 128)
    out = pl.pallas_call(
        functools.partial(step_kernel, n),
        out_shape=[jax.ShapeDtypeStruct((stack, width), f32)] * 4
        + [jax.ShapeDtypeStruct((2, n, 8, width), f32)]
        + [jax.ShapeDtypeStruct(send_shape, f32)] * (chips - 1),
        in_specs=[VMEM] * (2 * chips + 4),
        out_specs=[VMEM] * (chips + 4),
        scratch_shapes=[
            pltpu.VMEM((NF, stack, width), f32),
            pltpu.VMEM((stack, width), f32),
            pltpu.VMEM((2, stack, width), f32),
            pltpu.VMEM((2, chips, 8, width), f32),
        ],
        compiler_params=params,
        name="substeps",
    )(code, *mine, *theirs, across, across_sib, sweep)
    arrived = [to_chip(x, path, 1) for x, path in zip(out[5:], routes(chips, False)[1:])]
    vel, home, labels = pl.pallas_call(
        functools.partial(side_kernel, n),
        out_shape=[
            jax.ShapeDtypeStruct((2, rows, width), f32),
            jax.ShapeDtypeStruct(send_shape, f32),
            jax.ShapeDtypeStruct((chips, 8, 128), f32),
        ],
        in_specs=[VMEM] * (6 + 2 * chips),
        out_specs=[VMEM] * 3,
        compiler_params=params,
        name="velocities",
    )(*out[:5], code, *mine, *theirs)
    arrived = [home] + arrived
    early = 2
    sums = pl.pallas_call(
        functools.partial(land_kernel, n, False),
        out_shape=jax.ShapeDtypeStruct((2, rows, width), f32),
        in_specs=[VMEM] * (1 + early),
        out_specs=VMEM,
        compiler_params=params,
        name="sums",
    )(labels, *arrived[:early])
    mass, energy = pl.pallas_call(
        functools.partial(land_kernel, n, True),
        out_shape=[jax.ShapeDtypeStruct((rows, width), f32)] * 2,
        in_specs=[VMEM] * (2 + chips - early),
        out_specs=[pl.BlockSpec(memory_space=pl.ANY)] * 2,
        scratch_shapes=[pltpu.VMEM((2, rows, width), f32), pltpu.SemaphoreType.DMA((2, chips))],
        compiler_params=params,
        name="land",
    )(labels, sums, *arrived[early:])
    return mass, energy, vel


def solution(mesh):
    placed = (
        P(None, ("grp", "bis"), None),
        P(("grp", "bis"), None),
        P(("grp", "bis"), None),
        P(("grp", "bis"), None),
        P(("grp", "bis")),
    )
    return jax.shard_map(
        shards,
        mesh=mesh,
        in_specs=placed,
        out_specs=(P(("grp", "bis"), None), P(("grp", "bis"), None), P(None, ("grp", "bis"), None)),
        check_vma=False,
    )
```

```python
import functools

import jax
import jax.numpy as jnp
from jax import lax
from jax.experimental import pallas as pl
from jax.experimental.pallas import tpu as pltpu
from jax.sharding import PartitionSpec as P

BR = 4
CAP = 2
ZR = 8
HALF_DT = 0.075
NF = 5
RHO, ENE, VELU, VELV, GAM = range(NF)
FAR_P, FAR_U, INFO = 5, 6, 7
SMEM = pl.BlockSpec(memory_space=pltpu.SMEM)
VMEM = pl.BlockSpec(memory_space=pltpu.VMEM)


def sublane(width):
    return lax.broadcasted_iota(jnp.int32, (8, width), 0)


def turn(tile, shift):
    return pltpu.roll(tile, shift, 0)


def left_right(x):
    width = x.shape[1]
    lane = lax.broadcasted_iota(jnp.int32, x.shape, 1)
    left = jnp.where(lane == 0, 0.0, pltpu.roll(x, 1, 1))
    right = jnp.where(lane == width - 1, 0.0, pltpu.roll(x, width - 1, 1))
    return right - left


def at(tile):
    return pl.ds(pl.multiple_of(tile * 8, 8), 8)


def down_up(ref, tile, x, clip=None):
    sub = sublane(x.shape[1])
    before = ref[at(tile - 1 if clip is None else jnp.maximum(tile - 1, 0)), :]
    after = ref[at(tile + 1 if clip is None else jnp.minimum(tile + 1, clip)), :]
    return turn(jnp.where(sub == 0, after, x), 7) - turn(jnp.where(sub == 7, before, x), 1)


def target(path, core):
    return 2 * reached(path, core) + (1 if path[0] else 0)


def where_am_i():
    return lax.axis_index("grp"), lax.axis_index("bis")


def routes(chips, swapped):
    bits = chips.bit_length() - 1
    half = bits // 2 if swapped and bits % 2 == 0 else 0
    swap = lambda mask: (mask << half | mask >> bits - half) & chips - 1
    masks = sorted(range(1, chips), key=lambda mask: (-mask.bit_count(), mask))
    return [(0, 0)] + [(mask, swap(mask)) for mask in masks]


def reached(route, core):
    return route[0] if route[0] == route[1] else jnp.where(core == 0, route[0], route[1])


def pack_kernel(n, *refs):
    chips = n // 2
    order_in, owner_in, slot_in, sweep_in, state_in = refs[:5]
    chip_bufs, across = refs[5 : 5 + chips], refs[5 + chips]
    order, owner, slot, state, sems = refs[6 + chips :]
    width = state.shape[2]
    rows = state.shape[1]
    home = 8 * (NF + 1)
    copies = [pltpu.make_async_copy(order_in, order, sems.at[0])]
    copies += [pltpu.make_async_copy(state_in.at[field], state.at[field], sems.at[1 + field]) for field in range(NF)]
    halves = [slice(0, rows // 2), slice(rows // 2, rows)]
    copies += [
        pltpu.make_async_copy(owner_in, owner, sems.at[1 + NF]),
        pltpu.make_async_copy(slot_in, slot, sems.at[2 + NF]),
        pltpu.make_async_copy(sweep_in, chip_bufs[0].at[home : home + rows, :], sems.at[3 + NF]),
    ]
    copies[0].start()
    for field in range(NF):
        for half in halves:
            pltpu.make_async_copy(state_in.at[field, half, :], state.at[field, half, :], sems.at[1 + field]).start()
    for copy in copies[1 + NF :]:
        copy.start()
    _, me = where_am_i()
    chip, core = me // 2, me % 2
    sub = sublane(width)
    first = me == 0
    goals = [chip ^ reached(route, core) for route in routes(chips, True)]
    copies[0].wait()

    def rim_rows(index):
        start = order[index] * BR
        return start + jnp.where(first, 0, BR - 1), start + jnp.where(first, 1, BR - 2)

    def halo(buf, base, near, far):
        for field in range(NF):
            buf[base + field : base + field + 1, :] = state[field, pl.ds(near, 1), :]
        line = lambda field: state[field, pl.ds(far, 1), :]
        buf[base + FAR_P : base + FAR_P + 1, :] = (line(GAM) - 1.0) * line(RHO) * line(ENE)
        buf[base + FAR_U : base + FAR_U + 1, :] = line(VELU)

    picks = [(order[2 * goal], order[2 * goal + 1]) for goal in goals]
    beyond = [jnp.where(first, jnp.minimum(2 * goal + 2, n - 1), jnp.maximum(2 * goal - 1, 0)) for goal in goals]
    rims = [rim_rows(index) for index in beyond + [jnp.where(first, 0, n - 1)]]
    for field in range(NF):
        copies[1 + field].wait()
        for buf, (low, high) in zip(chip_bufs, picks):
            ta = state[field, pl.ds(pl.multiple_of(low // 2 * 8, 8), 8), :]
            tb = state[field, pl.ds(pl.multiple_of(high // 2 * 8, 8), 8), :]
            even = jnp.where(low % 2 == 0, ta, turn(ta, 4))
            odd = jnp.where(high % 2 == 1, tb, turn(tb, 4))
            buf[8 * field : 8 * field + 8, :] = jnp.where(sub < 4, even, odd)
    for buf, rim in zip(chip_bufs, rims):
        halo(buf, 8 * NF, *rim)
    halo(across, 0, *rims[-1])
    for copy in copies[1 + NF :]:
        copy.wait()
    lane = lax.broadcasted_iota(jnp.int32, (1, width), 1)
    info = jnp.zeros((1, width), jnp.int32)
    for index in range(2 * n):
        value = owner[index] if index < n else slot[index - n]
        info = jnp.where(lane // (width // (2 * n)) == index, value, info)
    for buf in chip_bufs:
        buf[8 * NF + INFO : 8 * NF + INFO + 1, :] = info.astype(jnp.float32)
    for block in range(n):
        line = jnp.where(lane < width // 2, owner[block], slot[block])
        chip_bufs[0][home + rows + block : home + rows + block + 1, :] = line.astype(jnp.float32)


def code_kernel(n, rows, own_home, sib_home, code):
    _, me = where_am_i()
    span = pl.ds(8 * (NF + 1) + rows, n)
    own, sib = own_home[span, 0:128].astype(jnp.int32), sib_home[span, 0:128].astype(jnp.int32)
    line_id = lax.broadcasted_iota(jnp.int32, (n, 128), 0)
    for device in range(2):
        owner = jnp.where(me % 2 == device, own, sib)
        rank = jnp.zeros((n, 128), jnp.int32)
        for block in range(n):
            same = jnp.logical_and(owner == owner[block : block + 1, :], line_id > block)
            rank = jnp.where(same, rank + 1, rank)
        code[device] = (owner ^ me) * (2 * CAP) + (device * CAP) + rank


def labels_of(n, me, infos):
    step = infos[0].shape[1] // (2 * n)
    sub = sublane(128)
    tile = jnp.full((8, 128), -1.0, jnp.float32)
    for device, info in enumerate(infos):
        value = lambda index: jnp.broadcast_to(info[:, index * step : index * step + 1], (8, 128))
        place = jnp.full((8, 128), device * CAP, jnp.int32)
        for block in range(n):
            hit = value(block) == me.astype(jnp.float32)
            tile = jnp.where(jnp.logical_and(hit, sub == place), value(n + block), tile)
            place = jnp.where(hit, place + 1, place)
    return tile


def pack_partials(n, paths, core, code, parts, sends):
    width = parts.shape[3]
    pieces = width // 128
    lanes = [slice(piece * 128, piece * 128 + 128) for piece in range(pieces)]
    for device in range(2):
        wants = [target(path, core) * (2 * CAP) + device * CAP + again for path in paths for again in range(CAP)]
        found = [[jnp.zeros((8, 128), jnp.float32)] * pieces for _ in wants]
        for block in range(n):
            taken = jnp.broadcast_to(code[device, block : block + 1, :], (8, 128))
            tile = [parts[device, block, :, lane] for lane in lanes]
            for index, want in enumerate(wants):
                hit = taken == want
                found[index] = [jnp.where(hit, new, old) for new, old in zip(tile, found[index])]
        for index in range(len(wants)):
            rank = device * CAP + index % CAP
            for piece in range(pieces):
                sends[index // CAP][rank * pieces + piece] = found[index][piece]


def step_kernel(n, *refs):
    chips = n // 2
    refs = list(refs)
    take = lambda count: [refs.pop(0) for _ in range(count)]
    (code,) = take(1)
    mine, theirs = take(chips), take(chips)
    across, across_sib, sweep = take(3)
    nxt_prs, nxt_u, nxt_v, coef = take(4)
    (parts,) = take(1)
    sends = take(chips - 1)
    fld, prs, vols, halo = take(4)
    grp, me = where_am_i()
    chip, core = me // 2, me % 2
    width = sweep.shape[1]
    rows = sweep.shape[0]
    home = 8 * (NF + 1)
    sweep_sib = theirs[0].at[home : home + rows, :]
    tiles = 2 * chips
    sub = sublane(width)
    is_low = core == 0

    def pair(own, sib):
        return jnp.where(is_low, own, sib), jnp.where(is_low, sib, own)

    for index, path in enumerate(routes(chips, True)):
        source = chip ^ reached(path, core)
        own, sib = mine[index], theirs[routes(chips, True).index((path[1], path[0]))]
        for field in range(NF):
            span = pl.ds(8 * field, 8)
            even, odd = pair(own[span, :], sib[span, :])
            fld[field, at(1 + source), :] = jnp.where(sub < 4, even, turn(odd, 4))
            fld[field, at(1 + chips + source), :] = jnp.where(sub < 4, turn(even, 4), odd)
        even, odd = pair(own[8 * NF : home, :], sib[8 * NF : home, :])
        halo[0, source] = even
        halo[1, source] = odd
    even, odd = pair(across[0:8, :], across_sib[0:8, :])
    inside_top = jnp.logical_or(grp > 0, chip > 0)
    inside_bottom = jnp.logical_or(grp < lax.axis_size("grp") - 1, chip < chips - 1)
    top = jnp.where(inside_top, jnp.where(chip == 0, even, halo[1, chips - 1]), 0.0)
    bottom = jnp.where(inside_bottom, jnp.where(chip == chips - 1, odd, halo[0, 0]), 0.0)

    def line(tile, index):
        return jnp.broadcast_to(tile[index : index + 1, :], (8, width))

    for tile, place, near in ((top, 0, 7), (bottom, tiles + 1, 0)):
        span = at(place)
        for field in (RHO, ENE, VELV, GAM):
            fld[field, span, :] = line(tile, field)
        fld[VELU, span, :] = jnp.where(sub == near, line(tile, VELU), line(tile, FAR_U))
        press = (line(tile, GAM) - 1.0) * line(tile, RHO) * line(tile, ENE)
        prs[span, :] = jnp.where(sub == near, press, line(tile, FAR_P))

    def pressure(tile, _):
        span = at(tile)
        prs[span, :] = (fld[GAM, span, :] - 1.0) * fld[RHO, span, :] * fld[ENE, span, :]
        return 0

    lax.fori_loop(1, tiles + 1, pressure, 0, unroll=n <= 8)

    def first(tile, _):
        span = at(tile)
        velu, velv, press = fld[VELU, span, :], fld[VELV, span, :], prs[span, :]
        push = HALF_DT * (down_up(fld.at[VELU], tile, velu, tiles + 1) + left_right(velv))
        grow = 1.0 + push
        scale = HALF_DT / fld[RHO, span, :]
        keep = 1.0 - (fld[GAM, span, :] - 1.0) * push
        nxt_prs[span, :] = press * keep / grow
        nxt_u[span, :] = velu - down_up(prs, tile, press, tiles + 1) * scale
        nxt_v[span, :] = velv - left_right(press) * scale
        coef[span, :] = scale * grow
        vols[0, span, :] = grow
        vols[1, span, :] = fld[ENE, span, :] * keep
        return 0

    lax.fori_loop(0, tiles + 2, first, 0, unroll=n <= 8)
    for place, inside in ((0, inside_top), (tiles + 1, inside_bottom)):
        span = at(place)
        nxt_prs[span, :] = jnp.where(inside, nxt_prs[span, :], 0.0)
        nxt_u[span, :] = jnp.where(inside, nxt_u[span, :], 0.0)

    def cyclic(x):
        return jnp.where(sub % BR == 0, turn(x, 8 - (BR - 1)), turn(x, 1))

    def second(device, index):
        tile = 1 + device * chips + index
        span = at(tile)
        push = HALF_DT * (down_up(nxt_u, tile, nxt_u[span, :]) + left_right(nxt_v[span, :]))
        volume = vols[0, span, :] * (1.0 + push)
        heat_e = vols[1, span, :] * (1.0 - (fld[GAM, span, :] - 1.0) * push)
        mass = fld[RHO, span, :]
        heat = mass * heat_e
        from_own = (core == 0) if device == 0 else (core == 1)
        swept = jnp.where(from_own, sweep[at(index), :], sweep_sib[at(index), :])
        frac = swept * volume / (1.0 + volume)
        mass_go, heat_go = frac * mass, frac * heat
        mass_part = mass - mass_go + cyclic(mass_go)
        heat_part = heat - heat_go + cyclic(heat_go)
        parts[device, 2 * index] = jnp.where(sub < 4, mass_part, turn(heat_part, 4))
        parts[device, 2 * index + 1] = jnp.where(sub < 4, turn(mass_part, 4), heat_part)

    for device in range(2):
        lax.fori_loop(0, chips, lambda index, _, device=device: (second(device, index), 0)[1], 0, unroll=n <= 8)

    pack_partials(n, routes(chips, False)[1:], core, code, parts, sends)


def side_kernel(n, *refs):
    chips = n // 2
    prs, velu, velv, coef, parts, code = refs[:6]
    mine, theirs = refs[6 : 6 + chips], refs[6 + chips : 6 + 2 * chips]
    vel, home, labels = refs[6 + 2 * chips :]
    _, me = where_am_i()
    core = me % 2
    pack_partials(n, routes(chips, False)[:1], core, code, parts, [home])
    paths = routes(chips, True)
    line = slice(8 * NF + INFO, 8 * NF + INFO + 1)
    for index, (mask, _) in enumerate(routes(chips, False)):
        low, high = [path[0] for path in paths].index(mask), [path[1] for path in paths].index(mask)
        even = jnp.where(core == 0, mine[low][line, :], theirs[low][line, :])
        odd = jnp.where(core == 0, theirs[high][line, :], mine[high][line, :])
        labels[index] = labels_of(n, me, (even, odd))

    def one(index, _):
        tile = 1 + core * chips + index
        span, dest = at(tile), at(index)
        press, scale = prs[span, :], coef[span, :]
        vel[0, dest, :] = velu[span, :] - down_up(prs, tile, press) * scale
        vel[1, dest, :] = velv[span, :] - left_right(press) * scale
        return 0

    lax.fori_loop(0, chips, one, 0, unroll=n <= 8)


def land_kernel(n, final, *refs):
    chips = n // 2
    refs = list(refs)
    labels = refs.pop(0)
    if final:
        mass_out, energy_out, sums_out, sems = refs[-4:]
        sums_in, arrived = refs[0], refs[1:-4]
    else:
        sums_in, arrived, sums_out = None, refs[:-1], refs[-1]
    skipped = chips - len(arrived) if final else 0
    parts = sums_out.shape[2] // 128
    sub = sublane(128)

    def send(which, index):
        span = pl.ds(pl.multiple_of(index * 8, 8), 8)
        target_ref = energy_out if which else mass_out
        return pltpu.make_async_copy(sums_out.at[which, span, :], target_ref.at[span, :], sems.at[which, index])

    def tile_pair(index, _):
        span = pl.ds(pl.multiple_of(index * 8, 8), 8)
        sums = [[jnp.zeros((8, 128), jnp.float32) for _ in range(parts)] for _ in range(2)]
        for number, buf in enumerate(arrived):
            for rank in range(2 * CAP):
                tag = jnp.broadcast_to(labels[skipped + number, rank : rank + 1, :], (8, 128))
                for bit in range(2):
                    hit = tag == (2 * index + bit) * 1.0
                    for part in range(parts):
                        sums[bit][part] += jnp.where(hit, buf[rank * parts + part], 0.0)
        for part in range(parts):
            cols = slice(part * 128, part * 128 + 128)
            even, odd = sums[0][part], sums[1][part]
            mass, energy = jnp.where(sub < 4, even, turn(odd, 4)), jnp.where(sub < 4, turn(even, 4), odd)
            if final:
                mass, energy = mass + sums_in[0, span, cols], energy + sums_in[1, span, cols]
            sums_out[0, span, cols] = mass
            sums_out[1, span, cols] = energy
        if final:
            send(0, index).start()
            send(1, index).start()
        return 0

    lax.fori_loop(0, chips, tile_pair, 0, unroll=n <= 8)
    if final:
        for index in range(chips):
            send(0, index).wait()
            send(1, index).wait()


def across_links(groups, n):
    pairs = []
    for grp in range(groups):
        base = grp * n
        pairs += [(base + i, base + i + 1) for i in range(2, n - 2, 2)]
        if grp + 1 < groups:
            turn_at = n - 2 if grp % 2 == 0 else 1
            pairs += [(base + n - 1, base + n), (base + turn_at, base + n + turn_at)]
    used = {i for pair in pairs for i in pair}
    left = [i for i in range(groups * n) if i not in used]
    pairs += [(left[i], left[i + 1]) for i in range(0, len(left), 2)]
    return [link for low, high in pairs for link in ((low, high), (high, low))]


def shards(state, order, sweep, owner, slot_target):
    n = lax.axis_size("bis")
    groups = lax.axis_size("grp")
    chips = n // 2
    rows, width = sweep.shape
    parts = width // 128
    f32 = jnp.float32
    params = pltpu.CompilerParams(vmem_limit_bytes=48 * 1024 * 1024)

    def to_sibling(x):
        return lax.ppermute(x, "bis", [(i, i ^ 1) for i in range(n)])

    def to_chip(x, path, cross):
        links = [(i, i ^ 2 * path[i % 2] ^ cross) for i in range(n)]
        return lax.ppermute(x, "bis", links) if path[0] else x

    paths = routes(chips, True)

    owner = owner.reshape(n)
    extra = -(-(rows + n) // 8) * 8
    packed = pl.pallas_call(
        functools.partial(pack_kernel, n),
        out_shape=[
            jax.ShapeDtypeStruct((8 * (NF + 1) + (0 if mask else extra), width), f32) for mask in range(chips)
        ]
        + [jax.ShapeDtypeStruct((ZR, width), f32)],
        in_specs=[pl.BlockSpec(memory_space=pl.ANY)] * 5,
        out_specs=[VMEM] * (chips + 1),
        scratch_shapes=[
            pltpu.SMEM((n,), jnp.int32),
            pltpu.SMEM((n,), jnp.int32),
            pltpu.SMEM((n,), jnp.int32),
            pltpu.VMEM((NF, rows, width), f32),
            pltpu.SemaphoreType.DMA((NF + 4,)),
        ],
        compiler_params=params,
        name="pack",
    )(*[pltpu.with_memory_space_constraint(x, pltpu.HBM) for x in (order.reshape(n), owner, slot_target, sweep, state)])
    across = lax.ppermute(packed[chips], ("grp", "bis"), across_links(groups, n))
    mine = [to_chip(x, path, 0) for x, path in zip(packed, paths)]
    theirs = [to_sibling(x) for x in mine]
    across_sib = to_sibling(jnp.concatenate([across] + [x[0:8] for x in mine[1:]]))

    code = pl.pallas_call(
        functools.partial(code_kernel, n, rows),
        out_shape=jax.ShapeDtypeStruct((2, n, 128), jnp.int32),
        in_specs=[VMEM] * 2,
        out_specs=VMEM,
        compiler_params=params,
        name="code",
    )(mine[0], theirs[0])

    stack = (2 * chips + 2) * 8
    send_shape = (2 * CAP * parts, 8, 128)
    out = pl.pallas_call(
        functools.partial(step_kernel, n),
        out_shape=[jax.ShapeDtypeStruct((stack, width), f32)] * 4
        + [jax.ShapeDtypeStruct((2, n, 8, width), f32)]
        + [jax.ShapeDtypeStruct(send_shape, f32)] * (chips - 1),
        in_specs=[VMEM] * (2 * chips + 4),
        out_specs=[VMEM] * (chips + 4),
        scratch_shapes=[
            pltpu.VMEM((NF, stack, width), f32),
            pltpu.VMEM((stack, width), f32),
            pltpu.VMEM((2, stack, width), f32),
            pltpu.VMEM((2, chips, 8, width), f32),
        ],
        compiler_params=params,
        name="substeps",
    )(code, *mine, *theirs, across, across_sib, sweep)
    arrived = [to_chip(x, path, 1) for x, path in zip(out[5:], routes(chips, False)[1:])]
    vel, home, labels = pl.pallas_call(
        functools.partial(side_kernel, n),
        out_shape=[
            jax.ShapeDtypeStruct((2, rows, width), f32),
            jax.ShapeDtypeStruct(send_shape, f32),
            jax.ShapeDtypeStruct((chips, 8, 128), f32),
        ],
        in_specs=[VMEM] * (6 + 2 * chips),
        out_specs=[VMEM] * 3,
        compiler_params=params,
        name="velocities",
    )(*out[:5], code, *mine, *theirs)
    arrived = [home] + arrived
    early = 2
    sums = pl.pallas_call(
        functools.partial(land_kernel, n, False),
        out_shape=jax.ShapeDtypeStruct((2, rows, width), f32),
        in_specs=[VMEM] * (1 + early),
        out_specs=VMEM,
        compiler_params=params,
        name="sums",
    )(labels, *arrived[:early])
    mass, energy = pl.pallas_call(
        functools.partial(land_kernel, n, True),
        out_shape=[jax.ShapeDtypeStruct((rows, width), f32)] * 2,
        in_specs=[VMEM] * (2 + chips - early),
        out_specs=[pl.BlockSpec(memory_space=pl.ANY)] * 2,
        scratch_shapes=[pltpu.VMEM((2, rows, width), f32), pltpu.SemaphoreType.DMA((2, chips))],
        compiler_params=params,
        name="land",
    )(labels, sums, *arrived[early:])
    return mass, energy, vel


def solution(mesh):
    placed = (
        P(None, ("grp", "bis"), None),
        P(("grp", "bis"), None),
        P(("grp", "bis"), None),
        P(("grp", "bis"), None),
        P(("grp", "bis")),
    )
    return jax.shard_map(
        shards,
        mesh=mesh,
        in_specs=placed,
        out_specs=(P(("grp", "bis"), None), P(("grp", "bis"), None), P(None, ("grp", "bis"), None)),
        check_vma=False,
    )
```

```python
import functools

import jax
import jax.numpy as jnp
from jax import lax
from jax.experimental import pallas as pl
from jax.experimental.pallas import tpu as pltpu
from jax.sharding import PartitionSpec as P

BR = 4
CAP = 2
ZR = 8
HALF_DT = 0.075
NF = 5
RHO, ENE, VELU, VELV, GAM = range(NF)
FAR_P, FAR_U, INFO = 5, 6, 7
SMEM = pl.BlockSpec(memory_space=pltpu.SMEM)
VMEM = pl.BlockSpec(memory_space=pltpu.VMEM)


def sublane(width):
    return lax.broadcasted_iota(jnp.int32, (8, width), 0)


def turn(tile, shift):
    return pltpu.roll(tile, shift, 0)


def left_right(x):
    width = x.shape[1]
    lane = lax.broadcasted_iota(jnp.int32, x.shape, 1)
    left = jnp.where(lane == 0, 0.0, pltpu.roll(x, 1, 1))
    right = jnp.where(lane == width - 1, 0.0, pltpu.roll(x, width - 1, 1))
    return right - left


def at(tile):
    return pl.ds(pl.multiple_of(tile * 8, 8), 8)


def down_up(ref, tile, x, clip=None):
    sub = sublane(x.shape[1])
    before = ref[at(tile - 1 if clip is None else jnp.maximum(tile - 1, 0)), :]
    after = ref[at(tile + 1 if clip is None else jnp.minimum(tile + 1, clip)), :]
    return turn(jnp.where(sub == 0, after, x), 7) - turn(jnp.where(sub == 7, before, x), 1)


def where_am_i():
    return lax.axis_index("grp"), lax.axis_index("bis")


def routes(chips):
    return [0] + sorted(range(1, chips), key=lambda mask: (-mask.bit_count(), mask))


def crossed(mask):
    return 1 if mask.bit_count() == 1 else 0


def target(mask):
    return 2 * mask + crossed(mask)


def pack_kernel(n, *refs):
    chips = n // 2
    order_in, owner_in, slot_in, sweep_in, state_in = refs[:5]
    chip_bufs, across = refs[5 : 5 + chips], refs[5 + chips]
    order, owner, slot, state, sems = refs[6 + chips :]
    width = state.shape[2]
    rows = state.shape[1]
    home = 8 * (NF + 1)
    copies = [pltpu.make_async_copy(order_in, order, sems.at[0])]
    copies += [pltpu.make_async_copy(state_in.at[field], state.at[field], sems.at[1 + field]) for field in range(NF)]
    halves = [slice(0, rows // 2), slice(rows // 2, rows)]
    copies += [
        pltpu.make_async_copy(owner_in, owner, sems.at[1 + NF]),
        pltpu.make_async_copy(slot_in, slot, sems.at[2 + NF]),
        pltpu.make_async_copy(sweep_in, chip_bufs[0].at[home : home + rows, :], sems.at[3 + NF]),
    ]
    copies[0].start()
    for field in range(NF):
        for half in halves:
            pltpu.make_async_copy(state_in.at[field, half, :], state.at[field, half, :], sems.at[1 + field]).start()
    for copy in copies[1 + NF :]:
        copy.start()
    _, me = where_am_i()
    chip, core = me // 2, me % 2
    sub = sublane(width)
    first = me == 0
    goals = [chip ^ mask for mask in routes(chips)]
    copies[0].wait()

    def rim_rows(index):
        start = order[index] * BR
        return start + jnp.where(first, 0, BR - 1), start + jnp.where(first, 1, BR - 2)

    def halo(buf, base, near, far):
        for field in range(NF):
            buf[base + field : base + field + 1, :] = state[field, pl.ds(near, 1), :]
        line = lambda field: state[field, pl.ds(far, 1), :]
        buf[base + FAR_P : base + FAR_P + 1, :] = (line(GAM) - 1.0) * line(RHO) * line(ENE)
        buf[base + FAR_U : base + FAR_U + 1, :] = line(VELU)

    picks = [(order[2 * goal], order[2 * goal + 1]) for goal in goals]
    beyond = [jnp.where(first, jnp.minimum(2 * goal + 2, n - 1), jnp.maximum(2 * goal - 1, 0)) for goal in goals]
    rims = [rim_rows(index) for index in beyond + [jnp.where(first, 0, n - 1)]]
    for field in range(NF):
        copies[1 + field].wait()
        for buf, (low, high) in zip(chip_bufs, picks):
            ta = state[field, pl.ds(pl.multiple_of(low // 2 * 8, 8), 8), :]
            tb = state[field, pl.ds(pl.multiple_of(high // 2 * 8, 8), 8), :]
            even = jnp.where(low % 2 == 0, ta, turn(ta, 4))
            odd = jnp.where(high % 2 == 1, tb, turn(tb, 4))
            buf[8 * field : 8 * field + 8, :] = jnp.where(sub < 4, even, odd)
    for buf, rim in zip(chip_bufs, rims):
        halo(buf, 8 * NF, *rim)
    halo(across, 0, *rims[-1])
    for copy in copies[1 + NF :]:
        copy.wait()
    lane = lax.broadcasted_iota(jnp.int32, (1, width), 1)
    info = jnp.zeros((1, width), jnp.int32)
    for index in range(2 * n):
        value = owner[index] if index < n else slot[index - n]
        info = jnp.where(lane // (width // (2 * n)) == index, value, info)
    for buf in chip_bufs:
        buf[8 * NF + INFO : 8 * NF + INFO + 1, :] = info.astype(jnp.float32)
    for block in range(n):
        line = jnp.where(lane < width // 2, owner[block], slot[block])
        chip_bufs[0][home + rows + block : home + rows + block + 1, :] = line.astype(jnp.float32)


def code_kernel(n, rows, own_home, sib_home, code):
    _, me = where_am_i()
    span = pl.ds(8 * (NF + 1) + rows, n)
    own, sib = own_home[span, 0:128].astype(jnp.int32), sib_home[span, 0:128].astype(jnp.int32)
    line_id = lax.broadcasted_iota(jnp.int32, (n, 128), 0)
    for device in range(2):
        owner = jnp.where(me % 2 == device, own, sib)
        rank = jnp.zeros((n, 128), jnp.int32)
        for block in range(n):
            same = jnp.logical_and(owner == owner[block : block + 1, :], line_id > block)
            rank = jnp.where(same, rank + 1, rank)
        code[device] = (owner ^ me) * (2 * CAP) + (device * CAP) + rank


def labels_of(n, me, infos):
    step = infos[0].shape[1] // (2 * n)
    sub = sublane(128)
    tile = jnp.full((8, 128), -1.0, jnp.float32)
    for device, info in enumerate(infos):
        value = lambda index: jnp.broadcast_to(info[:, index * step : index * step + 1], (8, 128))
        place = jnp.full((8, 128), device * CAP, jnp.int32)
        for block in range(n):
            hit = value(block) == me.astype(jnp.float32)
            tile = jnp.where(jnp.logical_and(hit, sub == place), value(n + block), tile)
            place = jnp.where(hit, place + 1, place)
    return tile


def pack_partials(n, masks, code, parts, sends):
    width = parts.shape[3]
    pieces = width // 128
    lanes = [slice(piece * 128, piece * 128 + 128) for piece in range(pieces)]
    for device in range(2):
        wants = [target(mask) * (2 * CAP) + device * CAP + again for mask in masks for again in range(CAP)]
        found = [[jnp.zeros((8, 128), jnp.float32)] * pieces for _ in wants]
        for block in range(n):
            taken = jnp.broadcast_to(code[device, block : block + 1, :], (8, 128))
            tile = [parts[device, block, :, lane] for lane in lanes]
            for index, want in enumerate(wants):
                hit = taken == want
                found[index] = [jnp.where(hit, new, old) for new, old in zip(tile, found[index])]
        for index in range(len(wants)):
            rank = device * CAP + index % CAP
            for piece in range(pieces):
                sends[index // CAP][rank * pieces + piece] = found[index][piece]


def step_kernel(n, *refs):
    chips = n // 2
    refs = list(refs)
    take = lambda count: [refs.pop(0) for _ in range(count)]
    (code,) = take(1)
    mine, theirs = take(chips), take(chips)
    across, across_sib, sweep = take(3)
    nxt_prs, nxt_u, nxt_v, coef = take(4)
    (parts,) = take(1)
    sends = take(chips - 1)
    fld, prs, vols, halo = take(4)
    grp, me = where_am_i()
    chip, core = me // 2, me % 2
    width = sweep.shape[1]
    rows = sweep.shape[0]
    home = 8 * (NF + 1)
    sweep_sib = theirs[0].at[home : home + rows, :]
    tiles = 2 * chips
    sub = sublane(width)
    is_low = core == 0

    def pair(own, sib):
        return jnp.where(is_low, own, sib), jnp.where(is_low, sib, own)

    for index, mask in enumerate(routes(chips)):
        source = chip ^ mask
        own, sib = mine[index], theirs[index]
        if crossed(mask):
            own, sib = sib, own
        for field in range(NF):
            span = pl.ds(8 * field, 8)
            even, odd = pair(own[span, :], sib[span, :])
            fld[field, at(1 + source), :] = jnp.where(sub < 4, even, turn(odd, 4))
            fld[field, at(1 + chips + source), :] = jnp.where(sub < 4, turn(even, 4), odd)
        even, odd = pair(own[8 * NF : home, :], sib[8 * NF : home, :])
        halo[0, source] = even
        halo[1, source] = odd
    even, odd = pair(across[0:8, :], across_sib[0:8, :])
    inside_top = jnp.logical_or(grp > 0, chip > 0)
    inside_bottom = jnp.logical_or(grp < lax.axis_size("grp") - 1, chip < chips - 1)
    top = jnp.where(inside_top, jnp.where(chip == 0, even, halo[1, chips - 1]), 0.0)
    bottom = jnp.where(inside_bottom, jnp.where(chip == chips - 1, odd, halo[0, 0]), 0.0)

    def line(tile, index):
        return jnp.broadcast_to(tile[index : index + 1, :], (8, width))

    for tile, place, near in ((top, 0, 7), (bottom, tiles + 1, 0)):
        span = at(place)
        for field in (RHO, ENE, VELV, GAM):
            fld[field, span, :] = line(tile, field)
        fld[VELU, span, :] = jnp.where(sub == near, line(tile, VELU), line(tile, FAR_U))
        press = (line(tile, GAM) - 1.0) * line(tile, RHO) * line(tile, ENE)
        prs[span, :] = jnp.where(sub == near, press, line(tile, FAR_P))

    def pressure(tile, _):
        span = at(tile)
        prs[span, :] = (fld[GAM, span, :] - 1.0) * fld[RHO, span, :] * fld[ENE, span, :]
        return 0

    lax.fori_loop(1, tiles + 1, pressure, 0, unroll=n <= 8)

    def first(tile, _):
        span = at(tile)
        velu, velv, press = fld[VELU, span, :], fld[VELV, span, :], prs[span, :]
        push = HALF_DT * (down_up(fld.at[VELU], tile, velu, tiles + 1) + left_right(velv))
        grow = 1.0 + push
        scale = HALF_DT / fld[RHO, span, :]
        keep = 1.0 - (fld[GAM, span, :] - 1.0) * push
        nxt_prs[span, :] = press * keep / grow
        nxt_u[span, :] = velu - down_up(prs, tile, press, tiles + 1) * scale
        nxt_v[span, :] = velv - left_right(press) * scale
        coef[span, :] = scale * grow
        vols[0, span, :] = grow
        vols[1, span, :] = fld[ENE, span, :] * keep
        return 0

    lax.fori_loop(0, tiles + 2, first, 0, unroll=n <= 8)
    for place, inside in ((0, inside_top), (tiles + 1, inside_bottom)):
        span = at(place)
        nxt_prs[span, :] = jnp.where(inside, nxt_prs[span, :], 0.0)
        nxt_u[span, :] = jnp.where(inside, nxt_u[span, :], 0.0)

    def cyclic(x):
        return jnp.where(sub % BR == 0, turn(x, 8 - (BR - 1)), turn(x, 1))

    def second(device, index):
        tile = 1 + device * chips + index
        span = at(tile)
        push = HALF_DT * (down_up(nxt_u, tile, nxt_u[span, :]) + left_right(nxt_v[span, :]))
        volume = vols[0, span, :] * (1.0 + push)
        heat_e = vols[1, span, :] * (1.0 - (fld[GAM, span, :] - 1.0) * push)
        mass = fld[RHO, span, :]
        heat = mass * heat_e
        from_own = (core == 0) if device == 0 else (core == 1)
        swept = jnp.where(from_own, sweep[at(index), :], sweep_sib[at(index), :])
        frac = swept * volume / (1.0 + volume)
        mass_go, heat_go = frac * mass, frac * heat
        mass_part = mass - mass_go + cyclic(mass_go)
        heat_part = heat - heat_go + cyclic(heat_go)
        parts[device, 2 * index] = jnp.where(sub < 4, mass_part, turn(heat_part, 4))
        parts[device, 2 * index + 1] = jnp.where(sub < 4, turn(mass_part, 4), heat_part)

    for device in range(2):
        lax.fori_loop(0, chips, lambda index, _, device=device: (second(device, index), 0)[1], 0, unroll=n <= 8)

    pack_partials(n, routes(chips)[1:], code, parts, sends)


def side_kernel(n, *refs):
    chips = n // 2
    prs, velu, velv, coef, parts, code = refs[:6]
    mine, theirs = refs[6 : 6 + chips], refs[6 + chips : 6 + 2 * chips]
    vel, home, labels = refs[6 + 2 * chips :]
    _, me = where_am_i()
    core = me % 2
    pack_partials(n, routes(chips)[:1], code, parts, [home])
    line = slice(8 * NF + INFO, 8 * NF + INFO + 1)
    for index, mask in enumerate(routes(chips)):
        own, sib = mine[index][line, :], theirs[index][line, :]
        if crossed(mask):
            own, sib = sib, own
        labels[index] = labels_of(n, me, (jnp.where(core == 0, own, sib), jnp.where(core == 0, sib, own)))

    def one(index, _):
        tile = 1 + core * chips + index
        span, dest = at(tile), at(index)
        press, scale = prs[span, :], coef[span, :]
        vel[0, dest, :] = velu[span, :] - down_up(prs, tile, press) * scale
        vel[1, dest, :] = velv[span, :] - left_right(press) * scale
        return 0

    lax.fori_loop(0, chips, one, 0, unroll=n <= 8)


def land_kernel(n, final, *refs):
    chips = n // 2
    refs = list(refs)
    labels = refs.pop(0)
    if final:
        mass_out, energy_out, sums_out, sems = refs[-4:]
        sums_in, arrived = refs[0], refs[1:-4]
    else:
        sums_in, arrived, sums_out = None, refs[:-1], refs[-1]
    skipped = chips - len(arrived) if final else 0
    parts = sums_out.shape[2] // 128
    sub = sublane(128)

    def send(which, index):
        span = pl.ds(pl.multiple_of(index * 8, 8), 8)
        target_ref = energy_out if which else mass_out
        return pltpu.make_async_copy(sums_out.at[which, span, :], target_ref.at[span, :], sems.at[which, index])

    def tile_pair(index, _):
        span = pl.ds(pl.multiple_of(index * 8, 8), 8)
        sums = [[jnp.zeros((8, 128), jnp.float32) for _ in range(parts)] for _ in range(2)]
        for number, buf in enumerate(arrived):
            for rank in range(2 * CAP):
                tag = jnp.broadcast_to(labels[skipped + number, rank : rank + 1, :], (8, 128))
                for bit in range(2):
                    hit = tag == (2 * index + bit) * 1.0
                    for part in range(parts):
                        sums[bit][part] += jnp.where(hit, buf[rank * parts + part], 0.0)
        for part in range(parts):
            cols = slice(part * 128, part * 128 + 128)
            even, odd = sums[0][part], sums[1][part]
            mass, energy = jnp.where(sub < 4, even, turn(odd, 4)), jnp.where(sub < 4, turn(even, 4), odd)
            if final:
                mass, energy = mass + sums_in[0, span, cols], energy + sums_in[1, span, cols]
            sums_out[0, span, cols] = mass
            sums_out[1, span, cols] = energy
        if final:
            send(0, index).start()
            send(1, index).start()
        return 0

    lax.fori_loop(0, chips, tile_pair, 0, unroll=n <= 8)
    if final:
        for index in range(chips):
            send(0, index).wait()
            send(1, index).wait()


def across_links(groups, n):
    pairs = []
    for grp in range(groups):
        base = grp * n
        pairs += [(base + i, base + i + 1) for i in range(2, n - 2, 2)]
        if grp + 1 < groups:
            turn_at = n - 2 if grp % 2 == 0 else 1
            pairs += [(base + n - 1, base + n), (base + turn_at, base + n + turn_at)]
    used = {i for pair in pairs for i in pair}
    left = [i for i in range(groups * n) if i not in used]
    pairs += [(left[i], left[i + 1]) for i in range(0, len(left), 2)]
    return [link for low, high in pairs for link in ((low, high), (high, low))]


def shards(state, order, sweep, owner, slot_target):
    n = lax.axis_size("bis")
    groups = lax.axis_size("grp")
    chips = n // 2
    rows, width = sweep.shape
    parts = width // 128
    f32 = jnp.float32
    params = pltpu.CompilerParams(vmem_limit_bytes=48 * 1024 * 1024)

    def to_sibling(x):
        return lax.ppermute(x, "bis", [(i, i ^ 1) for i in range(n)])

    def to_chip(x, mask):
        return lax.ppermute(x, "bis", [(i, i ^ target(mask)) for i in range(n)]) if mask else x

    masks = routes(chips)
    owner = owner.reshape(n)
    extra = -(-(rows + n) // 8) * 8
    packed = pl.pallas_call(
        functools.partial(pack_kernel, n),
        out_shape=[
            jax.ShapeDtypeStruct((8 * (NF + 1) + (0 if mask else extra), width), f32) for mask in range(chips)
        ]
        + [jax.ShapeDtypeStruct((ZR, width), f32)],
        in_specs=[pl.BlockSpec(memory_space=pl.ANY)] * 5,
        out_specs=[VMEM] * (chips + 1),
        scratch_shapes=[
            pltpu.SMEM((n,), jnp.int32),
            pltpu.SMEM((n,), jnp.int32),
            pltpu.SMEM((n,), jnp.int32),
            pltpu.VMEM((NF, rows, width), f32),
            pltpu.SemaphoreType.DMA((NF + 4,)),
        ],
        compiler_params=params,
        name="pack",
    )(*[pltpu.with_memory_space_constraint(x, pltpu.HBM) for x in (order.reshape(n), owner, slot_target, sweep, state)])
    across = lax.ppermute(packed[chips], ("grp", "bis"), across_links(groups, n))
    mine = [to_chip(x, mask) for x, mask in zip(packed, masks)]
    theirs = [to_sibling(x) for x in mine]
    across_sib = to_sibling(jnp.concatenate([across] + [x[0:8] for x in mine[1:]]))

    code = pl.pallas_call(
        functools.partial(code_kernel, n, rows),
        out_shape=jax.ShapeDtypeStruct((2, n, 128), jnp.int32),
        in_specs=[VMEM] * 2,
        out_specs=VMEM,
        compiler_params=params,
        name="code",
    )(mine[0], theirs[0])

    stack = (2 * chips + 2) * 8
    send_shape = (2 * CAP * parts, 8, 128)
    out = pl.pallas_call(
        functools.partial(step_kernel, n),
        out_shape=[jax.ShapeDtypeStruct((stack, width), f32)] * 4
        + [jax.ShapeDtypeStruct((2, n, 8, width), f32)]
        + [jax.ShapeDtypeStruct(send_shape, f32)] * (chips - 1),
        in_specs=[VMEM] * (2 * chips + 4),
        out_specs=[VMEM] * (chips + 4),
        scratch_shapes=[
            pltpu.VMEM((NF, stack, width), f32),
            pltpu.VMEM((stack, width), f32),
            pltpu.VMEM((2, stack, width), f32),
            pltpu.VMEM((2, chips, 8, width), f32),
        ],
        compiler_params=params,
        name="substeps",
    )(code, *mine, *theirs, across, across_sib, sweep)
    arrived = [to_chip(x, mask) for x, mask in zip(out[5:], masks[1:])]
    vel, home, labels = pl.pallas_call(
        functools.partial(side_kernel, n),
        out_shape=[
            jax.ShapeDtypeStruct((2, rows, width), f32),
            jax.ShapeDtypeStruct(send_shape, f32),
            jax.ShapeDtypeStruct((chips, 8, 128), f32),
        ],
        in_specs=[VMEM] * (6 + 2 * chips),
        out_specs=[VMEM] * 3,
        compiler_params=params,
        name="velocities",
    )(*out[:5], code, *mine, *theirs)
    arrived = [home] + arrived
    early = 2
    sums = pl.pallas_call(
        functools.partial(land_kernel, n, False),
        out_shape=jax.ShapeDtypeStruct((2, rows, width), f32),
        in_specs=[VMEM] * (1 + early),
        out_specs=VMEM,
        compiler_params=params,
        name="sums",
    )(labels, *arrived[:early])
    mass, energy = pl.pallas_call(
        functools.partial(land_kernel, n, True),
        out_shape=[jax.ShapeDtypeStruct((rows, width), f32)] * 2,
        in_specs=[VMEM] * (2 + chips - early),
        out_specs=[pl.BlockSpec(memory_space=pl.ANY)] * 2,
        scratch_shapes=[pltpu.VMEM((2, rows, width), f32), pltpu.SemaphoreType.DMA((2, chips))],
        compiler_params=params,
        name="land",
    )(labels, sums, *arrived[early:])
    return mass, energy, vel


def solution(mesh):
    placed = (
        P(None, ("grp", "bis"), None),
        P(("grp", "bis"), None),
        P(("grp", "bis"), None),
        P(("grp", "bis"), None),
        P(("grp", "bis")),
    )
    return jax.shard_map(
        shards,
        mesh=mesh,
        in_specs=placed,
        out_specs=(P(("grp", "bis"), None), P(("grp", "bis"), None), P(None, ("grp", "bis"), None)),
        check_vma=False,
    )
```

```python
import functools

import jax
import jax.numpy as jnp
from jax import lax
from jax.experimental import pallas as pl
from jax.experimental.pallas import tpu as pltpu
from jax.sharding import PartitionSpec as P

BR = 4
CAP = 2
ZR = 8
HALF_DT = 0.075
NF = 5
RHO, ENE, VELU, VELV, GAM = range(NF)
FAR_P, FAR_U, INFO = 5, 6, 7
SMEM = pl.BlockSpec(memory_space=pltpu.SMEM)
VMEM = pl.BlockSpec(memory_space=pltpu.VMEM)


def sublane(width):
    return lax.broadcasted_iota(jnp.int32, (8, width), 0)


def turn(tile, shift):
    return pltpu.roll(tile, shift, 0)


def left_right(x):
    width = x.shape[1]
    lane = lax.broadcasted_iota(jnp.int32, x.shape, 1)
    left = jnp.where(lane == 0, 0.0, pltpu.roll(x, 1, 1))
    right = jnp.where(lane == width - 1, 0.0, pltpu.roll(x, width - 1, 1))
    return right - left


def at(tile):
    return pl.ds(pl.multiple_of(tile * 8, 8), 8)


def down_up(ref, tile, x, clip=None):
    sub = sublane(x.shape[1])
    before = ref[at(tile - 1 if clip is None else jnp.maximum(tile - 1, 0)), :]
    after = ref[at(tile + 1 if clip is None else jnp.minimum(tile + 1, clip)), :]
    return turn(jnp.where(sub == 0, after, x), 7) - turn(jnp.where(sub == 7, before, x), 1)


def where_am_i():
    return lax.axis_index("grp"), lax.axis_index("bis")


def routes(chips):
    return [0] + sorted(range(1, chips), key=lambda mask: (-mask.bit_count(), mask))


def crossed(mask):
    return 1 if mask.bit_count() == 1 else 0


def target(mask):
    return 2 * mask + crossed(mask)


def pack_kernel(n, *refs):
    chips = n // 2
    order_in, owner_in, slot_in, sweep_in, state_in = refs[:5]
    chip_bufs, across = refs[5 : 5 + chips], refs[5 + chips]
    order, owner, slot, state, sems = refs[6 + chips :]
    width = state.shape[2]
    rows = state.shape[1]
    home = 8 * (NF + 1)
    copies = [pltpu.make_async_copy(order_in, order, sems.at[0])]
    copies += [pltpu.make_async_copy(state_in.at[field], state.at[field], sems.at[1 + field]) for field in range(NF)]
    halves = [slice(0, rows // 2), slice(rows // 2, rows)]
    copies += [
        pltpu.make_async_copy(owner_in, owner, sems.at[1 + NF]),
        pltpu.make_async_copy(slot_in, slot, sems.at[2 + NF]),
        pltpu.make_async_copy(sweep_in, chip_bufs[0].at[home : home + rows, :], sems.at[3 + NF]),
    ]
    copies[0].start()
    for field in range(NF):
        for half in halves:
            pltpu.make_async_copy(state_in.at[field, half, :], state.at[field, half, :], sems.at[1 + field]).start()
    for copy in copies[1 + NF :]:
        copy.start()
    _, me = where_am_i()
    chip, core = me // 2, me % 2
    sub = sublane(width)
    first = me == 0
    goals = [chip ^ mask for mask in routes(chips)]
    copies[0].wait()

    def rim_rows(index):
        start = order[index] * BR
        return start + jnp.where(first, 0, BR - 1), start + jnp.where(first, 1, BR - 2)

    def halo(buf, base, near, far):
        for field in range(NF):
            buf[base + field : base + field + 1, :] = state[field, pl.ds(near, 1), :]
        line = lambda field: state[field, pl.ds(far, 1), :]
        buf[base + FAR_P : base + FAR_P + 1, :] = (line(GAM) - 1.0) * line(RHO) * line(ENE)
        buf[base + FAR_U : base + FAR_U + 1, :] = line(VELU)

    picks = [(order[2 * goal], order[2 * goal + 1]) for goal in goals]
    beyond = [jnp.where(first, jnp.minimum(2 * goal + 2, n - 1), jnp.maximum(2 * goal - 1, 0)) for goal in goals]
    rims = [rim_rows(index) for index in beyond + [jnp.where(first, 0, n - 1)]]
    for field in range(NF):
        copies[1 + field].wait()
        for buf, (low, high) in zip(chip_bufs, picks):
            ta = state[field, pl.ds(pl.multiple_of(low // 2 * 8, 8), 8), :]
            tb = state[field, pl.ds(pl.multiple_of(high // 2 * 8, 8), 8), :]
            even = jnp.where(low % 2 == 0, ta, turn(ta, 4))
            odd = jnp.where(high % 2 == 1, tb, turn(tb, 4))
            buf[8 * field : 8 * field + 8, :] = jnp.where(sub < 4, even, odd)
    for buf, rim in zip(chip_bufs, rims):
        halo(buf, 8 * NF, *rim)
    halo(across, 0, *rims[-1])
    for copy in copies[1 + NF :]:
        copy.wait()
    lane = lax.broadcasted_iota(jnp.int32, (1, width), 1)
    info = jnp.zeros((1, width), jnp.int32)
    for index in range(2 * n):
        value = owner[index] if index < n else slot[index - n]
        info = jnp.where(lane // (width // (2 * n)) == index, value, info)
    for buf in chip_bufs:
        buf[8 * NF + INFO : 8 * NF + INFO + 1, :] = info.astype(jnp.float32)
    for block in range(n):
        line = jnp.where(lane < width // 2, owner[block], slot[block])
        chip_bufs[0][home + rows + block : home + rows + block + 1, :] = line.astype(jnp.float32)


def code_kernel(n, rows, own_home, sib_home, code):
    _, me = where_am_i()
    span = pl.ds(8 * (NF + 1) + rows, n)
    own, sib = own_home[span, 0:128].astype(jnp.int32), sib_home[span, 0:128].astype(jnp.int32)
    line_id = lax.broadcasted_iota(jnp.int32, (n, 128), 0)
    for device in range(2):
        owner = jnp.where(me % 2 == device, own, sib)
        rank = jnp.zeros((n, 128), jnp.int32)
        for block in range(n):
            same = jnp.logical_and(owner == owner[block : block + 1, :], line_id > block)
            rank = jnp.where(same, rank + 1, rank)
        code[device] = (owner ^ me) * (2 * CAP) + (device * CAP) + rank


def labels_of(n, me, infos):
    step = infos[0].shape[1] // (2 * n)
    sub = sublane(128)
    tile = jnp.full((8, 128), -1.0, jnp.float32)
    for device, info in enumerate(infos):
        value = lambda index: jnp.broadcast_to(info[:, index * step : index * step + 1], (8, 128))
        place = jnp.full((8, 128), device * CAP, jnp.int32)
        for block in range(n):
            hit = value(block) == me.astype(jnp.float32)
            tile = jnp.where(jnp.logical_and(hit, sub == place), value(n + block), tile)
            place = jnp.where(hit, place + 1, place)
    return tile


def pack_partials(n, masks, code, parts, sends):
    width = parts.shape[3]
    pieces = width // 128
    lanes = [slice(piece * 128, piece * 128 + 128) for piece in range(pieces)]
    for device in range(2):
        wants = [target(mask) * (2 * CAP) + device * CAP + again for mask in masks for again in range(CAP)]
        found = [[jnp.zeros((8, 128), jnp.float32)] * pieces for _ in wants]
        for block in range(n):
            taken = jnp.broadcast_to(code[device, block : block + 1, :], (8, 128))
            tile = [parts[device, block, :, lane] for lane in lanes]
            for index, want in enumerate(wants):
                hit = taken == want
                found[index] = [jnp.where(hit, new, old) for new, old in zip(tile, found[index])]
        for index in range(len(wants)):
            rank = device * CAP + index % CAP
            for piece in range(pieces):
                sends[index // CAP][rank * pieces + piece] = found[index][piece]


def step_kernel(n, *refs):
    chips = n // 2
    refs = list(refs)
    take = lambda count: [refs.pop(0) for _ in range(count)]
    (code,) = take(1)
    mine, theirs = take(chips), take(chips)
    across, across_sib, sweep = take(3)
    nxt_prs, nxt_u, nxt_v, coef = take(4)
    (parts,) = take(1)
    sends = take(chips - 1)
    fld, prs, vols, halo = take(4)
    grp, me = where_am_i()
    chip, core = me // 2, me % 2
    width = sweep.shape[1]
    rows = sweep.shape[0]
    home = 8 * (NF + 1)
    sweep_sib = theirs[0].at[home : home + rows, :]
    tiles = 2 * chips
    sub = sublane(width)
    is_low = core == 0

    def pair(own, sib):
        return jnp.where(is_low, own, sib), jnp.where(is_low, sib, own)

    for index, mask in enumerate(routes(chips)):
        source = chip ^ mask
        own, sib = mine[index], theirs[index]
        if crossed(mask):
            own, sib = sib, own
        placed = (at(1 + source), at(1 + chips + source))
        blocks = []
        for field in range(NF):
            span = pl.ds(8 * field, 8)
            even, odd = pair(own[span, :], sib[span, :])
            blocks.append((jnp.where(sub < 4, even, turn(odd, 4)), jnp.where(sub < 4, turn(even, 4), odd)))
            for where_to, block in zip(placed, blocks[field]):
                fld[field, where_to, :] = block
        for device, where_to in enumerate(placed):
            prs[where_to, :] = (blocks[GAM][device] - 1.0) * blocks[RHO][device] * blocks[ENE][device]
        even, odd = pair(own[8 * NF : home, :], sib[8 * NF : home, :])
        halo[0, source] = even
        halo[1, source] = odd
    even, odd = pair(across[0:8, :], across_sib[0:8, :])
    inside_top = jnp.logical_or(grp > 0, chip > 0)
    inside_bottom = jnp.logical_or(grp < lax.axis_size("grp") - 1, chip < chips - 1)
    top = jnp.where(inside_top, jnp.where(chip == 0, even, halo[1, chips - 1]), 0.0)
    bottom = jnp.where(inside_bottom, jnp.where(chip == chips - 1, odd, halo[0, 0]), 0.0)

    def line(tile, index):
        return jnp.broadcast_to(tile[index : index + 1, :], (8, width))

    for tile, place, near in ((top, 0, 7), (bottom, tiles + 1, 0)):
        span = at(place)
        for field in (RHO, ENE, VELV, GAM):
            fld[field, span, :] = line(tile, field)
        fld[VELU, span, :] = jnp.where(sub == near, line(tile, VELU), line(tile, FAR_U))
        press = (line(tile, GAM) - 1.0) * line(tile, RHO) * line(tile, ENE)
        prs[span, :] = jnp.where(sub == near, press, line(tile, FAR_P))

    def first(tile, _):
        span = at(tile)
        velu, velv, press = fld[VELU, span, :], fld[VELV, span, :], prs[span, :]
        push = HALF_DT * (down_up(fld.at[VELU], tile, velu, tiles + 1) + left_right(velv))
        grow = 1.0 + push
        scale = HALF_DT / fld[RHO, span, :]
        keep = 1.0 - (fld[GAM, span, :] - 1.0) * push
        nxt_prs[span, :] = press * keep / grow
        nxt_u[span, :] = velu - down_up(prs, tile, press, tiles + 1) * scale
        nxt_v[span, :] = velv - left_right(press) * scale
        coef[span, :] = scale * grow
        vols[0, span, :] = grow
        vols[1, span, :] = fld[ENE, span, :] * keep
        return 0

    lax.fori_loop(0, tiles + 2, first, 0, unroll=n <= 8)
    for place, inside in ((0, inside_top), (tiles + 1, inside_bottom)):
        span = at(place)
        nxt_prs[span, :] = jnp.where(inside, nxt_prs[span, :], 0.0)
        nxt_u[span, :] = jnp.where(inside, nxt_u[span, :], 0.0)

    def cyclic(x):
        return jnp.where(sub % BR == 0, turn(x, 8 - (BR - 1)), turn(x, 1))

    def second(device, index):
        tile = 1 + device * chips + index
        span = at(tile)
        push = HALF_DT * (down_up(nxt_u, tile, nxt_u[span, :]) + left_right(nxt_v[span, :]))
        volume = vols[0, span, :] * (1.0 + push)
        heat_e = vols[1, span, :] * (1.0 - (fld[GAM, span, :] - 1.0) * push)
        mass = fld[RHO, span, :]
        heat = mass * heat_e
        from_own = (core == 0) if device == 0 else (core == 1)
        swept = jnp.where(from_own, sweep[at(index), :], sweep_sib[at(index), :])
        frac = swept * volume / (1.0 + volume)
        mass_go, heat_go = frac * mass, frac * heat
        mass_part = mass - mass_go + cyclic(mass_go)
        heat_part = heat - heat_go + cyclic(heat_go)
        parts[device, 2 * index] = jnp.where(sub < 4, mass_part, turn(heat_part, 4))
        parts[device, 2 * index + 1] = jnp.where(sub < 4, turn(mass_part, 4), heat_part)

    for device in range(2):
        lax.fori_loop(0, chips, lambda index, _, device=device: (second(device, index), 0)[1], 0, unroll=n <= 8)

    pack_partials(n, routes(chips)[1:], code, parts, sends)


def side_kernel(n, *refs):
    chips = n // 2
    prs, velu, velv, coef, parts, code = refs[:6]
    mine, theirs = refs[6 : 6 + chips], refs[6 + chips : 6 + 2 * chips]
    vel, home, labels = refs[6 + 2 * chips :]
    _, me = where_am_i()
    core = me % 2
    pack_partials(n, routes(chips)[:1], code, parts, [home])
    line = slice(8 * NF + INFO, 8 * NF + INFO + 1)
    for index, mask in enumerate(routes(chips)):
        own, sib = mine[index][line, :], theirs[index][line, :]
        if crossed(mask):
            own, sib = sib, own
        labels[index] = labels_of(n, me, (jnp.where(core == 0, own, sib), jnp.where(core == 0, sib, own)))

    def one(index, _):
        tile = 1 + core * chips + index
        span, dest = at(tile), at(index)
        press, scale = prs[span, :], coef[span, :]
        vel[0, dest, :] = velu[span, :] - down_up(prs, tile, press) * scale
        vel[1, dest, :] = velv[span, :] - left_right(press) * scale
        return 0

    lax.fori_loop(0, chips, one, 0, unroll=n <= 8)


def land_kernel(n, final, *refs):
    chips = n // 2
    refs = list(refs)
    labels = refs.pop(0)
    if final:
        mass_out, energy_out, sums_out, sems = refs[-4:]
        sums_in, arrived = refs[0], refs[1:-4]
    else:
        sums_in, arrived, sums_out = None, refs[:-1], refs[-1]
    skipped = chips - len(arrived) if final else 0
    parts = sums_out.shape[2] // 128
    sub = sublane(128)

    def send(which, index):
        span = pl.ds(pl.multiple_of(index * 8, 8), 8)
        target_ref = energy_out if which else mass_out
        return pltpu.make_async_copy(sums_out.at[which, span, :], target_ref.at[span, :], sems.at[which, index])

    def tile_pair(index, _):
        span = pl.ds(pl.multiple_of(index * 8, 8), 8)
        sums = [[jnp.zeros((8, 128), jnp.float32) for _ in range(parts)] for _ in range(2)]
        for number, buf in enumerate(arrived):
            for rank in range(2 * CAP):
                tag = jnp.broadcast_to(labels[skipped + number, rank : rank + 1, :], (8, 128))
                for bit in range(2):
                    hit = tag == (2 * index + bit) * 1.0
                    for part in range(parts):
                        sums[bit][part] += jnp.where(hit, buf[rank * parts + part], 0.0)
        for part in range(parts):
            cols = slice(part * 128, part * 128 + 128)
            even, odd = sums[0][part], sums[1][part]
            mass, energy = jnp.where(sub < 4, even, turn(odd, 4)), jnp.where(sub < 4, turn(even, 4), odd)
            if final:
                mass, energy = mass + sums_in[0, span, cols], energy + sums_in[1, span, cols]
            sums_out[0, span, cols] = mass
            sums_out[1, span, cols] = energy
        if final:
            send(0, index).start()
            send(1, index).start()
        return 0

    lax.fori_loop(0, chips, tile_pair, 0, unroll=n <= 8)
    if final:
        for index in range(chips):
            send(0, index).wait()
            send(1, index).wait()


def across_links(groups, n):
    pairs = []
    for grp in range(groups):
        base = grp * n
        pairs += [(base + i, base + i + 1) for i in range(2, n - 2, 2)]
        if grp + 1 < groups:
            turn_at = n - 2 if grp % 2 == 0 else 1
            pairs += [(base + n - 1, base + n), (base + turn_at, base + n + turn_at)]
    used = {i for pair in pairs for i in pair}
    left = [i for i in range(groups * n) if i not in used]
    pairs += [(left[i], left[i + 1]) for i in range(0, len(left), 2)]
    return [link for low, high in pairs for link in ((low, high), (high, low))]


def shards(state, order, sweep, owner, slot_target):
    n = lax.axis_size("bis")
    groups = lax.axis_size("grp")
    chips = n // 2
    rows, width = sweep.shape
    parts = width // 128
    f32 = jnp.float32
    params = pltpu.CompilerParams(vmem_limit_bytes=48 * 1024 * 1024)

    def to_sibling(x):
        return lax.ppermute(x, "bis", [(i, i ^ 1) for i in range(n)])

    def to_chip(x, mask):
        return lax.ppermute(x, "bis", [(i, i ^ target(mask)) for i in range(n)]) if mask else x

    masks = routes(chips)
    owner = owner.reshape(n)
    extra = -(-(rows + n) // 8) * 8
    packed = pl.pallas_call(
        functools.partial(pack_kernel, n),
        out_shape=[
            jax.ShapeDtypeStruct((8 * (NF + 1) + (0 if mask else extra), width), f32) for mask in range(chips)
        ]
        + [jax.ShapeDtypeStruct((ZR, width), f32)],
        in_specs=[pl.BlockSpec(memory_space=pl.ANY)] * 5,
        out_specs=[VMEM] * (chips + 1),
        scratch_shapes=[
            pltpu.SMEM((n,), jnp.int32),
            pltpu.SMEM((n,), jnp.int32),
            pltpu.SMEM((n,), jnp.int32),
            pltpu.VMEM((NF, rows, width), f32),
            pltpu.SemaphoreType.DMA((NF + 4,)),
        ],
        compiler_params=params,
        name="pack",
    )(*[pltpu.with_memory_space_constraint(x, pltpu.HBM) for x in (order.reshape(n), owner, slot_target, sweep, state)])
    across = lax.ppermute(packed[chips], ("grp", "bis"), across_links(groups, n))
    mine = [to_chip(x, mask) for x, mask in zip(packed, masks)]
    theirs = [to_sibling(x) for x in mine]
    across_sib = to_sibling(jnp.concatenate([across] + [x[0:8] for x in mine[1:]]))

    code = pl.pallas_call(
        functools.partial(code_kernel, n, rows),
        out_shape=jax.ShapeDtypeStruct((2, n, 128), jnp.int32),
        in_specs=[VMEM] * 2,
        out_specs=VMEM,
        compiler_params=params,
        name="code",
    )(mine[0], theirs[0])

    stack = (2 * chips + 2) * 8
    send_shape = (2 * CAP * parts, 8, 128)
    out = pl.pallas_call(
        functools.partial(step_kernel, n),
        out_shape=[jax.ShapeDtypeStruct((stack, width), f32)] * 4
        + [jax.ShapeDtypeStruct((2, n, 8, width), f32)]
        + [jax.ShapeDtypeStruct(send_shape, f32)] * (chips - 1),
        in_specs=[VMEM] * (2 * chips + 4),
        out_specs=[VMEM] * (chips + 4),
        scratch_shapes=[
            pltpu.VMEM((NF, stack, width), f32),
            pltpu.VMEM((stack, width), f32),
            pltpu.VMEM((2, stack, width), f32),
            pltpu.VMEM((2, chips, 8, width), f32),
        ],
        compiler_params=params,
        name="substeps",
    )(code, *mine, *theirs, across, across_sib, sweep)
    arrived = [to_chip(x, mask) for x, mask in zip(out[5:], masks[1:])]
    vel, home, labels = pl.pallas_call(
        functools.partial(side_kernel, n),
        out_shape=[
            jax.ShapeDtypeStruct((2, rows, width), f32),
            jax.ShapeDtypeStruct(send_shape, f32),
            jax.ShapeDtypeStruct((chips, 8, 128), f32),
        ],
        in_specs=[VMEM] * (6 + 2 * chips),
        out_specs=[VMEM] * 3,
        compiler_params=params,
        name="velocities",
    )(*out[:5], code, *mine, *theirs)
    arrived = [home] + arrived
    early = 2
    sums = pl.pallas_call(
        functools.partial(land_kernel, n, False),
        out_shape=jax.ShapeDtypeStruct((2, rows, width), f32),
        in_specs=[VMEM] * (1 + early),
        out_specs=VMEM,
        compiler_params=params,
        name="sums",
    )(labels, *arrived[:early])
    mass, energy = pl.pallas_call(
        functools.partial(land_kernel, n, True),
        out_shape=[jax.ShapeDtypeStruct((rows, width), f32)] * 2,
        in_specs=[VMEM] * (2 + chips - early),
        out_specs=[pl.BlockSpec(memory_space=pl.ANY)] * 2,
        scratch_shapes=[pltpu.VMEM((2, rows, width), f32), pltpu.SemaphoreType.DMA((2, chips))],
        compiler_params=params,
        name="land",
    )(labels, sums, *arrived[early:])
    return mass, energy, vel


def solution(mesh):
    placed = (
        P(None, ("grp", "bis"), None),
        P(("grp", "bis"), None),
        P(("grp", "bis"), None),
        P(("grp", "bis"), None),
        P(("grp", "bis")),
    )
    return jax.shard_map(
        shards,
        mesh=mesh,
        in_specs=placed,
        out_specs=(P(("grp", "bis"), None), P(("grp", "bis"), None), P(None, ("grp", "bis"), None)),
        check_vma=False,
    )
```

```python
import functools

import jax
import jax.numpy as jnp
from jax import lax
from jax.experimental import pallas as pl
from jax.experimental.pallas import tpu as pltpu
from jax.sharding import PartitionSpec as P

BR = 4
CAP = 2
ZR = 8
HALF_DT = 0.075
NF = 5
RHO, ENE, VELU, VELV, GAM = range(NF)
FAR_P, FAR_U, INFO = 5, 6, 7
SMEM = pl.BlockSpec(memory_space=pltpu.SMEM)
VMEM = pl.BlockSpec(memory_space=pltpu.VMEM)


def sublane(width):
    return lax.broadcasted_iota(jnp.int32, (8, width), 0)


def turn(tile, shift):
    return pltpu.roll(tile, shift, 0)


def left_right(x):
    width = x.shape[1]
    lane = lax.broadcasted_iota(jnp.int32, x.shape, 1)
    left = jnp.where(lane == 0, 0.0, pltpu.roll(x, 1, 1))
    right = jnp.where(lane == width - 1, 0.0, pltpu.roll(x, width - 1, 1))
    return right - left


def at(tile):
    return pl.ds(pl.multiple_of(tile * 8, 8), 8)


def down_up(ref, tile, x, clip=None):
    sub = sublane(x.shape[1])
    before = ref[at(tile - 1 if clip is None else jnp.maximum(tile - 1, 0)), :]
    after = ref[at(tile + 1 if clip is None else jnp.minimum(tile + 1, clip)), :]
    return turn(jnp.where(sub == 0, after, x), 7) - turn(jnp.where(sub == 7, before, x), 1)


def where_am_i():
    return lax.axis_index("grp"), lax.axis_index("bis")


def routes(chips):
    return [0] + sorted(range(1, chips), key=lambda mask: (-mask.bit_count(), mask))


def crossed(mask):
    return 1 if mask.bit_count() == 1 else 0


def target(mask):
    return 2 * mask + crossed(mask)


def pack_kernel(n, *refs):
    chips = n // 2
    order_in, owner_in, slot_in, sweep_in, state_in = refs[:5]
    chip_bufs, across = refs[5 : 5 + chips], refs[5 + chips]
    order, owner, slot, state, sems = refs[6 + chips :]
    width = state.shape[2]
    rows = state.shape[1]
    home = 8 * (NF + 1)
    copies = [pltpu.make_async_copy(order_in, order, sems.at[0])]
    copies += [pltpu.make_async_copy(state_in.at[field], state.at[field], sems.at[1 + field]) for field in range(NF)]
    halves = [slice(0, rows // 2), slice(rows // 2, rows)]
    copies += [
        pltpu.make_async_copy(owner_in, owner, sems.at[1 + NF]),
        pltpu.make_async_copy(slot_in, slot, sems.at[2 + NF]),
        pltpu.make_async_copy(sweep_in, chip_bufs[0].at[home : home + rows, :], sems.at[3 + NF]),
    ]
    copies[0].start()
    for field in range(NF):
        for half in halves:
            pltpu.make_async_copy(state_in.at[field, half, :], state.at[field, half, :], sems.at[1 + field]).start()
    for copy in copies[1 + NF :]:
        copy.start()
    _, me = where_am_i()
    chip, core = me // 2, me % 2
    sub = sublane(width)
    first = me == 0
    goals = [chip ^ mask for mask in routes(chips)]
    copies[0].wait()

    def rim_rows(index):
        start = order[index] * BR
        return start + jnp.where(first, 0, BR - 1), start + jnp.where(first, 1, BR - 2)

    def halo(buf, base, near, far):
        for field in range(NF):
            buf[base + field : base + field + 1, :] = state[field, pl.ds(near, 1), :]
        line = lambda field: state[field, pl.ds(far, 1), :]
        buf[base + FAR_P : base + FAR_P + 1, :] = (line(GAM) - 1.0) * line(RHO) * line(ENE)
        buf[base + FAR_U : base + FAR_U + 1, :] = line(VELU)

    picks = [(order[2 * goal], order[2 * goal + 1]) for goal in goals]
    beyond = [jnp.where(first, jnp.minimum(2 * goal + 2, n - 1), jnp.maximum(2 * goal - 1, 0)) for goal in goals]
    rims = [rim_rows(index) for index in beyond + [jnp.where(first, 0, n - 1)]]
    for field in range(NF):
        copies[1 + field].wait()
        for buf, (low, high) in zip(chip_bufs, picks):
            ta = state[field, pl.ds(pl.multiple_of(low // 2 * 8, 8), 8), :]
            tb = state[field, pl.ds(pl.multiple_of(high // 2 * 8, 8), 8), :]
            even = jnp.where(low % 2 == 0, ta, turn(ta, 4))
            odd = jnp.where(high % 2 == 1, tb, turn(tb, 4))
            buf[8 * field : 8 * field + 8, :] = jnp.where(sub < 4, even, odd)
    for buf, rim in zip(chip_bufs, rims):
        halo(buf, 8 * NF, *rim)
    halo(across, 0, *rims[-1])
    for copy in copies[1 + NF :]:
        copy.wait()
    lane = lax.broadcasted_iota(jnp.int32, (1, width), 1)
    info = jnp.zeros((1, width), jnp.int32)
    for index in range(2 * n):
        value = owner[index] if index < n else slot[index - n]
        info = jnp.where(lane // (width // (2 * n)) == index, value, info)
    for buf in chip_bufs:
        buf[8 * NF + INFO : 8 * NF + INFO + 1, :] = info.astype(jnp.float32)
    for block in range(n):
        line = jnp.where(lane < width // 2, owner[block], slot[block])
        chip_bufs[0][home + rows + block : home + rows + block + 1, :] = line.astype(jnp.float32)


def code_kernel(n, rows, own_home, sib_home, code):
    _, me = where_am_i()
    span = pl.ds(8 * (NF + 1) + rows, n)
    own, sib = own_home[span, 0:128].astype(jnp.int32), sib_home[span, 0:128].astype(jnp.int32)
    line_id = lax.broadcasted_iota(jnp.int32, (n, 128), 0)
    for device in range(2):
        owner = jnp.where(me % 2 == device, own, sib)
        rank = jnp.zeros((n, 128), jnp.int32)
        for block in range(n):
            same = jnp.logical_and(owner == owner[block : block + 1, :], line_id > block)
            rank = jnp.where(same, rank + 1, rank)
        code[device] = (owner ^ me) * (2 * CAP) + (device * CAP) + rank


def labels_of(n, me, infos):
    step = infos[0].shape[1] // (2 * n)
    sub = sublane(128)
    tile = jnp.full((8, 128), -1.0, jnp.float32)
    for device, info in enumerate(infos):
        value = lambda index: jnp.broadcast_to(info[:, index * step : index * step + 1], (8, 128))
        place = jnp.full((8, 128), device * CAP, jnp.int32)
        for block in range(n):
            hit = value(block) == me.astype(jnp.float32)
            tile = jnp.where(jnp.logical_and(hit, sub == place), value(n + block), tile)
            place = jnp.where(hit, place + 1, place)
    return tile


def pack_partials(n, masks, code, parts, sends):
    width = parts.shape[3]
    pieces = width // 128
    lanes = [slice(piece * 128, piece * 128 + 128) for piece in range(pieces)]
    for device in range(2):
        wants = [target(mask) * (2 * CAP) + device * CAP + again for mask in masks for again in range(CAP)]
        found = [[jnp.zeros((8, 128), jnp.float32)] * pieces for _ in wants]
        for block in range(n):
            taken = jnp.broadcast_to(code[device, block : block + 1, :], (8, 128))
            tile = [parts[device, block, :, lane] for lane in lanes]
            for index, want in enumerate(wants):
                hit = taken == want
                found[index] = [jnp.where(hit, new, old) for new, old in zip(tile, found[index])]
        for index in range(len(wants)):
            rank = device * CAP + index % CAP
            for piece in range(pieces):
                sends[index // CAP][rank * pieces + piece] = found[index][piece]


def step_kernel(n, *refs):
    chips = n // 2
    refs = list(refs)
    take = lambda count: [refs.pop(0) for _ in range(count)]
    (code,) = take(1)
    mine, theirs = take(chips), take(chips)
    across, across_sib, sweep = take(3)
    nxt_prs, nxt_u, nxt_v, coef = take(4)
    (parts,) = take(1)
    sends = take(chips - 1)
    fld, prs, vols, halo = take(4)
    grp, me = where_am_i()
    chip, core = me // 2, me % 2
    width = sweep.shape[1]
    rows = sweep.shape[0]
    home = 8 * (NF + 1)
    sweep_sib = theirs[0].at[home : home + rows, :]
    tiles = 2 * chips
    sub = sublane(width)
    is_low = core == 0

    def pair(own, sib):
        return jnp.where(is_low, own, sib), jnp.where(is_low, sib, own)

    for index, mask in enumerate(routes(chips)):
        source = chip ^ mask
        own, sib = mine[index], theirs[index]
        if crossed(mask):
            own, sib = sib, own
        placed = (at(1 + source), at(1 + chips + source))
        blocks = []
        for field in range(NF):
            span = pl.ds(8 * field, 8)
            even, odd = pair(own[span, :], sib[span, :])
            blocks.append((jnp.where(sub < 4, even, turn(odd, 4)), jnp.where(sub < 4, turn(even, 4), odd)))
            for where_to, block in zip(placed, blocks[field]):
                fld[field, where_to, :] = block
        for device, where_to in enumerate(placed):
            prs[where_to, :] = (blocks[GAM][device] - 1.0) * blocks[RHO][device] * blocks[ENE][device]
        even, odd = pair(own[8 * NF : home, :], sib[8 * NF : home, :])
        halo[0, source] = even
        halo[1, source] = odd
    even, odd = pair(across[0:8, :], across_sib[0:8, :])
    inside_top = jnp.logical_or(grp > 0, chip > 0)
    inside_bottom = jnp.logical_or(grp < lax.axis_size("grp") - 1, chip < chips - 1)
    top = jnp.where(inside_top, jnp.where(chip == 0, even, halo[1, chips - 1]), 0.0)
    bottom = jnp.where(inside_bottom, jnp.where(chip == chips - 1, odd, halo[0, 0]), 0.0)

    def line(tile, index):
        return jnp.broadcast_to(tile[index : index + 1, :], (8, width))

    for tile, place, near in ((top, 0, 7), (bottom, tiles + 1, 0)):
        span = at(place)
        for field in (RHO, ENE, VELV, GAM):
            fld[field, span, :] = line(tile, field)
        fld[VELU, span, :] = jnp.where(sub == near, line(tile, VELU), line(tile, FAR_U))
        press = (line(tile, GAM) - 1.0) * line(tile, RHO) * line(tile, ENE)
        prs[span, :] = jnp.where(sub == near, press, line(tile, FAR_P))

    def first(tile, _):
        span = at(tile)
        velu, velv, press = fld[VELU, span, :], fld[VELV, span, :], prs[span, :]
        push = HALF_DT * (down_up(fld.at[VELU], tile, velu, tiles + 1) + left_right(velv))
        grow = 1.0 + push
        scale = HALF_DT / fld[RHO, span, :]
        keep = 1.0 - (fld[GAM, span, :] - 1.0) * push
        nxt_prs[span, :] = press * keep / grow
        nxt_u[span, :] = velu - down_up(prs, tile, press, tiles + 1) * scale
        nxt_v[span, :] = velv - left_right(press) * scale
        coef[span, :] = scale * grow
        vols[0, span, :] = grow
        vols[1, span, :] = fld[ENE, span, :] * keep
        return 0

    lax.fori_loop(0, tiles + 2, first, 0, unroll=n <= 8)
    for place, inside in ((0, inside_top), (tiles + 1, inside_bottom)):
        span = at(place)
        nxt_prs[span, :] = jnp.where(inside, nxt_prs[span, :], 0.0)
        nxt_u[span, :] = jnp.where(inside, nxt_u[span, :], 0.0)

    def cyclic(x):
        return jnp.where(sub % BR == 0, turn(x, 8 - (BR - 1)), turn(x, 1))

    def second(device, index):
        tile = 1 + device * chips + index
        span = at(tile)
        push = HALF_DT * (down_up(nxt_u, tile, nxt_u[span, :]) + left_right(nxt_v[span, :]))
        volume = vols[0, span, :] * (1.0 + push)
        heat_e = vols[1, span, :] * (1.0 - (fld[GAM, span, :] - 1.0) * push)
        mass = fld[RHO, span, :]
        heat = mass * heat_e
        from_own = (core == 0) if device == 0 else (core == 1)
        swept = jnp.where(from_own, sweep[at(index), :], sweep_sib[at(index), :])
        frac = swept * volume / (1.0 + volume)
        mass_go, heat_go = frac * mass, frac * heat
        mass_part = mass - mass_go + cyclic(mass_go)
        heat_part = heat - heat_go + cyclic(heat_go)
        parts[device, 2 * index] = jnp.where(sub < 4, mass_part, turn(heat_part, 4))
        parts[device, 2 * index + 1] = jnp.where(sub < 4, turn(mass_part, 4), heat_part)

    for device in range(2):
        lax.fori_loop(0, chips, lambda index, _, device=device: (second(device, index), 0)[1], 0, unroll=n <= 8)

    pack_partials(n, routes(chips)[1:], code, parts, sends)


def side_kernel(n, *refs):
    chips = n // 2
    prs, velu, velv, coef, parts, code = refs[:6]
    mine, theirs = refs[6 : 6 + chips], refs[6 + chips : 6 + 2 * chips]
    vel, home, labels = refs[6 + 2 * chips :]
    _, me = where_am_i()
    core = me % 2
    pack_partials(n, routes(chips)[:1], code, parts, [home])
    line = slice(8 * NF + INFO, 8 * NF + INFO + 1)
    for index, mask in enumerate(routes(chips)):
        own, sib = mine[index][line, :], theirs[index][line, :]
        if crossed(mask):
            own, sib = sib, own
        labels[index] = labels_of(n, me, (jnp.where(core == 0, own, sib), jnp.where(core == 0, sib, own)))

    def one(index, _):
        tile = 1 + core * chips + index
        span, dest = at(tile), at(index)
        press, scale = prs[span, :], coef[span, :]
        vel[0, dest, :] = velu[span, :] - down_up(prs, tile, press) * scale
        vel[1, dest, :] = velv[span, :] - left_right(press) * scale
        return 0

    lax.fori_loop(0, chips, one, 0, unroll=n <= 8)


def land_kernel(n, final, *refs):
    chips = n // 2
    refs = list(refs)
    labels = refs.pop(0)
    if final:
        mass_out, energy_out, sums_out, sems = refs[-4:]
        sums_in, arrived = refs[0], refs[1:-4]
    else:
        sums_in, arrived, sums_out = None, refs[:-1], refs[-1]
    skipped = chips - len(arrived) if final else 0
    parts = sums_out.shape[2] // 128
    sub = sublane(128)

    def send(which, index):
        span = pl.ds(pl.multiple_of(index * 8, 8), 8)
        target_ref = energy_out if which else mass_out
        return pltpu.make_async_copy(sums_out.at[which, span, :], target_ref.at[span, :], sems.at[which, index])

    def tile_pair(index, _):
        span = pl.ds(pl.multiple_of(index * 8, 8), 8)
        sums = [[jnp.zeros((8, 128), jnp.float32) for _ in range(parts)] for _ in range(2)]
        for number, buf in enumerate(arrived):
            for rank in range(2 * CAP):
                tag = jnp.broadcast_to(labels[skipped + number, rank : rank + 1, :], (8, 128))
                for bit in range(2):
                    hit = tag == (2 * index + bit) * 1.0
                    for part in range(parts):
                        sums[bit][part] += jnp.where(hit, buf[rank * parts + part], 0.0)
        for part in range(parts):
            cols = slice(part * 128, part * 128 + 128)
            even, odd = sums[0][part], sums[1][part]
            mass, energy = jnp.where(sub < 4, even, turn(odd, 4)), jnp.where(sub < 4, turn(even, 4), odd)
            if final:
                mass, energy = mass + sums_in[0, span, cols], energy + sums_in[1, span, cols]
            sums_out[0, span, cols] = mass
            sums_out[1, span, cols] = energy
        if final:
            send(0, index).start()
            send(1, index).start()
        return 0

    lax.fori_loop(0, chips, tile_pair, 0, unroll=n <= 8)
    if final:
        for index in range(chips):
            send(0, index).wait()
            send(1, index).wait()


def across_links(groups, n):
    pairs = []
    for grp in range(groups):
        base = grp * n
        pairs += [(base + i, base + i + 1) for i in range(2, n - 2, 2)]
        if grp + 1 < groups:
            turn_at = n - 2 if grp % 2 == 0 else 1
            pairs += [(base + n - 1, base + n), (base + turn_at, base + n + turn_at)]
    used = {i for pair in pairs for i in pair}
    left = [i for i in range(groups * n) if i not in used]
    pairs += [(left[i], left[i + 1]) for i in range(0, len(left), 2)]
    return [link for low, high in pairs for link in ((low, high), (high, low))]


def shards(state, order, sweep, owner, slot_target):
    n = lax.axis_size("bis")
    groups = lax.axis_size("grp")
    chips = n // 2
    rows, width = sweep.shape
    parts = width // 128
    f32 = jnp.float32
    params = pltpu.CompilerParams(vmem_limit_bytes=48 * 1024 * 1024)

    def to_sibling(x):
        return lax.ppermute(x, "bis", [(i, i ^ 1) for i in range(n)])

    def to_chip(x, mask):
        return lax.ppermute(x, "bis", [(i, i ^ target(mask)) for i in range(n)]) if mask else x

    masks = routes(chips)
    owner = owner.reshape(n)
    extra = -(-(rows + n) // 8) * 8
    packed = pl.pallas_call(
        functools.partial(pack_kernel, n),
        out_shape=[
            jax.ShapeDtypeStruct((8 * (NF + 1) + (0 if mask else extra), width), f32) for mask in range(chips)
        ]
        + [jax.ShapeDtypeStruct((ZR, width), f32)],
        in_specs=[pl.BlockSpec(memory_space=pl.ANY)] * 5,
        out_specs=[VMEM] * (chips + 1),
        scratch_shapes=[
            pltpu.SMEM((n,), jnp.int32),
            pltpu.SMEM((n,), jnp.int32),
            pltpu.SMEM((n,), jnp.int32),
            pltpu.VMEM((NF, rows, width), f32),
            pltpu.SemaphoreType.DMA((NF + 4,)),
        ],
        compiler_params=params,
        name="pack",
    )(*[pltpu.with_memory_space_constraint(x, pltpu.HBM) for x in (order.reshape(n), owner, slot_target, sweep, state)])
    across = lax.ppermute(packed[chips], ("grp", "bis"), across_links(groups, n))
    mine = [to_chip(x, mask) for x, mask in zip(packed, masks)]
    theirs = [to_sibling(x) for x in mine]
    across_sib = to_sibling(jnp.concatenate([across] + [x[0:8] for x in mine[1:]]))

    code = pl.pallas_call(
        functools.partial(code_kernel, n, rows),
        out_shape=jax.ShapeDtypeStruct((2, n, 128), jnp.int32),
        in_specs=[VMEM] * 2,
        out_specs=VMEM,
        compiler_params=params,
        name="code",
    )(mine[0], theirs[0])

    stack = (2 * chips + 2) * 8
    send_shape = (2 * CAP * parts, 8, 128)
    out = pl.pallas_call(
        functools.partial(step_kernel, n),
        out_shape=[jax.ShapeDtypeStruct((stack, width), f32)] * 4
        + [jax.ShapeDtypeStruct((2, n, 8, width), f32)]
        + [jax.ShapeDtypeStruct(send_shape, f32)] * (chips - 1),
        in_specs=[VMEM] * (2 * chips + 4),
        out_specs=[VMEM] * (chips + 4),
        scratch_shapes=[
            pltpu.VMEM((NF, stack, width), f32),
            pltpu.VMEM((stack, width), f32),
            pltpu.VMEM((2, stack, width), f32),
            pltpu.VMEM((2, chips, 8, width), f32),
        ],
        compiler_params=params,
        name="substeps",
    )(code, *mine, *theirs, across, across_sib, sweep)
    sends = dict(zip(masks[1:], out[5:]))
    onward = sorted(sends, key=lambda mask: (-mask.bit_count(), -mask))
    got = {mask: to_chip(sends[mask], mask) for mask in onward}
    arrived = [got[mask] for mask in masks[1:]]
    vel, home, labels = pl.pallas_call(
        functools.partial(side_kernel, n),
        out_shape=[
            jax.ShapeDtypeStruct((2, rows, width), f32),
            jax.ShapeDtypeStruct(send_shape, f32),
            jax.ShapeDtypeStruct((chips, 8, 128), f32),
        ],
        in_specs=[VMEM] * (6 + 2 * chips),
        out_specs=[VMEM] * 3,
        compiler_params=params,
        name="velocities",
    )(*out[:5], code, *mine, *theirs)
    arrived = [home] + arrived
    early = 2
    sums = pl.pallas_call(
        functools.partial(land_kernel, n, False),
        out_shape=jax.ShapeDtypeStruct((2, rows, width), f32),
        in_specs=[VMEM] * (1 + early),
        out_specs=VMEM,
        compiler_params=params,
        name="sums",
    )(labels, *arrived[:early])
    mass, energy = pl.pallas_call(
        functools.partial(land_kernel, n, True),
        out_shape=[jax.ShapeDtypeStruct((rows, width), f32)] * 2,
        in_specs=[VMEM] * (2 + chips - early),
        out_specs=[pl.BlockSpec(memory_space=pl.ANY)] * 2,
        scratch_shapes=[pltpu.VMEM((2, rows, width), f32), pltpu.SemaphoreType.DMA((2, chips))],
        compiler_params=params,
        name="land",
    )(labels, sums, *arrived[early:])
    return mass, energy, vel


def solution(mesh):
    placed = (
        P(None, ("grp", "bis"), None),
        P(("grp", "bis"), None),
        P(("grp", "bis"), None),
        P(("grp", "bis"), None),
        P(("grp", "bis")),
    )
    return jax.shard_map(
        shards,
        mesh=mesh,
        in_specs=placed,
        out_specs=(P(("grp", "bis"), None), P(("grp", "bis"), None), P(None, ("grp", "bis"), None)),
        check_vma=False,
    )
```

```python
import functools

import jax
import jax.numpy as jnp
from jax import lax
from jax.experimental import pallas as pl
from jax.experimental.pallas import tpu as pltpu
from jax.sharding import PartitionSpec as P

BR = 4
CAP = 2
ZR = 8
HALF_DT = 0.075
NF = 5
RHO, ENE, VELU, VELV, GAM = range(NF)
FAR_P, FAR_U, INFO = 5, 6, 7
SMEM = pl.BlockSpec(memory_space=pltpu.SMEM)
VMEM = pl.BlockSpec(memory_space=pltpu.VMEM)


def sublane(width):
    return lax.broadcasted_iota(jnp.int32, (8, width), 0)


def turn(tile, shift):
    return pltpu.roll(tile, shift, 0)


def left_right(x):
    width = x.shape[1]
    lane = lax.broadcasted_iota(jnp.int32, x.shape, 1)
    left = jnp.where(lane == 0, 0.0, pltpu.roll(x, 1, 1))
    right = jnp.where(lane == width - 1, 0.0, pltpu.roll(x, width - 1, 1))
    return right - left


def at(tile):
    return pl.ds(pl.multiple_of(tile * 8, 8), 8)


def down_up(ref, tile, x, clip=None):
    sub = sublane(x.shape[1])
    before = ref[at(tile - 1 if clip is None else jnp.maximum(tile - 1, 0)), :]
    after = ref[at(tile + 1 if clip is None else jnp.minimum(tile + 1, clip)), :]
    return turn(jnp.where(sub == 0, after, x), 7) - turn(jnp.where(sub == 7, before, x), 1)


def where_am_i():
    return lax.axis_index("grp"), lax.axis_index("bis")


def routes(chips):
    return [0] + sorted(range(1, chips), key=lambda mask: (-mask.bit_count(), mask))


def crossed(mask):
    return 1 if mask.bit_count() == 1 else 0


def target(mask):
    return 2 * mask + crossed(mask)


def pack_kernel(n, *refs):
    chips = n // 2
    order_in, owner_in, slot_in, sweep_in, state_in = refs[:5]
    chip_bufs, across = refs[5 : 5 + chips], refs[5 + chips]
    order, owner, slot, state, sems = refs[6 + chips :]
    width = state.shape[2]
    rows = state.shape[1]
    home = 8 * (NF + 1)
    copies = [pltpu.make_async_copy(order_in, order, sems.at[0])]
    copies += [pltpu.make_async_copy(state_in.at[field], state.at[field], sems.at[1 + field]) for field in range(NF)]
    halves = [slice(0, rows // 2), slice(rows // 2, rows)]
    copies += [
        pltpu.make_async_copy(owner_in, owner, sems.at[1 + NF]),
        pltpu.make_async_copy(slot_in, slot, sems.at[2 + NF]),
        pltpu.make_async_copy(sweep_in, chip_bufs[0].at[home : home + rows, :], sems.at[3 + NF]),
    ]
    copies[0].start()
    for field in range(NF):
        for half in halves:
            pltpu.make_async_copy(state_in.at[field, half, :], state.at[field, half, :], sems.at[1 + field]).start()
    for copy in copies[1 + NF :]:
        copy.start()
    _, me = where_am_i()
    chip, core = me // 2, me % 2
    sub = sublane(width)
    first = me == 0
    goals = [chip ^ mask for mask in routes(chips)]
    copies[0].wait()

    def rim_rows(index):
        start = order[index] * BR
        return start + jnp.where(first, 0, BR - 1), start + jnp.where(first, 1, BR - 2)

    def halo(buf, base, near, far):
        for field in range(NF):
            buf[base + field : base + field + 1, :] = state[field, pl.ds(near, 1), :]
        line = lambda field: state[field, pl.ds(far, 1), :]
        buf[base + FAR_P : base + FAR_P + 1, :] = (line(GAM) - 1.0) * line(RHO) * line(ENE)
        buf[base + FAR_U : base + FAR_U + 1, :] = line(VELU)

    picks = [(order[2 * goal], order[2 * goal + 1]) for goal in goals]
    beyond = [jnp.where(first, jnp.minimum(2 * goal + 2, n - 1), jnp.maximum(2 * goal - 1, 0)) for goal in goals]
    rims = [rim_rows(index) for index in beyond + [jnp.where(first, 0, n - 1)]]
    for field in range(NF):
        copies[1 + field].wait()
        for buf, (low, high) in zip(chip_bufs, picks):
            ta = state[field, pl.ds(pl.multiple_of(low // 2 * 8, 8), 8), :]
            tb = state[field, pl.ds(pl.multiple_of(high // 2 * 8, 8), 8), :]
            even = jnp.where(low % 2 == 0, ta, turn(ta, 4))
            odd = jnp.where(high % 2 == 1, tb, turn(tb, 4))
            buf[8 * field : 8 * field + 8, :] = jnp.where(sub < 4, even, odd)
    for buf, rim in zip(chip_bufs, rims):
        halo(buf, 8 * NF, *rim)
    halo(across, 0, *rims[-1])
    for copy in copies[1 + NF :]:
        copy.wait()
    lane = lax.broadcasted_iota(jnp.int32, (1, width), 1)
    info = jnp.zeros((1, width), jnp.int32)
    for index in range(2 * n):
        value = owner[index] if index < n else slot[index - n]
        info = jnp.where(lane // (width // (2 * n)) == index, value, info)
    for buf in chip_bufs:
        buf[8 * NF + INFO : 8 * NF + INFO + 1, :] = info.astype(jnp.float32)
    for block in range(n):
        line = jnp.where(lane < width // 2, owner[block], slot[block])
        chip_bufs[0][home + rows + block : home + rows + block + 1, :] = line.astype(jnp.float32)


def code_kernel(n, rows, own_home, sib_home, code):
    _, me = where_am_i()
    span = pl.ds(8 * (NF + 1) + rows, n)
    own, sib = own_home[span, 0:128].astype(jnp.int32), sib_home[span, 0:128].astype(jnp.int32)
    line_id = lax.broadcasted_iota(jnp.int32, (n, 128), 0)
    for device in range(2):
        owner = jnp.where(me % 2 == device, own, sib)
        rank = jnp.zeros((n, 128), jnp.int32)
        for block in range(n):
            same = jnp.logical_and(owner == owner[block : block + 1, :], line_id > block)
            rank = jnp.where(same, rank + 1, rank)
        code[device] = (owner ^ me) * (2 * CAP) + (device * CAP) + rank


def labels_of(n, me, infos):
    step = infos[0].shape[1] // (2 * n)
    sub = sublane(128)
    tile = jnp.full((8, 128), -1.0, jnp.float32)
    for device, info in enumerate(infos):
        value = lambda index: jnp.broadcast_to(info[:, index * step : index * step + 1], (8, 128))
        place = jnp.full((8, 128), device * CAP, jnp.int32)
        for block in range(n):
            hit = value(block) == me.astype(jnp.float32)
            tile = jnp.where(jnp.logical_and(hit, sub == place), value(n + block), tile)
            place = jnp.where(hit, place + 1, place)
    return tile


def pack_partials(n, masks, code, parts, sends):
    width = parts.shape[3]
    pieces = width // 128
    lanes = [slice(piece * 128, piece * 128 + 128) for piece in range(pieces)]
    for device in range(2):
        wants = [target(mask) * (2 * CAP) + device * CAP + again for mask in masks for again in range(CAP)]
        found = [[jnp.zeros((8, 128), jnp.float32)] * pieces for _ in wants]
        for block in range(n):
            taken = jnp.broadcast_to(code[device, block : block + 1, :], (8, 128))
            tile = [parts[device, block, :, lane] for lane in lanes]
            for index, want in enumerate(wants):
                hit = taken == want
                found[index] = [jnp.where(hit, new, old) for new, old in zip(tile, found[index])]
        for index in range(len(wants)):
            rank = device * CAP + index % CAP
            for piece in range(pieces):
                sends[index // CAP][rank * pieces + piece] = found[index][piece]


def step_kernel(n, *refs):
    chips = n // 2
    refs = list(refs)
    take = lambda count: [refs.pop(0) for _ in range(count)]
    (code,) = take(1)
    mine, theirs = take(chips), take(chips)
    across, across_sib, sweep = take(3)
    nxt_prs, nxt_u, nxt_v, coef = take(4)
    (parts,) = take(1)
    sends = take(chips - 1)
    fld, prs, vols, halo = take(4)
    grp, me = where_am_i()
    chip, core = me // 2, me % 2
    width = sweep.shape[1]
    rows = sweep.shape[0]
    home = 8 * (NF + 1)
    sweep_sib = theirs[0].at[home : home + rows, :]
    tiles = 2 * chips
    sub = sublane(width)
    is_low = core == 0

    def pair(own, sib):
        return jnp.where(is_low, own, sib), jnp.where(is_low, sib, own)

    for index, mask in enumerate(routes(chips)):
        source = chip ^ mask
        own, sib = mine[index], theirs[index]
        if crossed(mask):
            own, sib = sib, own
        placed = (at(1 + source), at(1 + chips + source))
        blocks = []
        for field in range(NF):
            span = pl.ds(8 * field, 8)
            even, odd = pair(own[span, :], sib[span, :])
            blocks.append((jnp.where(sub < 4, even, turn(odd, 4)), jnp.where(sub < 4, turn(even, 4), odd)))
            for where_to, block in zip(placed, blocks[field]):
                fld[field, where_to, :] = block
        for device, where_to in enumerate(placed):
            prs[where_to, :] = (blocks[GAM][device] - 1.0) * blocks[RHO][device] * blocks[ENE][device]
        even, odd = pair(own[8 * NF : home, :], sib[8 * NF : home, :])
        halo[0, source] = even
        halo[1, source] = odd
    even, odd = pair(across[0:8, :], across_sib[0:8, :])
    inside_top = jnp.logical_or(grp > 0, chip > 0)
    inside_bottom = jnp.logical_or(grp < lax.axis_size("grp") - 1, chip < chips - 1)
    top = jnp.where(inside_top, jnp.where(chip == 0, even, halo[1, chips - 1]), 0.0)
    bottom = jnp.where(inside_bottom, jnp.where(chip == chips - 1, odd, halo[0, 0]), 0.0)

    def line(tile, index):
        return jnp.broadcast_to(tile[index : index + 1, :], (8, width))

    for tile, place, near in ((top, 0, 7), (bottom, tiles + 1, 0)):
        span = at(place)
        for field in (RHO, ENE, VELV, GAM):
            fld[field, span, :] = line(tile, field)
        fld[VELU, span, :] = jnp.where(sub == near, line(tile, VELU), line(tile, FAR_U))
        press = (line(tile, GAM) - 1.0) * line(tile, RHO) * line(tile, ENE)
        prs[span, :] = jnp.where(sub == near, press, line(tile, FAR_P))

    def first(tile, _):
        span = at(tile)
        velu, velv, press = fld[VELU, span, :], fld[VELV, span, :], prs[span, :]
        push = HALF_DT * (down_up(fld.at[VELU], tile, velu, tiles + 1) + left_right(velv))
        grow = 1.0 + push
        scale = HALF_DT / fld[RHO, span, :]
        keep = 1.0 - (fld[GAM, span, :] - 1.0) * push
        nxt_prs[span, :] = press * keep / grow
        nxt_u[span, :] = velu - down_up(prs, tile, press, tiles + 1) * scale
        nxt_v[span, :] = velv - left_right(press) * scale
        coef[span, :] = scale * grow
        vols[0, span, :] = grow
        vols[1, span, :] = fld[ENE, span, :] * keep
        return 0

    lax.fori_loop(0, tiles + 2, first, 0, unroll=n <= 8)
    for place, inside in ((0, inside_top), (tiles + 1, inside_bottom)):
        span = at(place)
        nxt_prs[span, :] = jnp.where(inside, nxt_prs[span, :], 0.0)
        nxt_u[span, :] = jnp.where(inside, nxt_u[span, :], 0.0)

    def cyclic(x):
        return jnp.where(sub % BR == 0, turn(x, 8 - (BR - 1)), turn(x, 1))

    def second(device, index):
        tile = 1 + device * chips + index
        span = at(tile)
        push = HALF_DT * (down_up(nxt_u, tile, nxt_u[span, :]) + left_right(nxt_v[span, :]))
        volume = vols[0, span, :] * (1.0 + push)
        heat_e = vols[1, span, :] * (1.0 - (fld[GAM, span, :] - 1.0) * push)
        mass = fld[RHO, span, :]
        heat = mass * heat_e
        from_own = (core == 0) if device == 0 else (core == 1)
        swept = jnp.where(from_own, sweep[at(index), :], sweep_sib[at(index), :])
        frac = swept * volume / (1.0 + volume)
        mass_go, heat_go = frac * mass, frac * heat
        mass_part = mass - mass_go + cyclic(mass_go)
        heat_part = heat - heat_go + cyclic(heat_go)
        parts[device, 2 * index] = jnp.where(sub < 4, mass_part, turn(heat_part, 4))
        parts[device, 2 * index + 1] = jnp.where(sub < 4, turn(mass_part, 4), heat_part)

    for device in range(2):
        lax.fori_loop(0, chips, lambda index, _, device=device: (second(device, index), 0)[1], 0, unroll=n <= 8)

    pack_partials(n, routes(chips)[1:], code, parts, sends)


def side_kernel(n, *refs):
    chips = n // 2
    prs, velu, velv, coef, parts, code = refs[:6]
    vel, home = refs[6:]
    _, me = where_am_i()
    core = me % 2
    pack_partials(n, routes(chips)[:1], code, parts, [home])
    def one(index, _):
        tile = 1 + core * chips + index
        span, dest = at(tile), at(index)
        press, scale = prs[span, :], coef[span, :]
        vel[0, dest, :] = velu[span, :] - down_up(prs, tile, press) * scale
        vel[1, dest, :] = velv[span, :] - left_right(press) * scale
        return 0

    lax.fori_loop(0, chips, one, 0, unroll=n <= 8)


def label_kernel(n, *refs):
    chips = n // 2
    mine, theirs, labels = refs[:chips], refs[chips : 2 * chips], refs[2 * chips]
    _, me = where_am_i()
    core = me % 2
    line = slice(8 * NF + INFO, 8 * NF + INFO + 1)
    for index, mask in enumerate(routes(chips)):
        own, sib = mine[index][line, :], theirs[index][line, :]
        if crossed(mask):
            own, sib = sib, own
        labels[index] = labels_of(n, me, (jnp.where(core == 0, own, sib), jnp.where(core == 0, sib, own)))


def land_kernel(n, final, *refs):
    chips = n // 2
    refs = list(refs)
    labels = refs.pop(0)
    if final:
        mass_out, energy_out, sums_out, sems = refs[-4:]
        sums_in, arrived = refs[0], refs[1:-4]
    else:
        sums_in, arrived, sums_out = None, refs[:-1], refs[-1]
    skipped = chips - len(arrived) if final else 0
    parts = sums_out.shape[2] // 128
    sub = sublane(128)

    def send(which, index):
        span = pl.ds(pl.multiple_of(index * 8, 8), 8)
        target_ref = energy_out if which else mass_out
        return pltpu.make_async_copy(sums_out.at[which, span, :], target_ref.at[span, :], sems.at[which, index])

    def tile_pair(index, _):
        span = pl.ds(pl.multiple_of(index * 8, 8), 8)
        sums = [[jnp.zeros((8, 128), jnp.float32) for _ in range(parts)] for _ in range(2)]
        for number, buf in enumerate(arrived):
            for rank in range(2 * CAP):
                tag = jnp.broadcast_to(labels[skipped + number, rank : rank + 1, :], (8, 128))
                for bit in range(2):
                    hit = tag == (2 * index + bit) * 1.0
                    for part in range(parts):
                        sums[bit][part] += jnp.where(hit, buf[rank * parts + part], 0.0)
        for part in range(parts):
            cols = slice(part * 128, part * 128 + 128)
            even, odd = sums[0][part], sums[1][part]
            mass, energy = jnp.where(sub < 4, even, turn(odd, 4)), jnp.where(sub < 4, turn(even, 4), odd)
            if final:
                mass, energy = mass + sums_in[0, span, cols], energy + sums_in[1, span, cols]
            sums_out[0, span, cols] = mass
            sums_out[1, span, cols] = energy
        if final:
            send(0, index).start()
            send(1, index).start()
        return 0

    lax.fori_loop(0, chips, tile_pair, 0, unroll=n <= 8)
    if final:
        for index in range(chips):
            send(0, index).wait()
            send(1, index).wait()


def across_links(groups, n):
    pairs = []
    for grp in range(groups):
        base = grp * n
        pairs += [(base + i, base + i + 1) for i in range(2, n - 2, 2)]
        if grp + 1 < groups:
            turn_at = n - 2 if grp % 2 == 0 else 1
            pairs += [(base + n - 1, base + n), (base + turn_at, base + n + turn_at)]
    used = {i for pair in pairs for i in pair}
    left = [i for i in range(groups * n) if i not in used]
    pairs += [(left[i], left[i + 1]) for i in range(0, len(left), 2)]
    return [link for low, high in pairs for link in ((low, high), (high, low))]


def shards(state, order, sweep, owner, slot_target):
    n = lax.axis_size("bis")
    groups = lax.axis_size("grp")
    chips = n // 2
    rows, width = sweep.shape
    parts = width // 128
    f32 = jnp.float32
    params = pltpu.CompilerParams(vmem_limit_bytes=48 * 1024 * 1024)

    def to_sibling(x):
        return lax.ppermute(x, "bis", [(i, i ^ 1) for i in range(n)])

    def to_chip(x, mask):
        return lax.ppermute(x, "bis", [(i, i ^ target(mask)) for i in range(n)]) if mask else x

    masks = routes(chips)
    owner = owner.reshape(n)
    extra = -(-(rows + n) // 8) * 8
    packed = pl.pallas_call(
        functools.partial(pack_kernel, n),
        out_shape=[
            jax.ShapeDtypeStruct((8 * (NF + 1) + (0 if mask else extra), width), f32) for mask in range(chips)
        ]
        + [jax.ShapeDtypeStruct((ZR, width), f32)],
        in_specs=[pl.BlockSpec(memory_space=pl.ANY)] * 5,
        out_specs=[VMEM] * (chips + 1),
        scratch_shapes=[
            pltpu.SMEM((n,), jnp.int32),
            pltpu.SMEM((n,), jnp.int32),
            pltpu.SMEM((n,), jnp.int32),
            pltpu.VMEM((NF, rows, width), f32),
            pltpu.SemaphoreType.DMA((NF + 4,)),
        ],
        compiler_params=params,
        name="pack",
    )(*[pltpu.with_memory_space_constraint(x, pltpu.HBM) for x in (order.reshape(n), owner, slot_target, sweep, state)])
    across = lax.ppermute(packed[chips], ("grp", "bis"), across_links(groups, n))
    mine = [to_chip(x, mask) for x, mask in zip(packed, masks)]
    theirs = [to_sibling(x) for x in mine]
    across_sib = to_sibling(jnp.concatenate([across] + [x[0:8] for x in mine[1:]]))

    code = pl.pallas_call(
        functools.partial(code_kernel, n, rows),
        out_shape=jax.ShapeDtypeStruct((2, n, 128), jnp.int32),
        in_specs=[VMEM] * 2,
        out_specs=VMEM,
        compiler_params=params,
        name="code",
    )(mine[0], theirs[0])

    stack = (2 * chips + 2) * 8
    send_shape = (2 * CAP * parts, 8, 128)
    out = pl.pallas_call(
        functools.partial(step_kernel, n),
        out_shape=[jax.ShapeDtypeStruct((stack, width), f32)] * 4
        + [jax.ShapeDtypeStruct((2, n, 8, width), f32)]
        + [jax.ShapeDtypeStruct(send_shape, f32)] * (chips - 1),
        in_specs=[VMEM] * (2 * chips + 4),
        out_specs=[VMEM] * (chips + 4),
        scratch_shapes=[
            pltpu.VMEM((NF, stack, width), f32),
            pltpu.VMEM((stack, width), f32),
            pltpu.VMEM((2, stack, width), f32),
            pltpu.VMEM((2, chips, 8, width), f32),
        ],
        compiler_params=params,
        name="substeps",
    )(code, *mine, *theirs, across, across_sib, sweep)
    arrived = [to_chip(x, mask) for x, mask in zip(out[5:], masks[1:])]
    labels = pl.pallas_call(
        functools.partial(label_kernel, n),
        out_shape=jax.ShapeDtypeStruct((chips, 8, 128), f32),
        in_specs=[VMEM] * (2 * chips),
        out_specs=VMEM,
        compiler_params=params,
        name="labels",
    )(*mine, *theirs)
    vel, home = pl.pallas_call(
        functools.partial(side_kernel, n),
        out_shape=[
            jax.ShapeDtypeStruct((2, rows, width), f32),
            jax.ShapeDtypeStruct(send_shape, f32),
        ],
        in_specs=[VMEM] * 6,
        out_specs=[VMEM] * 2,
        compiler_params=params,
        name="velocities",
    )(*out[:5], code)
    arrived = [home] + arrived
    early = 2
    sums = pl.pallas_call(
        functools.partial(land_kernel, n, False),
        out_shape=jax.ShapeDtypeStruct((2, rows, width), f32),
        in_specs=[VMEM] * (1 + early),
        out_specs=VMEM,
        compiler_params=params,
        name="sums",
    )(labels, *arrived[:early])
    mass, energy = pl.pallas_call(
        functools.partial(land_kernel, n, True),
        out_shape=[jax.ShapeDtypeStruct((rows, width), f32)] * 2,
        in_specs=[VMEM] * (2 + chips - early),
        out_specs=[pl.BlockSpec(memory_space=pl.ANY)] * 2,
        scratch_shapes=[pltpu.VMEM((2, rows, width), f32), pltpu.SemaphoreType.DMA((2, chips))],
        compiler_params=params,
        name="land",
    )(labels, sums, *arrived[early:])
    return mass, energy, vel


def solution(mesh):
    placed = (
        P(None, ("grp", "bis"), None),
        P(("grp", "bis"), None),
        P(("grp", "bis"), None),
        P(("grp", "bis"), None),
        P(("grp", "bis")),
    )
    return jax.shard_map(
        shards,
        mesh=mesh,
        in_specs=placed,
        out_specs=(P(("grp", "bis"), None), P(("grp", "bis"), None), P(None, ("grp", "bis"), None)),
        check_vma=False,
    )
```
